32 devices in a mesh: section: 2 (over x), dp: 8 (over z, core), rep: 2 (over y).
Axes of the slice: x: 2, y: 2, z: 4, core: 2. Of those that a mesh axis runs over, the one named last changes fastest.
Arguments:
- points: bfloat16 [48, 256, 384], P(('dp', 'rep')), may hold values from -6 to 6
- segments: int32 [48, 256], P(('dp', 'rep')), may hold values from 0 to 1, as said below
- neighbours: int32 [48, 256, 16], P(('dp', 'rep')), may hold values from 0 to 255, as said below
- condition: bfloat16 [48, 2, 384], P(('dp', 'rep')), may hold values from -6 to 6
- msg_in: bfloat16 [2, 768, 384], P('section', None, 'dp'), may hold values from -0.3125 to 0.3125
- msg_out: bfloat16 [2, 384, 384], P('section', 'dp'), may hold values from -0.625 to 0.625
- norm_gain: bfloat16 [2, 384], P('section', 'dp'), may hold values from 0.5 to 1.5
- mod_weight: bfloat16 [2, 384, 1536], P('section', 'dp'), may hold values from -0.15625 to 0.15625
- query_base: bfloat16 [2, 256, 384], P('section', None, 'dp'), may hold values from -6 to 6
- q_weight: bfloat16 [2, 384, 384], P('section', 'dp'), may hold values from -0.3125 to 0.3125
- kv_weight: bfloat16 [2, 384, 768], P('section', 'dp'), may hold values from -0.3125 to 0.3125
- o_weight: bfloat16 [2, 384, 384], P('section', 'dp'), may hold values from -1.25 to 1.25
- up_weight: bfloat16 [2, 384, 1536], P('section', 'dp'), may hold values from -0.3125 to 0.3125
- down_weight: bfloat16 [2, 1536, 384], P('section', None, 'dp'), may hold values from -0.15625 to 0.15625
- cotangent: bfloat16 [2, 48, 512, 384], P('section', ('dp', 'rep')), may hold values from -6 to 6
Outputs:
- latents: bfloat16 [2, 48, 512, 384], P('section', ('dp', 'rep'))
- grad_points: float32 [48, 256, 384], P(('dp', 'rep'))
- grad_msg_in: float32 [2, 768, 384], P('section', None, 'dp')
- grad_msg_out: float32 [2, 384, 384], P('section', 'dp')
- grad_norm_gain: float32 [2, 384], P('section', 'dp')
- grad_mod_weight: float32 [2, 384, 1536], P('section', 'dp')
- grad_query_base: float32 [2, 256, 384], P('section', None, 'dp')
- grad_q_weight: float32 [2, 384, 384], P('section', 'dp')
- grad_kv_weight: float32 [2, 384, 768], P('section', 'dp')
- grad_o_weight: float32 [2, 384, 384], P('section', 'dp')
- grad_up_weight: float32 [2, 384, 1536], P('section', 'dp')
- grad_down_weight: float32 [2, 1536, 384], P('section', None, 'dp')
The draws below stay inside these ranges and needn't reach their ends.
Inputs may be any that keep to these rules, and one draw needn't show every extreme that they name: `segments`: non-decreasing along each buffer; each of the 2 evolutions holds some supernodes of every buffer. `neighbours`: each supernode's 16 sources lie in its own evolution.
All inputs are finite; a program needn't handle non-finite values.
Results may differ from the reference program's by a relative error of at most 0.019.
Values may be sent and summed in bfloat16 or wider, within the bound.
A program may use at most 256 MiB of HBM per device.

```python
import jax
import jax.numpy as jnp
from jax import lax

D = 384
HEADS = 6
HEAD_DIM = 64
FF = 1536
QPS = 256
NBR = 16
SIMS = 2
L = 256
BUFFERS = 48
QUERIES = 512


def draw_layout(key):
    spread = max(L // (4 * SIMS), 1)
    jitter = jax.random.randint(key, (BUFFERS, SIMS - 1), -spread, spread + 1)
    sizes = (L // SIMS + jitter).astype(jnp.int32)
    bounds = jnp.cumsum(sizes, axis=1).astype(jnp.int32)
    places = jnp.arange(L, dtype=jnp.int32)
    segment = jnp.sum((places[None, :, None] >= bounds[:, None, :]).astype(jnp.int32), axis=2).astype(jnp.int32)
    return (segment, bounds)


def draw_segments(key, part):
    segment, bounds = draw_layout(key)
    return segment


def draw_neighbours(key, part):
    segment, bounds = draw_layout(key)
    key = jax.random.fold_in(key, 2)
    starts = jnp.concatenate([jnp.zeros((BUFFERS, 1), jnp.int32), bounds], axis=1)
    stops = jnp.concatenate([bounds, jnp.full((BUFFERS, 1), L, jnp.int32)], axis=1)
    lower = jnp.take_along_axis(starts, segment, axis=1)
    upper = jnp.take_along_axis(stops, segment, axis=1)
    picked = jax.random.randint(key, (BUFFERS, L, NBR), lower[:, :, None], upper[:, :, None])
    return picked.astype(jnp.int32)


def block_scale(stream_key, extent, split, low, largest):
    gain, own = 1.0, jax.random.fold_in(stream_key, 6)
    for axis_at, parts in split:
        steps = jnp.exp(jax.random.uniform(jax.random.fold_in(own, axis_at), (parts,), jnp.float32, low / len(split), largest / len(split)))
        gain = gain * jnp.repeat(steps, extent[axis_at] // parts).reshape([-1 if axis == axis_at else 1 for axis in range(len(extent))])
    return gain


def bell_draw(key, extent, scale, most, cuts=(), kind=jnp.bfloat16):
    drawn = jax.random.normal(key, extent, jnp.float32) * scale
    if len(cuts) > 0:
        drawn = block_scale(key, extent, cuts, -0.22, 0.18) * drawn
    return jnp.clip(drawn, min=-most, max=most).astype(kind)


def setup_inputs(seed: int = 0) -> dict:
    arg_keys = jax.random.split(jax.random.key(seed), 16)
    points = bell_draw(arg_keys[0], (BUFFERS, L, D), 1.0, 6.0, ((0, 16),))
    segments = draw_segments(jax.random.fold_in(arg_keys[15], 71), 0)
    neighbours = draw_neighbours(jax.random.fold_in(arg_keys[15], 71), 0)
    condition = bell_draw(arg_keys[3], (BUFFERS, SIMS, D), 1.0, 6.0, ((0, 16),))
    msg_in = bell_draw(arg_keys[4], (2, 2 * D, D), D ** -0.5, 0.3125, ((0, 2), (2, 8)))
    msg_out = bell_draw(arg_keys[5], (2, D, D), (D // 4) ** -0.5, 0.625, ((0, 2), (1, 8)))
    norm_gain = jnp.clip(1.0 + 0.1 * jax.random.normal(arg_keys[6], (2, D), jnp.float32), 0.5, 1.5).astype(jnp.bfloat16)
    mod_weight = bell_draw(arg_keys[7], (2, D, 4 * D), (4 * D) ** -0.5, 0.15625, ((0, 2), (1, 8)))
    query_base = bell_draw(arg_keys[8], (2, QPS, D), 1.0, 6.0, ((0, 2), (2, 8)))
    q_weight = bell_draw(arg_keys[9], (2, D, D), D ** -0.5, 0.3125, ((0, 2), (1, 8)))
    kv_weight = bell_draw(arg_keys[10], (2, D, 2 * D), D ** -0.5, 0.3125, ((0, 2), (1, 8)))
    o_weight = bell_draw(arg_keys[11], (2, D, D), (D // 16) ** -0.5, 1.25, ((0, 2), (1, 8)))
    up_weight = bell_draw(arg_keys[12], (2, D, FF), D ** -0.5, 0.3125, ((0, 2), (1, 8)))
    down_weight = bell_draw(arg_keys[13], (2, FF, D), FF ** -0.5, 0.15625, ((0, 2), (2, 8)))
    cotangent = bell_draw(arg_keys[14], (2, BUFFERS, QUERIES, D), 1.0, 6.0, ((0, 2), (1, 16)))
    return dict(points=points, segments=segments, neighbours=neighbours, condition=condition, msg_in=msg_in, msg_out=msg_out, norm_gain=norm_gain, mod_weight=mod_weight, query_base=query_base, q_weight=q_weight, kv_weight=kv_weight, o_weight=o_weight, up_weight=up_weight, down_weight=down_weight, cotangent=cotangent)


@jax.custom_vjp
def low(v):
    return lax.optimization_barrier(v.astype(jnp.bfloat16)).astype(jnp.float32)

@jax.custom_vjp
def low_back(v):
    return v

def low_keep(v):
    return (low(v), None)

def low_pass(kept, grad):
    return (grad,)

def back_keep(v):
    return (v, None)

def back_low(kept, grad):
    return (low(grad),)
low.defvjp(low_keep, low_pass)
low_back.defvjp(back_keep, back_low)
EPSILON = 1e-05

def matmul_high(left_op, right_op):
    return jnp.dot(left_op, right_op, precision=lax.Precision.HIGHEST)

def layer_norm(values):
    centre = values - lax.optimization_barrier(jnp.mean(values, axis=-1, keepdims=True))
    spread = lax.optimization_barrier(jnp.mean(centre * centre, axis=-1, keepdims=True))
    return centre * lax.rsqrt(spread + EPSILON)

def section_layer(weights, points, tokens, segment, neighbour, condition):
    msg_in, msg_out, norm_gain, mod_weight, query_base, q_weight, kv_weight, o_weight, up_weight, down_weight = weights
    at_source = low_back(matmul_high(points, msg_in[:D]))
    at_target = low_back(matmul_high(tokens, msg_in[D:]))
    inside = at_source[neighbour] + at_target[:, None, :]
    mixed = low(lax.optimization_barrier(jnp.mean(jax.nn.gelu(inside), axis=1)))
    supernode = tokens + low_back(matmul_high(mixed, msg_out))
    normed = low(layer_norm(supernode) * norm_gain)
    keyval = low(low_back(matmul_high(normed, kv_weight)))
    key_heads = keyval[:, :D].reshape(L, HEADS, HEAD_DIM)
    value_heads = keyval[:, D:].reshape(L, HEADS, HEAD_DIM)
    modulation = low_back(matmul_high(condition, mod_weight)).reshape(SIMS, 4, 1, D)
    query_rows = jnp.broadcast_to(query_base, (SIMS, QPS, D))
    first_in = low(((1.0 + modulation[:, 0]) * layer_norm(query_rows) + modulation[:, 1]).reshape(QUERIES, D))
    query_heads = low(low_back(matmul_high(first_in, q_weight))).reshape(QUERIES, HEADS, HEAD_DIM)
    owner_sim = jnp.arange(QUERIES, dtype=jnp.int32) // QPS
    allowed = owner_sim[:, None] == segment[None, :]
    raw_scores = low_back(jnp.einsum('qhe,khe->hqk', query_heads, key_heads, precision=lax.Precision.HIGHEST))
    scores = jnp.where(allowed[None], raw_scores * HEAD_DIM ** (-0.5), -1000000000.0)
    attention = low(jax.nn.softmax(scores, axis=-1))
    attended = low(low_back(jnp.einsum('hqk,khe->qhe', attention, value_heads, precision=lax.Precision.HIGHEST))).reshape(QUERIES, D)
    residual = query_rows.reshape(QUERIES, D) + low_back(matmul_high(attended, o_weight))
    second = low(((1.0 + modulation[:, 2]) * layer_norm(residual.reshape(SIMS, QPS, D)) + modulation[:, 3]).reshape(QUERIES, D))
    hidden = low(jax.nn.gelu(low_back(matmul_high(second, up_weight))))
    latents = residual + low_back(matmul_high(hidden, down_weight))
    return (latents, supernode)

def buffer_forward(first_set, second_set, points, segment, neighbour, condition):
    lat_first, node_first = section_layer(first_set, points, points, segment, neighbour, condition)
    passed = low_back(low(node_first))
    lat_second, node_second = section_layer(second_set, points, passed, segment, neighbour, condition)
    return jnp.stack([lat_first, lat_second])

def reference(points, segments, neighbours, condition, msg_in, msg_out, norm_gain, mod_weight, query_base, q_weight, kv_weight, o_weight, up_weight, down_weight, cotangent):
    weights = tuple((member.astype(jnp.float32) for member in (msg_in, msg_out, norm_gain, mod_weight, query_base, q_weight, kv_weight, o_weight, up_weight, down_weight)))
    point_values = points.astype(jnp.float32)
    cond_values = condition.astype(jnp.float32)
    step_fn = jax.checkpoint(buffer_forward)

    def forward(point_arg, weight_arg):
        first_set = tuple((member[0] for member in weight_arg))
        second_set = tuple((member[1] for member in weight_arg))
        stacked = lax.map(lambda bundle: step_fn(first_set, second_set, *bundle), (point_arg, segments, neighbours, cond_values))
        return jnp.transpose(stacked, (1, 0, 2, 3))
    latents, pullback = jax.vjp(forward, point_values, weights)
    grad_points, grad_weights = pullback(cotangent.astype(jnp.float32))
    return (latents.astype(jnp.bfloat16), grad_points, grad_weights[0], grad_weights[1], grad_weights[2], grad_weights[3], grad_weights[4], grad_weights[5], grad_weights[6], grad_weights[7], grad_weights[8], grad_weights[9])
```

```python
import functools

import jax
import jax.numpy as jnp
from jax import lax
from jax.experimental import pallas as pl
from jax.experimental.pallas import tpu as pltpu
from jax.sharding import PartitionSpec as P

HEADS = 6
HEAD_DIM = 64
EPSILON = 1e-05
TANH_ONE = 0.7978845608028654
TANH_THREE = 0.7978845608028654 * 0.044715
LOW = jnp.bfloat16
WIDE = jnp.float32
VMEM_BYTES = 60 * 1024 * 1024


def product(left_op, right_op):
    return jnp.dot(left_op, right_op, preferred_element_type=WIDE)


def trans_left(left_op, right_op):
    return lax.dot_general(left_op, right_op, (((0,), (0,)), ((), ())), preferred_element_type=WIDE)


def trans_right(left_op, right_op):
    return lax.dot_general(left_op, right_op, (((1,), (1,)), ((), ())), preferred_element_type=WIDE)


def gelu_pair(inside):
    square = inside * inside
    half = 0.5 + 0.5 * jnp.tanh(inside * (TANH_ONE + TANH_THREE * square))
    value = inside * half
    slope = half + value * (1.0 - half) * (2.0 * TANH_ONE + 6.0 * TANH_THREE * square)
    return value, slope


def normalised(values):
    centre = values - jnp.mean(values, axis=-1, keepdims=True)
    spread = jnp.mean(centre * centre, axis=-1, keepdims=True)
    scale = lax.rsqrt(spread + EPSILON)
    return centre * scale, scale


def normalised_back(d_out, unit, scale):
    first = jnp.mean(d_out, axis=-1, keepdims=True)
    second = jnp.mean(d_out * unit, axis=-1, keepdims=True)
    return scale * (d_out - first - unit * second)


class Columns:
    def __init__(self, width, hidden, per_sim):
        self.pieces = (
            ("source", width),
            ("target", width),
            ("msg_out", width),
            ("gain", 128),
            ("kv", 2 * width),
            ("q", width),
            ("o", width),
            ("base", per_sim),
            ("mod", 4 * width),
            ("up", hidden),
            ("down", hidden),
        )
        at = 0
        for name, extent in self.pieces:
            setattr(self, name, slice(at, at + extent))
            at += extent
        self.total = at


def message_forward(b, cols, packed, points, tokens, neighbours, source, target, mixed, slope, slope_sum, node):
    width = points.shape[-1]
    length = points.shape[1]
    count = neighbours.shape[-1]
    rows = 32
    source[...] = trans_right(points[b], packed[:, cols.source]).astype(LOW)
    target[...] = trans_right(tokens[b], packed[:, cols.target])

    def step(at, carry):
        here = pl.ds(pl.multiple_of(at * rows, rows), rows)
        near = neighbours[b, here, :]
        lane = lax.broadcasted_iota(jnp.int32, (rows, length), 1)
        picks = [jnp.where(near[:, k : k + 1] == lane, 1.0, 0.0).astype(LOW) for k in range(count)]
        inside = product(jnp.concatenate(picks, axis=0), source[...])
        inside = inside.reshape(count, rows, width) + target[here, :][None]
        value, steep = gelu_pair(inside)
        mixed[b, here, :] = (jnp.sum(value, axis=0) * (1.0 / count)).astype(LOW)
        slope_sum[b, here, :] = jnp.sum(steep, axis=0)
        slope[b, :, here, :] = steep.astype(LOW)
        return carry

    lax.fori_loop(0, length // rows, step, 0)
    node[b] = tokens[b].astype(WIDE) + product(mixed[b], packed[:, cols.msg_out])


def message_back(
    b, cols, packed, points, tokens, neighbours_t, mixed, slope, slope_sum, d_node, grads, d_points, d_tokens, total
):
    length = points.shape[1]
    count = neighbours_t.shape[1]
    node_low = d_node.astype(LOW)
    grads[:, cols.msg_out] += trans_left(mixed[b], node_low)
    d_mixed = trans_right(node_low, packed[:, cols.msg_out]) * (1.0 / count)
    d_target = (d_mixed * slope_sum[b]).astype(LOW)
    mixed_low = d_mixed.astype(LOW)
    group = 4
    total[...] = jnp.zeros_like(total)
    for at in range(0, count, group):
        spot = lax.broadcasted_iota(jnp.int32, (length, length), 0)
        picks = [
            jnp.where(neighbours_t[b, k : k + 1, :] == spot, 1.0, 0.0).astype(LOW) for k in range(at, at + group)
        ]
        inside = [slope[b, k] * mixed_low for k in range(at, at + group)]
        total[...] += product(jnp.concatenate(picks, axis=1), jnp.concatenate(inside, axis=0))
    d_source = total[...].astype(LOW)
    grads[:, cols.source] += trans_left(d_source, points[b])
    grads[:, cols.target] += trans_left(d_target, tokens[b])
    d_points[b] = product(d_source, packed[:, cols.source])
    d_tokens[b] = d_node + product(d_target, packed[:, cols.target])


def perceiver(
    b,
    cols,
    packed,
    node,
    segments,
    modulation,
    base_unit,
    base_rows,
    gain_row,
    cotangent,
    latents,
    grads,
    d_node,
    d_gain,
    d_base_unit,
    d_base,
    d_mod,
    scr,
):
    length, width = node.shape[1:]
    per_sim = base_rows.shape[0]
    queries = 2 * per_sim
    pairs = HEADS // 2
    block = 2 * HEAD_DIM
    unit, node_scale = normalised(node[b])
    gain = gain_row[...]
    normed = (unit * gain).astype(LOW)
    keyval = product(normed, packed[:, cols.kv]).astype(LOW)
    keyval_t = scr["keyval_t"]
    keyval_t[...] = keyval.T
    second_count = jnp.sum(segments[b], axis=1, keepdims=True)
    first_count = length - second_count
    own_col = (lax.broadcasted_iota(jnp.int32, (length, 1), 0) < first_count).astype(WIDE)
    own_row = (lax.broadcasted_iota(jnp.int32, (1, length), 1) < first_count).astype(WIDE)
    low_col = (own_col.astype(LOW), (1.0 - own_col).astype(LOW))
    low_row = (own_row.astype(LOW), (1.0 - own_row).astype(LOW))
    lane = lax.broadcasted_iota(jnp.int32, (1, block), 1)
    half = ((lane < HEAD_DIM).astype(WIDE).astype(LOW), (lane >= HEAD_DIM).astype(WIDE).astype(LOW))
    scale_one, shift_one, scale_two, shift_two = (
        [modulation[b, s : s + 1, width * n : width * (n + 1)] for s in range(2)] for n in range(4)
    )

    first_in, query = scr["first_in"], scr["query"]
    for s in range(2):
        first_in[s * per_sim : (s + 1) * per_sim, :] = (
            (1.0 + scale_one[s]) * base_unit[...] + shift_one[s]
        ).astype(LOW)
    query[...] = (product(first_in[...], packed[:, cols.q]).astype(LOW) * 0.125).astype(LOW)

    def spread_heads(values):
        return [
            jnp.concatenate([values * low_col[0] * half[h], values * low_col[1] * half[h]], axis=1) for h in range(2)
        ]

    def by_sim(rows_in, pair):
        here = slice(pair * block, (pair + 1) * block)
        return jnp.concatenate([rows_in[:per_sim, here], rows_in[per_sim:, here]], axis=1)

    weights_t = scr["weights_t"]
    attended_t = scr["attended_t"]
    mask = own_col > 0.5
    for pair in range(pairs):
        keys = spread_heads(keyval[:, pair * block : (pair + 1) * block])
        query_pair = by_sim(query, pair)
        for h in range(2):
            head = 2 * pair + h
            raw = trans_right(keys[h], query_pair)
            top_first = jnp.max(jnp.where(mask, raw, -3e38), axis=0, keepdims=True)
            top_second = jnp.max(jnp.where(mask, -3e38, raw), axis=0, keepdims=True)
            grown = jnp.exp(raw - jnp.where(mask, top_first, top_second))
            sum_first = jnp.sum(jnp.where(mask, grown, 0.0), axis=0, keepdims=True)
            sum_second = jnp.sum(jnp.where(mask, 0.0, grown), axis=0, keepdims=True)
            share = (grown * jnp.where(mask, 1.0 / sum_first, 1.0 / sum_second)).astype(LOW)
            weights_t[head] = share
            value_t = keyval_t[width + head * HEAD_DIM : width + (head + 1) * HEAD_DIM, :]
            value_sims = jnp.concatenate([value_t * low_row[0], value_t * low_row[1]], axis=0)
            out_t = product(value_sims, share).astype(LOW)
            here = slice(head * HEAD_DIM, (head + 1) * HEAD_DIM)
            attended_t[here, :per_sim] = out_t[:HEAD_DIM]
            attended_t[here, per_sim:] = out_t[HEAD_DIM:]

    residual = trans_left(attended_t[...], packed[:, cols.o])
    residual = residual + jnp.concatenate([base_rows[...]] * 2, axis=0)
    res_unit, res_scale = normalised(residual)
    second = jnp.concatenate(
        [(1.0 + scale_two[s]) * res_unit[s * per_sim : (s + 1) * per_sim] + shift_two[s] for s in range(2)], axis=0
    ).astype(LOW)
    cot = cotangent[b]
    second_t, cot_t = scr["second_t"], scr["cot_t"]
    second_t[...] = second.T
    cot_t[...] = cot.T
    lat = None
    d_second = None
    hidden_width = cols.up.stop - cols.up.start
    chunk = 512
    for at in range(0, hidden_width, chunk):
        up = slice(cols.up.start + at, cols.up.start + at + chunk)
        down = slice(cols.down.start + at, cols.down.start + at + chunk)
        value, steep = gelu_pair(product(second, packed[:, up]))
        hidden = value.astype(LOW)
        d_up = (product(cot, packed[:, down]) * steep).astype(LOW)
        part = trans_right(hidden, packed[:, down])
        lat = part if lat is None else lat + part
        part = trans_right(d_up, packed[:, up])
        d_second = part if d_second is None else d_second + part
        grads[:, down] += product(cot_t[...], hidden)
        grads[:, up] += product(second_t[...], d_up)
    latents[b] = (residual + lat).astype(LOW)

    d_res = []
    mod_rows = [[], []]
    for s in range(2):
        rows_at = slice(s * per_sim, (s + 1) * per_sim)
        d_sim = d_second[rows_at]
        unit_sim = res_unit[rows_at]
        mod_rows[s] = [
            jnp.sum(d_sim * unit_sim, axis=0, keepdims=True),
            jnp.sum(d_sim, axis=0, keepdims=True),
        ]
        d_res.append(
            cot[rows_at].astype(WIDE)
            + normalised_back(d_sim * (1.0 + scale_two[s]), unit_sim, res_scale[rows_at])
        )
    d_base[...] += d_res[0] + d_res[1]
    res_low = jnp.concatenate(d_res, axis=0).astype(LOW)
    grads[:, cols.o] += product(attended_t[...], res_low)
    d_att = trans_right(packed[:, cols.o], res_low).astype(LOW)
    d_query_t = scr["query_t"]
    d_keyval = scr["d_keyval"]
    left_half = lane < HEAD_DIM
    for pair in range(pairs):
        values = spread_heads(keyval[:, width + pair * block : width + (pair + 1) * block])
        query_pair = by_sim(query, pair)
        here = slice(pair * block, (pair + 1) * block)
        d_att_pair = jnp.concatenate([d_att[here, :per_sim], d_att[here, per_sim:]], axis=0)
        d_keys, d_values = [], []
        for h in range(2):
            head = 2 * pair + h
            there = slice(head * HEAD_DIM, (head + 1) * HEAD_DIM)
            both = d_att[there, :].astype(WIDE) * attended_t[there, :].astype(WIDE)
            both = jnp.sum(both, axis=0, keepdims=True)
            share = weights_t[head]
            d_share = product(values[h], d_att_pair)
            d_raw = (
                share.astype(WIDE) * (d_share - jnp.where(mask, both[:, :per_sim], both[:, per_sim:]))
            ).astype(LOW)
            key_t = keyval_t[there, :]
            key_sims = jnp.concatenate([key_t * low_row[0], key_t * low_row[1]], axis=0)
            d_q = (product(key_sims, d_raw) * 0.125).astype(LOW)
            d_query_t[there, :per_sim] = d_q[:HEAD_DIM]
            d_query_t[there, per_sim:] = d_q[HEAD_DIM:]
            full = trans_right(share, d_att_pair)
            d_values.append(jnp.where(mask, full[:, :block], full[:, block:]))
            full = product(d_raw, query_pair)
            d_keys.append(jnp.where(mask, full[:, :block], full[:, block:]))
        d_keyval[:, here] = jnp.where(left_half, d_keys[0], d_keys[1]).astype(LOW)
        d_keyval[:, width + here.start : width + here.stop] = jnp.where(
            left_half, d_values[0], d_values[1]
        ).astype(LOW)

    d_query = d_query_t[...].T
    grads[:, cols.q] += trans_left(first_in[...], d_query)
    d_first = trans_right(d_query, packed[:, cols.q])
    for s in range(2):
        d_sim = d_first[s * per_sim : (s + 1) * per_sim]
        mod_rows[s] = [
            jnp.sum(d_sim * base_unit[...], axis=0, keepdims=True),
            jnp.sum(d_sim, axis=0, keepdims=True),
        ] + mod_rows[s]
        d_base_unit[...] += d_sim * (1.0 + scale_one[s])
        d_mod[b, s : s + 1, :] = jnp.concatenate(mod_rows[s], axis=1)

    d_kv = d_keyval[...]
    grads[:, cols.kv] += trans_left(normed, d_kv)
    d_normed = trans_right(d_kv, packed[:, cols.kv])
    d_gain[...] += jnp.sum(d_normed * unit, axis=0, keepdims=True)
    d_node[b] = normalised_back(d_normed * gain, unit, node_scale)


def perceiver_scratch(length, width, per_sim):
    queries = 2 * per_sim
    return {
        "keyval_t": pltpu.VMEM((2 * width, length), LOW),
        "first_in": pltpu.VMEM((queries, width), LOW),
        "query": pltpu.VMEM((queries, width), LOW),
        "weights_t": pltpu.VMEM((HEADS, length, per_sim), LOW),
        "attended_t": pltpu.VMEM((width, queries), LOW),
        "second_t": pltpu.VMEM((width, queries), LOW),
        "cot_t": pltpu.VMEM((width, queries), LOW),
        "query_t": pltpu.VMEM((width, queries), LOW),
        "d_keyval": pltpu.VMEM((length, 2 * width), LOW),
    }


def whole_call(body, outs, scratch, flops, **named):
    spec = pl.BlockSpec(memory_space=pltpu.VMEM)
    return pl.pallas_call(
        body,
        out_shape=outs,
        in_specs=[spec] * len(named["args"]),
        out_specs=[spec] * len(outs),
        scratch_shapes=scratch,
        compiler_params=pltpu.CompilerParams(vmem_limit_bytes=VMEM_BYTES),
        cost_estimate=pl.CostEstimate(flops=flops, bytes_accessed=1 << 23, transcendentals=0),
        name=named["name"],
    )(*named["args"])


def forward_call(cols, packed, points, tokens, neighbours):
    count, length, width = points.shape
    near = neighbours.shape[-1]

    def body(packed, points, tokens, neighbours, mixed, slope, slope_sum, node, source, target):
        def step(b, carry):
            message_forward(
                b, cols, packed, points, tokens, neighbours, source, target, mixed, slope, slope_sum, node
            )
            return carry

        lax.fori_loop(0, count, step, 0)

    shape = jax.ShapeDtypeStruct
    return whole_call(
        body,
        [
            shape((count, length, width), LOW),
            shape((count, near, length, width), LOW),
            shape((count, length, width), WIDE),
            shape((count, length, width), WIDE),
        ],
        [pltpu.VMEM((length, width), LOW), pltpu.VMEM((length, width), WIDE)],
        10**9,
        args=(packed, points, tokens, neighbours),
        name="message_forward",
    )


def perceiver_call(cols, packed, node, segments, condition, cotangent):
    count, length, width = node.shape
    per_sim = cols.base.stop - cols.base.start
    names = list(perceiver_scratch(length, width, per_sim))

    def body(packed, node, segments, condition, cotangent, latents, grads, d_node, *rest):
        modulation, base_unit, base_rows, base_scale, gain_row, d_gain, d_base_unit, d_base, d_mod = rest[:9]
        scr = dict(zip(names, rest[9:]))
        grads[...] = jnp.zeros_like(grads)
        base = packed[:, cols.base].astype(WIDE).T
        base_rows[...] = base
        unit, scale = normalised(base)
        base_unit[...] = unit
        base_scale[...] = scale
        gain_row[...] = packed[:, cols.gain].astype(WIDE).T[:1]
        for b in range(count):
            modulation[b] = product(condition[b], packed[:, cols.mod])
        d_gain[...] = jnp.zeros_like(d_gain)
        d_base_unit[...] = jnp.zeros_like(d_base_unit)
        d_base[...] = jnp.zeros_like(d_base)

        def step(b, carry):
            perceiver(
                b, cols, packed, node, segments, modulation, base_unit, base_rows, gain_row, cotangent,
                latents, grads, d_node, d_gain, d_base_unit, d_base, d_mod, scr,
            )
            return carry

        lax.fori_loop(0, count, step, 0)
        d_rows = normalised_back(d_base_unit[...], base_unit[...], base_scale[...]) + d_base[...]
        grads[:, cols.base] = d_rows.T
        grads[:, cols.gain] = jnp.broadcast_to(d_gain[...], (128, width)).T
        for b in range(count):
            grads[:, cols.mod] += trans_left(condition[b], d_mod[b].astype(LOW))

    shape = jax.ShapeDtypeStruct
    return whole_call(
        body,
        [
            shape((count, 2 * per_sim, width), LOW),
            shape((width, cols.total), WIDE),
            shape((count, length, width), WIDE),
        ],
        [
            pltpu.VMEM((count, 2, 4 * width), WIDE),
            pltpu.VMEM((per_sim, width), WIDE),
            pltpu.VMEM((per_sim, width), WIDE),
            pltpu.VMEM((per_sim, 1), WIDE),
            pltpu.VMEM((1, width), WIDE),
            pltpu.VMEM((1, width), WIDE),
            pltpu.VMEM((per_sim, width), WIDE),
            pltpu.VMEM((per_sim, width), WIDE),
            pltpu.VMEM((count, 2, 4 * width), WIDE),
        ]
        + list(perceiver_scratch(length, width, per_sim).values()),
        10**10,
        args=(packed, node, segments, condition, cotangent),
        name="perceiver",
    )


def backward_call(cols, packed, points, tokens, neighbours_t, mixed, slope, slope_sum, d_node):
    count, length, width = points.shape

    def body(packed, points, tokens, neighbours_t, mixed, slope, slope_sum, d_node, grads, d_points, d_tokens, total):
        grads[...] = jnp.zeros_like(grads)

        def step(b, carry):
            message_back(
                b, cols, packed, points, tokens, neighbours_t, mixed, slope, slope_sum, d_node[b], grads,
                d_points, d_tokens, total,
            )
            return carry

        lax.fori_loop(0, count, step, 0)

    shape = jax.ShapeDtypeStruct
    return whole_call(
        body,
        [
            shape((width, cols.msg_out.stop), WIDE),
            shape((count, length, width), WIDE),
            shape((count, length, width), WIDE),
        ],
        [pltpu.VMEM((length, width), WIDE)],
        10**9,
        args=(packed, points, tokens, neighbours_t, mixed, slope, slope_sum, d_node),
        name="message_back",
    )


def on_device(
    points,
    segments,
    neighbours,
    condition,
    msg_in,
    msg_out,
    norm_gain,
    mod_weight,
    query_base,
    q_weight,
    kv_weight,
    o_weight,
    up_weight,
    down_weight,
    cotangent,
):
    count, length, width = points.shape
    per = q_weight.shape[1]
    hidden = up_weight.shape[2]
    per_sim = query_base.shape[1]
    cols = Columns(width, hidden, per_sim)
    turned = msg_in[0].T
    own = jnp.concatenate(
        [
            turned[:, :width],
            turned[:, width:],
            msg_out[0],
            jnp.broadcast_to(norm_gain[0][:, None], (per, 128)),
            kv_weight[0],
            q_weight[0],
            o_weight[0],
            query_base[0].T,
            mod_weight[0],
            up_weight[0],
            down_weight[0].T,
        ],
        axis=1,
    )
    packed = lax.all_gather(own, "dp", axis=0, tiled=True)
    first_section = lax.axis_index("section") == 0
    section_size = lax.axis_size("section")
    forth = [(i, i + 1) for i in range(section_size - 1)]
    back = [(i + 1, i) for i in range(section_size - 1)]
    neighbours_t = jnp.transpose(neighbours, (0, 2, 1))
    seg_rows = segments.reshape(count, 1, length)
    _, _, _, node = forward_call(cols, packed, points, points, neighbours)
    arrived = lax.ppermute(node.astype(LOW), "section", forth)
    tokens = jnp.where(first_section, points, arrived)
    mixed, slope, slope_sum, node = forward_call(cols, packed, points, tokens, neighbours)
    latents, grads, d_node = perceiver_call(cols, packed, node, seg_rows, condition, cotangent[0])
    _, _, d_tokens = backward_call(
        cols, packed, points, tokens, neighbours_t, mixed, slope, slope_sum, d_node
    )
    returned = lax.ppermute(d_tokens.astype(LOW), "section", back)
    d_node = d_node + jnp.where(first_section, returned.astype(WIDE), 0.0)
    grads_msg, d_points, d_tokens = backward_call(
        cols, packed, points, tokens, neighbours_t, mixed, slope, slope_sum, d_node
    )
    d_points = d_points + jnp.where(first_section, d_tokens, 0.0)
    point_sum = lax.psum(d_points.astype(LOW), "section").astype(WIDE)
    grads = jnp.concatenate([grads_msg, grads[:, cols.msg_out.stop :]], axis=1)
    share = lax.psum_scatter(grads, "dp", scatter_dimension=0, tiled=True)
    share = lax.psum(share.astype(LOW), "rep").astype(WIDE)
    return (
        latents[None],
        point_sum,
        share[:, : 2 * width].T[None],
        share[None, :, cols.msg_out],
        share[None, :, cols.gain.start],
        share[None, :, cols.mod],
        share[:, cols.base].T[None],
        share[None, :, cols.q],
        share[None, :, cols.kv],
        share[None, :, cols.o],
        share[None, :, cols.up],
        share[:, cols.down].T[None],
    )


def solution(mesh):
    placed = (
        P(("dp", "rep"), None, None),
        P(("dp", "rep"), None),
        P(("dp", "rep"), None, None),
        P(("dp", "rep"), None, None),
        P("section", None, "dp"),
        P("section", "dp", None),
        P("section", "dp"),
        P("section", "dp", None),
        P("section", None, "dp"),
        P("section", "dp", None),
        P("section", "dp", None),
        P("section", "dp", None),
        P("section", "dp", None),
        P("section", None, "dp"),
        P("section", ("dp", "rep"), None, None),
    )
    return jax.shard_map(
        on_device,
        mesh=mesh,
        in_specs=placed,
        out_specs=(
            P("section", ("dp", "rep"), None, None),
            P(("dp", "rep"), None, None),
            P("section", None, "dp"),
            P("section", "dp", None),
            P("section", "dp"),
            P("section", "dp", None),
            P("section", None, "dp"),
            P("section", "dp", None),
            P("section", "dp", None),
            P("section", "dp", None),
            P("section", "dp", None),
            P("section", None, "dp"),
        ),
        check_vma=False,
    )
```

```python
import types

import jax
import jax.numpy as jnp
from jax import lax
from jax.experimental import pallas as pl
from jax.experimental.pallas import tpu as pltpu
from jax.sharding import PartitionSpec as P

HEADS = 6
HEAD_DIM = 64
EPSILON = 1e-05
TANH_ONE = 0.7978845608028654
TANH_THREE = 0.7978845608028654 * 0.044715
CUBE = TANH_THREE ** (1.0 / 3.0)
SECTION, DP, REP = "section", "dp", "rep"
LOW = jnp.bfloat16
WIDE = jnp.float32
VMEM_BYTES = 63 * 1024 * 1024


def product(left_op, right_op):
    return jnp.dot(left_op, right_op, preferred_element_type=WIDE)


def trans_left(left_op, right_op):
    return lax.dot_general(left_op, right_op, (((0,), (0,)), ((), ())), preferred_element_type=WIDE)


def trans_right(left_op, right_op):
    return lax.dot_general(left_op, right_op, (((1,), (1,)), ((), ())), preferred_element_type=WIDE)


def gelu_pair(inside):
    square = inside * inside
    half = 0.5 + 0.5 * jnp.tanh(inside * (TANH_ONE + TANH_THREE * square))
    value = inside * half
    slope = half + value * (1.0 - half) * (2.0 * TANH_ONE + 6.0 * TANH_THREE * square)
    return value, slope


def gelu_cubed(inside):
    kind = inside.dtype
    square = inside * inside
    bend = jnp.tanh(inside * (square + jnp.asarray(TANH_ONE / CUBE, kind)))
    upper = bend + jnp.asarray(1.0, kind)
    value = inside * upper
    steep = value * (jnp.asarray(1.0, kind) - bend) * (square + jnp.asarray(TANH_ONE / (3.0 * CUBE), kind))
    return value, upper * jnp.asarray(1.0 / 3.0, kind) + steep


def normalised(values):
    centre = values - jnp.mean(values, axis=-1, keepdims=True)
    spread = jnp.mean(centre * centre, axis=-1, keepdims=True)
    scale = lax.rsqrt(spread + EPSILON)
    return centre * scale, scale


def normalised_back(d_out, unit, scale):
    first = jnp.mean(d_out, axis=-1, keepdims=True)
    second = jnp.mean(d_out * unit, axis=-1, keepdims=True)
    return scale * (d_out - first - unit * second)


class Columns:
    def __init__(self, width, hidden, per_sim):
        self.pieces = (
            ("source", width),
            ("gain", 128),
            ("target", width),
            ("msg_out", width),
            ("kv", 2 * width),
            ("q", width),
            ("o", width),
            ("base", per_sim),
            ("up", hidden),
            ("down", hidden),
            ("mod", 4 * width),
        )
        at = 0
        for name, extent in self.pieces:
            setattr(self, name, slice(at, at + extent))
            at += extent
        self.total = at


def evolution_masks(b, segments, length):
    second_count = jnp.sum(segments[pl.ds(b, 1), :], axis=1, keepdims=True)
    first_count = length - second_count
    own_col = (lax.broadcasted_iota(jnp.int32, (length, 1), 0) < first_count).astype(WIDE)
    own_row = (lax.broadcasted_iota(jnp.int32, (1, length), 1) < first_count).astype(WIDE)
    return own_col, own_row


def spread_heads(values, own_col):
    lane = lax.broadcasted_iota(jnp.int32, (1, values.shape[1]), 1)
    sims = (own_col.astype(LOW), (1.0 - own_col).astype(LOW))
    halves = ((lane < HEAD_DIM).astype(WIDE).astype(LOW), (lane >= HEAD_DIM).astype(WIDE).astype(LOW))
    return [jnp.concatenate([values * sims[0] * half, values * sims[1] * half], axis=1) for half in halves]


def by_sim(rows_in, pair):
    block = 2 * HEAD_DIM
    per_sim = rows_in.shape[0] // 2
    here = slice(pair * block, (pair + 1) * block)
    return jnp.concatenate([rows_in[:per_sim, here], rows_in[per_sim:, here]], axis=1)


def mod_rows(b, scr, width):
    return (
        [scr.modulation[pl.ds(2 * b + s, 1), width * n : width * (n + 1)] for s in range(2)] for n in range(4)
    )


def first_rows(b, scr, width):
    scale_one, shift_one, _, _ = mod_rows(b, scr, width)
    rows = [(1.0 + scale_one[s]) * scr.base_unit[...] + shift_one[s] for s in range(2)]
    return jnp.concatenate(rows, axis=0).astype(LOW)


def attend(b, cols, packed, segments, scr):
    length, width = scr.node.shape[1:]
    per_sim = scr.base_rows.shape[0]
    block = 2 * HEAD_DIM
    unit, _ = normalised(scr.node[b])
    normed = (unit * scr.gain_row[...]).astype(LOW)
    keyval = product(normed, packed[:, cols.kv]).astype(LOW)
    scr.keyval[b] = keyval
    scr.keyval_t[b] = keyval.T
    own_col, own_row = evolution_masks(b, segments, length)
    low_row = (own_row.astype(LOW), (1.0 - own_row).astype(LOW))
    query = (product(first_rows(b, scr, width), packed[:, cols.q]).astype(LOW) * 0.125).astype(LOW)
    scr.query[b] = query
    mask = own_col > 0.5
    for pair in range(HEADS // 2):
        keys = spread_heads(keyval[:, pair * block : (pair + 1) * block], own_col)
        query_pair = by_sim(query, pair)
        for h in range(2):
            head = 2 * pair + h
            raw = trans_right(keys[h], query_pair)
            top_first = jnp.max(jnp.where(mask, raw, -3e38), axis=0, keepdims=True)
            top_second = jnp.max(jnp.where(mask, -3e38, raw), axis=0, keepdims=True)
            grown = jnp.exp(raw - jnp.where(mask, top_first, top_second))
            sum_first = jnp.sum(jnp.where(mask, grown, 0.0), axis=0, keepdims=True)
            sum_second = jnp.sum(jnp.where(mask, 0.0, grown), axis=0, keepdims=True)
            share = (grown * jnp.where(mask, 1.0 / sum_first, 1.0 / sum_second)).astype(LOW)
            scr.weights_t[b, head] = share
            here = slice(head * HEAD_DIM, (head + 1) * HEAD_DIM)
            value_t = scr.keyval_t[b, width + here.start : width + here.stop, :]
            value_sims = jnp.concatenate([value_t * low_row[0], value_t * low_row[1]], axis=0)
            out_t = product(value_sims, share).astype(LOW)
            scr.attended_t[b, here, :per_sim] = out_t[:HEAD_DIM]
            scr.attended_t[b, here, per_sim:] = out_t[HEAD_DIM:]


def feed_forward(b, cols, packed, cotangent, latents, grads, scr):
    width = scr.node.shape[-1]
    per_sim = scr.base_rows.shape[0]
    _, _, scale_two, shift_two = mod_rows(b, scr, width)
    attended_t = scr.attended_t[b]
    residual = trans_left(attended_t, packed[:, cols.o])
    residual = residual + jnp.concatenate([scr.base_rows[...]] * 2, axis=0)
    res_unit, res_scale = normalised(residual)
    second = jnp.concatenate(
        [(1.0 + scale_two[s]) * res_unit[s * per_sim : (s + 1) * per_sim] + shift_two[s] for s in range(2)], axis=0
    ).astype(LOW)
    cot = cotangent[b]
    scr.second_t[...] = second.T
    scr.cot_t[...] = cot.T
    lat = None
    d_second = None
    chunk = 512
    for at in range(0, cols.up.stop - cols.up.start, chunk):
        up = slice(cols.up.start + at, cols.up.start + at + chunk)
        down = slice(cols.down.start + at, cols.down.start + at + chunk)
        value, steep = gelu_cubed((product(second, packed[:, up]) * CUBE).astype(LOW))
        hidden = value * jnp.asarray(0.5 / CUBE, LOW)
        d_up = (product(cot, packed[:, down]) * 1.5).astype(LOW) * steep
        part = trans_right(hidden, packed[:, down])
        lat = part if lat is None else lat + part
        part = trans_right(d_up, packed[:, up])
        d_second = part if d_second is None else d_second + part
        grads[:, down] += product(scr.cot_t[...], hidden)
        grads[:, up] += product(scr.second_t[...], d_up)
    out_copy = pltpu.make_async_copy(scr.lat_buf, latents.at[b], scr.lat_sem)

    @pl.when(b > 0)
    def _():
        out_copy.wait()

    scr.lat_buf[...] = (residual + lat).astype(LOW)
    out_copy.start()
    d_res = []
    for s in range(2):
        rows_at = slice(s * per_sim, (s + 1) * per_sim)
        d_sim = d_second[rows_at]
        unit_sim = res_unit[rows_at]
        scr.d_mod[pl.ds(2 * b + s, 1), 2 * width : 3 * width] = jnp.sum(d_sim * unit_sim, axis=0, keepdims=True)
        scr.d_mod[pl.ds(2 * b + s, 1), 3 * width :] = jnp.sum(d_sim, axis=0, keepdims=True)
        d_res.append(
            cot[rows_at].astype(WIDE)
            + normalised_back(d_sim * (1.0 + scale_two[s]), unit_sim, res_scale[rows_at])
        )
    scr.d_base[...] += d_res[0] + d_res[1]
    res_low = jnp.concatenate(d_res, axis=0).astype(LOW)
    grads[:, cols.o] += product(attended_t, res_low)
    d_att = trans_right(packed[:, cols.o], res_low).astype(LOW)
    both = d_att.astype(WIDE) * attended_t.astype(WIDE)
    for head in range(HEADS):
        scr.overlap[b, head : head + 1, :] = jnp.sum(
            both[head * HEAD_DIM : (head + 1) * HEAD_DIM], axis=0, keepdims=True
        )
    scr.attended_t[b] = d_att


def attend_back(b, cols, packed, segments, grads, scr):
    length, width = scr.node.shape[1:]
    per_sim = scr.base_rows.shape[0]
    block = 2 * HEAD_DIM
    own_col, own_row = evolution_masks(b, segments, length)
    low_row = (own_row.astype(LOW), (1.0 - own_row).astype(LOW))
    mask = own_col > 0.5
    left_half = lax.broadcasted_iota(jnp.int32, (1, block), 1) < HEAD_DIM
    keyval = scr.keyval[b]
    query = scr.query[b]
    d_att = scr.attended_t[b]
    for pair in range(HEADS // 2):
        values = spread_heads(keyval[:, width + pair * block : width + (pair + 1) * block], own_col)
        query_pair = by_sim(query, pair)
        here = slice(pair * block, (pair + 1) * block)
        d_att_pair = jnp.concatenate([d_att[here, :per_sim], d_att[here, per_sim:]], axis=0)
        d_keys, d_values = [], []
        for h in range(2):
            head = 2 * pair + h
            there = slice(head * HEAD_DIM, (head + 1) * HEAD_DIM)
            both = scr.overlap[b, head : head + 1, :]
            share = scr.weights_t[b, head]
            d_share = product(values[h], d_att_pair)
            d_raw = (
                share.astype(WIDE) * (d_share - jnp.where(mask, both[:, :per_sim], both[:, per_sim:]))
            ).astype(LOW)
            key_t = scr.keyval_t[b, there, :]
            key_sims = jnp.concatenate([key_t * low_row[0], key_t * low_row[1]], axis=0)
            d_q = (product(key_sims, d_raw) * 0.125).astype(LOW)
            scr.query_t[there, :per_sim] = d_q[:HEAD_DIM]
            scr.query_t[there, per_sim:] = d_q[HEAD_DIM:]
            full = trans_right(share, d_att_pair)
            d_values.append(jnp.where(mask, full[:, :block], full[:, block:]))
            full = product(d_raw, query_pair)
            d_keys.append(jnp.where(mask, full[:, :block], full[:, block:]))
        scr.d_keyval[:, here] = jnp.where(left_half, d_keys[0], d_keys[1]).astype(LOW)
        scr.d_keyval[:, width + here.start : width + here.stop] = jnp.where(
            left_half, d_values[0], d_values[1]
        ).astype(LOW)

    scale_one, shift_one, _, _ = mod_rows(b, scr, width)
    d_query = scr.query_t[...].T
    grads[:, cols.q] += trans_left(first_rows(b, scr, width), d_query)
    d_first = trans_right(d_query, packed[:, cols.q])
    for s in range(2):
        d_sim = d_first[s * per_sim : (s + 1) * per_sim]
        scr.d_mod[pl.ds(2 * b + s, 1), :width] = jnp.sum(d_sim * scr.base_unit[...], axis=0, keepdims=True)
        scr.d_mod[pl.ds(2 * b + s, 1), width : 2 * width] = jnp.sum(d_sim, axis=0, keepdims=True)
        scr.d_base_unit[...] += d_sim * (1.0 + scale_one[s])

    unit, node_scale = normalised(scr.node[b])
    gain = scr.gain_row[...]
    d_kv = scr.d_keyval[...]
    grads[:, cols.kv] += trans_left((unit * gain).astype(LOW), d_kv)
    d_normed = trans_right(d_kv, packed[:, cols.kv])
    scr.d_gain[...] += jnp.sum(d_normed * unit, axis=0, keepdims=True)
    scr.node[b] = normalised_back(d_normed * gain, unit, node_scale)


def perceiver_scratch(count, length, width, per_sim):
    queries = 2 * per_sim
    return dict(
        keyval=pltpu.VMEM((count, length, 2 * width), LOW),
        keyval_t=pltpu.VMEM((count, 2 * width, length), LOW),
        query=pltpu.VMEM((count, queries, width), LOW),
        weights_t=pltpu.VMEM((count, HEADS, length, per_sim), LOW),
        attended_t=pltpu.VMEM((count, width, queries), LOW),
        overlap=pltpu.VMEM((count, 8, queries), WIDE),
        second_t=pltpu.VMEM((width, queries), LOW),
        cot_t=pltpu.VMEM((width, queries), LOW),
        query_t=pltpu.VMEM((width, queries), LOW),
        d_keyval=pltpu.VMEM((length, 2 * width), LOW),
    )


def one_hot(near_t, edges, columns, length):
    picks = []
    for k in edges:
        row = near_t[k : k + 1, columns].astype(jnp.int16)
        spot = lax.broadcasted_iota(jnp.int16, (length, row.shape[1]), 0)
        picks.append(jnp.where(row == spot, jnp.asarray(1.0, LOW), jnp.asarray(0.0, LOW)))
    return jnp.concatenate(picks, axis=1)


def message_half(b, half, cols, packed, points, tokens, neighbours, scr):
    length, width = points.shape[1:]
    count = neighbours.shape[1]
    part = length // 2
    here = slice(half * part, (half + 1) * part)
    if half == 0:
        scr.source_t[...] = (trans_right(packed[:, cols.source], points[b]) * CUBE).astype(LOW)
    target = (trans_right(packed[:, cols.target], tokens[b, here, :]) * CUBE).astype(LOW)
    target = jnp.concatenate([target, target], axis=1)
    near_t = neighbours[b]
    group = 8
    for at in range(0, count, group):
        value, steep = None, None
        for k in range(at, at + group, 2):
            inside = product(scr.source_t[...], one_hot(near_t, (k, k + 1), here, length)).astype(LOW) + target
            v, t = gelu_cubed(inside)
            scr.slope[b, k, :, here] = t[:, :part]
            scr.slope[b, k + 1, :, here] = t[:, part:]
            v, t = v[:, :part] + v[:, part:], t[:, :part] + t[:, part:]
            value, steep = (v, t) if value is None else (value + v, steep + t)
        if at == 0:
            scr.value_sum[...] = value.astype(WIDE)
            scr.slope_sum[b, :, here] = steep.astype(WIDE)
        else:
            scr.value_sum[...] += value.astype(WIDE)
            scr.slope_sum[b, :, here] += steep.astype(WIDE)
    mixed = (scr.value_sum[...] * (0.5 / (count * CUBE))).astype(LOW)
    scr.mixed_t[b, :, here] = mixed
    scr.node[b, here, :] = tokens[b, here, :].astype(WIDE) + trans_left(mixed, packed[:, cols.msg_out])


def token_back(b, cols, packed, tokens, scr, grads):
    count = scr.slope.shape[1]
    d_out = scr.node[b]
    node_low = d_out.astype(LOW)
    grads[:, cols.msg_out] += product(scr.mixed_t[b], node_low)
    d_mixed = trans_right(packed[:, cols.msg_out], node_low) * (1.5 / count)
    scr.mixed_low[b] = d_mixed.astype(LOW)
    d_target = (d_mixed * scr.slope_sum[b]).astype(LOW)
    grads[:, cols.target] += product(d_target, tokens[b])
    return d_out + trans_left(d_target, packed[:, cols.target])


def source_back(b, cols, packed, points, neighbours, scr, grads):
    length = points.shape[1]
    count = neighbours.shape[1]
    near_t = neighbours[b]
    group = 4
    low = scr.mixed_low[b]
    for at in range(0, count, group):
        edges = range(at, at + group)
        inside = jnp.concatenate([scr.slope[b, k] * low for k in edges], axis=1)
        part = trans_right(inside, one_hot(near_t, edges, slice(0, length), length))
        if at == 0:
            scr.total[...] = part
        else:
            scr.total[...] += part
    d_source = scr.total[...].astype(LOW)
    grads[:, cols.source] += product(d_source, points[b])
    return trans_left(d_source, packed[:, cols.source])


def remote(src, dst, send, recv, to):
    return pltpu.make_async_remote_copy(
        src_ref=src, dst_ref=dst, send_sem=send, recv_sem=recv, device_id=to, device_id_type=pl.DeviceIdType.MESH
    )


class Gather:
    def __init__(self, place, packed, per, groups, sems):
        self.section, self.dp, self.rep, self.chips = place
        self.packed, self.per, self.groups = packed, per, groups
        self.core = lax.rem(self.dp, 2)
        self.chip = self.dp // 2
        self.sems = sems
        self.line = self.chips == 4

    def rows(self, dp):
        return pl.ds(pl.multiple_of(dp * self.per, 16), self.per)

    def half(self, group, which):
        start, stop = self.groups[group]
        size = (stop - start) // 2
        return pl.ds(pl.multiple_of(start + which * size, 128), size)

    def whole(self, group):
        start, stop = self.groups[group]
        return pl.ds(start, stop - start)

    def source_dp(self, k, core):
        return 2 * lax.rem(self.chip - k + self.chips, self.chips) + core

    def copy(self, kind, group, k, dp, columns, to):
        spot = self.packed.at[self.rows(dp), columns]
        at = group * self.chips + k
        return remote(spot, spot, self.sems[0].at[kind, at], self.sems[1].at[kind, at], to)

    def along(self, group, k, dp):
        far = 2 * lax.rem(self.chip + k, self.chips) + self.core
        return self.copy(0, group, k, dp, self.half(group, self.rep), (self.section, far, self.rep))

    def over_rep(self, group, k, dp, which):
        return self.copy(1, group, k, dp, self.half(group, which), (self.section, self.dp, 1 - self.rep))

    def sibling(self):
        return (self.section, 2 * self.chip + 1 - self.core, self.rep)

    def over_core(self, kind, group, k, dp, which):
        return self.copy(kind, group, k, dp, self.half(group, which), self.sibling())

    def own_core(self, group, dp):
        return self.copy(4, group, 0, dp, self.whole(group), self.sibling())

    def ends(self, k):
        return jnp.abs(lax.rem(self.chip + k, self.chips) - self.chip) == self.chips - 1

    def onward(self, group):
        to, k = 3 * (self.chip - 1), 2 * self.chip - 1
        spot = self.packed.at[self.rows(self.source_dp(2, self.core)), self.half(group, self.rep)]
        send, recv = self.sems[0].at[5, group * self.chips], self.sems[1].at[0, group * self.chips + k]
        return remote(spot, spot, send, recv, (self.section, 2 * to + self.core, self.rep))

    def inner(self):
        return (self.chip == 1) | (self.chip == 2)

    def begin(self, group):
        for k in range(1, self.chips):
            if self.line:

                @pl.when(jnp.logical_not(self.ends(k)))
                def _():
                    self.along(group, k, self.dp).start()

            else:
                self.along(group, k, self.dp).start()
        self.own_core(group, self.dp).start()

    def middle(self, group):
        order = list(range(1, self.chips))
        if self.line:
            last = jnp.where(self.chip == 0, 1, 3)
            order = [2, 4 - last, last]
        for n, k in enumerate(order):
            dp = self.source_dp(k, self.core)
            self.along(group, k, dp).wait_recv()
            if self.line and n == 0:

                @pl.when(self.inner())
                def _():
                    self.onward(group).start()

            self.over_rep(group, k, dp, self.rep).start()
            self.over_core(2, group, k, dp, self.rep).start()

    def late(self, group):
        for k in range(1, self.chips):
            dp = self.source_dp(k, self.core)
            self.over_rep(group, k, dp, 1 - self.rep).wait_recv()
            self.over_core(3, group, k, dp, 1 - self.rep).start()

    def finish(self, group):
        self.own_core(group, 2 * self.chip + 1 - self.core).wait_recv()
        for k in range(1, self.chips):
            dp = self.source_dp(k, 1 - self.core)
            self.over_core(2, group, k, dp, self.rep).wait_recv()
            self.over_core(3, group, k, dp, 1 - self.rep).wait_recv()

    def drain(self):
        for group in range(len(self.groups)):
            self.own_core(group, self.dp).wait_send()
            if self.line:

                @pl.when(self.inner())
                def _():
                    self.onward(group).wait_send()

            for k in range(1, self.chips):
                dp = self.source_dp(k, self.core)
                if self.line:

                    @pl.when(jnp.logical_not(self.ends(k)))
                    def _():
                        self.along(group, k, self.dp).wait_send()

                else:
                    self.along(group, k, self.dp).wait_send()
                self.over_rep(group, k, dp, self.rep).wait_send()
                self.over_core(2, group, k, dp, self.rep).wait_send()
                self.over_core(3, group, k, dp, 1 - self.rep).wait_send()


class Scatter:
    def __init__(self, place, grads, share, per, columns, sems, at, bufs):
        self.section, self.dp, self.rep, self.chips = place
        self.grads, self.share, self.per, self.columns = grads, share, per, columns
        self.core = lax.rem(self.dp, 2)
        self.chip = self.dp // 2
        self.sems, self.at = sems, at
        self.core_out, self.core_in, self.rep_in, self.far_in, self.end_out, self.end_in = bufs
        self.size = (columns[1] - columns[0]) // 2
        self.rep_out = self.core_out.at[:, :, : self.size]
        self.far_out = self.core_out.at[:, :, self.size :]

    def rows(self, chip, core):
        return pl.ds(pl.multiple_of((2 * chip + core) * self.per, 16), self.per)

    def half(self, which):
        return pl.ds(pl.multiple_of(self.columns[0] + which * self.size, 128), self.size)

    def local(self, which):
        return pl.ds(pl.multiple_of(which * self.size, 128), self.size)

    def pair(self, kind):
        return self.sems[0].at[self.at, kind], self.sems[1].at[self.at, kind]

    def core_copy(self):
        to = (self.section, 2 * self.chip + 1 - self.core, self.rep)
        return remote(self.core_out, self.core_in, *self.pair(0), to)

    def rep_copy(self):
        return remote(self.rep_out, self.rep_in, *self.pair(1), (self.section, self.dp, 1 - self.rep))

    def far_copy(self, k):
        to = (self.section, 2 * lax.rem(self.chip + k, self.chips) + self.core, self.rep)
        return remote(self.far_out.at[k - 1], self.far_in.at[k - 1], *self.pair(2 + k), to)

    def end_copy(self):
        return remote(self.end_out, self.end_in, *self.pair(2), (self.section, self.dp, 1 - self.rep))

    def begin(self):
        start, stop = self.columns
        for chip in range(self.chips):
            self.core_out[chip] = self.grads[self.rows(chip, 1 - self.core), start:stop].astype(LOW)
        self.core_copy().start()

    def middle(self):
        self.core_copy().wait()
        for chip in range(self.chips):
            rows = self.rows(chip, self.core)
            other = self.grads[rows, self.half(1 - self.rep)]
            self.rep_out[chip] = (other + self.core_in[chip, :, self.local(1 - self.rep)].astype(WIDE)).astype(LOW)
        self.rep_copy().start()

    def late(self):
        self.rep_copy().wait_recv()
        for k in range(self.chips):
            chip = lax.rem(self.chip + k, self.chips)
            rows = self.rows(chip, self.core)
            mine = self.grads[rows, self.half(self.rep)]
            mine = mine + self.core_in[chip, :, self.local(self.rep)].astype(WIDE)
            mine = mine + self.rep_in[chip].astype(WIDE)
            if k == 0:
                self.grads[rows, self.half(self.rep)] = mine
            else:
                self.far_out[k - 1] = mine.astype(LOW)
                self.far_copy(k).start()

    def finish(self):
        total = self.grads[self.rows(self.chip, self.core), self.half(self.rep)]
        for k in range(1, self.chips):
            self.far_copy(k).wait_recv()
            total = total + self.far_in[k - 1].astype(WIDE)
        low = total.astype(LOW)
        self.end_out[...] = low
        self.end_copy().start()
        self.share[:, self.half(self.rep)] = low

    def end(self):
        self.end_copy().wait_recv()
        self.share[:, self.half(1 - self.rep)] = self.end_in[...]
        self.rep_copy().wait_send()
        self.end_copy().wait_send()
        for k in range(1, self.chips):
            self.far_copy(k).wait_send()


class Packets:
    def __init__(self, place, scr):
        self.section, self.dp, self.rep, self.chips = place
        self.core, self.chip = lax.rem(self.dp, 2), self.dp // 2
        self.scr = scr
        self.rows = scr.d_mod.shape[0]

    def copy(self, spot, at, to):
        sems = self.scr.packet_sems
        return remote(spot, spot, sems.at[0, at], sems.at[1, at], to)

    def along(self, k, chip):
        spot = self.scr.packets.at[self.core, self.rep, chip]
        far = 2 * lax.rem(self.chip + k, self.chips) + self.core
        return self.copy(spot, k, (self.section, far, self.rep))

    def over_rep(self, rep):
        return self.copy(self.scr.packets.at[self.core, rep], 0, (self.section, self.dp, 1 - self.rep))

    def over_core(self, core):
        to = (self.section, 2 * self.chip + 1 - self.core, self.rep)
        return self.copy(self.scr.packets.at[core], self.chips, to)

    def begin(self):
        scr, width = self.scr, self.scr.node.shape[-1]
        spot = scr.packets.at[self.core, self.rep, self.chip]
        size = 2 * self.rows
        for n in range(2):
            pieces = [scr.d_mod[:, (2 * n + m) * width : (2 * n + m + 1) * width] for m in range(2)]
            spot[n * size : (n + 1) * size, :] = jnp.concatenate(pieces, axis=0).astype(LOW)
        spot[2 * size :, :] = scr.condition[...].astype(LOW)
        for k in range(1, self.chips):
            self.along(k, self.chip).start()

    def middle(self):
        for k in range(1, self.chips):
            self.along(k, lax.rem(self.chip - k + self.chips, self.chips)).wait_recv()
        self.over_rep(self.rep).start()

    def late(self):
        self.over_rep(1 - self.rep).wait_recv()
        self.over_core(self.core).start()

    def finish(self, out, per):
        self.over_core(1 - self.core).wait_recv()
        scr, width, rows = self.scr, self.scr.node.shape[-1], self.rows
        size = 2 * rows
        total = 4 * self.chips

        def gathered(piece):
            part = scr.packets[:, :, :, piece * size : (piece + 1) * size, :].astype(WIDE)
            part = part.reshape(total, 2, rows, width)
            return [part[:, m].reshape(total * rows, width).astype(LOW) for m in range(2)]

        scr.turned[...] = gathered(2)[0].T
        mine = scr.turned[pl.ds(pl.multiple_of(self.dp * per, 16), per), :]
        for n in range(2):
            for m, part in enumerate(gathered(n)):
                at = 2 * n + m
                out[:, at * width : (at + 1) * width] = product(mine, part)
        for k in range(1, self.chips):
            self.along(k, self.chip).wait_send()
        self.over_rep(self.rep).wait_send()
        self.over_core(self.core).wait_send()


def layer_call(cols, linked, sizes, packed_in, raw, points, segments, neighbours, condition, cotangent, per):
    count, length, width = points.shape
    near = neighbours.shape[1]
    per_sim = cols.base.stop - cols.base.start
    chips = sizes[DP] // 2
    part = length // 2
    groups = (
        (0, cols.msg_out.stop),
        (cols.kv.start, cols.base.stop),
        (cols.mod.start, cols.mod.stop),
        (cols.up.start, cols.up.stop),
        (cols.down.start, cols.down.stop),
    )
    summed = (
        (0, cols.gain.stop),
        (cols.target.start, cols.msg_out.stop),
        (cols.kv.start, cols.base.stop),
        (cols.up.start, cols.down.stop),
    )
    many = cols.mod.start
    rows = 8
    weights_in = list(raw) if linked else [packed_in]
    inputs = weights_in + [points, segments, neighbours, condition, cotangent]
    shape = jax.ShapeDtypeStruct
    hidden = cols.up.stop - cols.up.start
    outs = [
        shape((count, 2 * per_sim, width), LOW),
        shape((count, length, width), WIDE),
    ]
    outs.append(shape((per, many), LOW) if linked else shape((width, many), WIDE))
    outs.append(shape((per if linked else width, 4 * width), WIDE))
    scratch = dict(
        source_t=pltpu.VMEM((width, length), LOW),
        value_sum=pltpu.VMEM((width, part), WIDE),
        tokens=pltpu.VMEM((count, length, width), LOW),
        passed=pltpu.VMEM((count, length, width), LOW),
        mixed_t=pltpu.VMEM((count, width, length), LOW),
        slope=pltpu.VMEM((count, near, width, length), LOW),
        slope_sum=pltpu.VMEM((count, width, length), WIDE),
        node=pltpu.VMEM((count, length, width), WIDE),
        mixed_low=pltpu.VMEM((count, width, length), LOW),
        total=pltpu.VMEM((width, length), WIDE),
        point_out=pltpu.VMEM((count, length, width), LOW),
        point_in=pltpu.VMEM((count, length, width), LOW),
        back_in=pltpu.VMEM((count, length, width), LOW),
        modulation=pltpu.VMEM((rows, 4 * width), WIDE),
        condition=pltpu.VMEM((2 * rows, width), WIDE),
        base_unit=pltpu.VMEM((per_sim, width), WIDE),
        base_rows=pltpu.VMEM((per_sim, width), WIDE),
        base_scale=pltpu.VMEM((per_sim, 1), WIDE),
        gain_row=pltpu.VMEM((1, width), WIDE),
        d_gain=pltpu.VMEM((1, width), WIDE),
        d_base_unit=pltpu.VMEM((per_sim, width), WIDE),
        d_base=pltpu.VMEM((per_sim, width), WIDE),
        d_mod=pltpu.VMEM((rows, 4 * width), WIDE),
        lat_buf=pltpu.VMEM((2 * per_sim, width), LOW),
        lat_sem=pltpu.SemaphoreType.DMA,
        pass_sems=pltpu.SemaphoreType.DMA((2, 2 * count)),
        back_sems=pltpu.SemaphoreType.DMA((2, count)),
        point_sems=pltpu.SemaphoreType.DMA((2, count)),
    )
    scratch.update(perceiver_scratch(count, length, width, per_sim))
    bufs = []
    if linked:
        scratch.update(
            packed=pltpu.VMEM((width, cols.total), LOW),
            grads=pltpu.VMEM((width, many), WIDE),
            packets=pltpu.VMEM((2, 2, chips, 6 * rows, width), LOW),
            turned=pltpu.VMEM((width, 4 * chips * rows), LOW),
            packet_sems=pltpu.SemaphoreType.DMA((2, chips + 2)),
            gather_send=pltpu.SemaphoreType.DMA((6, len(groups) * chips)),
            gather_recv=pltpu.SemaphoreType.DMA((6, len(groups) * chips)),
            scatter_send=pltpu.SemaphoreType.DMA((len(summed), 2 + chips)),
            scatter_recv=pltpu.SemaphoreType.DMA((len(summed), 2 + chips)),
        )
        for start, stop in summed:
            size = stop - start
            bufs += [
                pltpu.VMEM((chips, per, size), LOW),
                pltpu.VMEM((chips, per, size), LOW),
                pltpu.VMEM((chips, per, size // 2), LOW),
                pltpu.VMEM((chips - 1, per, size // 2), LOW),
                pltpu.VMEM((per, size // 2), LOW),
                pltpu.VMEM((per, size // 2), LOW),
            ]
    names = list(scratch)

    def body(*refs):
        ins, refs = refs[: len(inputs)], refs[len(inputs) :]
        results, refs = refs[: len(outs)], refs[len(outs) :]
        scr = types.SimpleNamespace(**dict(zip(names, refs)))
        moved = refs[len(names) :]
        points, segments, neighbours, condition, cotangent = ins[-5:]
        latents, point_sum = results[:2]
        section, dp, rep = (lax.axis_index(name) for name in (SECTION, DP, REP))
        other = (1 - section, dp, rep)
        if linked:
            packed, grads = scr.packed, scr.grads
            core, chip = lax.rem(dp, 2), dp // 2
            partners = [other, (section, dp, 1 - rep), (section, 2 * chip + 1 - core, rep)]
            partners += [(section, 2 * lax.rem(chip + k, chips) + core, rep) for k in range(1, chips)]
        else:
            packed, grads = ins[0], results[2]
            partners = [other]
        barrier = pltpu.get_barrier_semaphore()
        for to in partners:
            pl.semaphore_signal(barrier, inc=1, device_id=to, device_id_type=pl.DeviceIdType.MESH)
        if linked:
            place = (section, dp, rep, chips)
            gather = Gather(place, packed, per, groups, (scr.gather_send, scr.gather_recv))
            msg_in, msg_out, norm_gain, mod_weight, query_base, q_weight, kv_weight, o_weight, up_weight, down_weight = ins[:10]
            mine = gather.rows(dp)
            packed[mine, cols.source] = msg_in[0, :, :width]
            packed[mine, cols.target] = msg_in[0, :, width:]
            packed[mine, cols.msg_out] = msg_out[0]
            gain = jnp.broadcast_to(norm_gain[...].astype(WIDE), (128, per)).T
            packed[mine, cols.gain] = gain.astype(LOW)
            packed[mine, cols.kv] = kv_weight[0]
            packed[mine, cols.q] = q_weight[0]
            packed[mine, cols.o] = o_weight[0]
            packed[mine, cols.base] = query_base[0]
            packed[mine, cols.mod] = mod_weight[0]
            packed[mine, cols.up] = up_weight[0]
            packed[mine, cols.down] = down_weight[0]
        pl.semaphore_wait(barrier, len(partners))
        if linked:
            for group in range(len(groups)):
                gather.begin(group)
        grads[...] = jnp.zeros_like(grads)
        for total in (scr.d_gain, scr.d_base_unit, scr.d_base, scr.d_mod, scr.condition):
            total[...] = jnp.zeros_like(total)
        for b in range(count):
            scr.condition[2 * b : 2 * b + 2, :] = condition[b].astype(WIDE)

        tokens = scr.tokens

        @pl.when(section == 0)
        def _():
            tokens[...] = points[...]

        if linked:
            gather.middle(0)
            gather.late(0)
            gather.finish(0)

        def pass_copy(n):
            b, half = n // 2, lax.rem(n, 2)
            rows = pl.ds(pl.multiple_of(half * part, part), part)
            return remote(
                scr.passed.at[b, rows, :], tokens.at[b, rows, :], scr.pass_sems.at[0, n], scr.pass_sems.at[1, n], other
            )

        def back_copy(b):
            return remote(scr.passed.at[b], scr.back_in.at[b], scr.back_sems.at[0, b], scr.back_sems.at[1, b], other)

        def point_copy(b):
            return remote(scr.point_out.at[b], scr.point_in.at[b], scr.point_sems.at[0, b], scr.point_sems.at[1, b], other)

        def forward(b, carry):
            for half in range(2):
                n = 2 * b + half

                @pl.when(section == 1)
                def _():
                    pass_copy(n).wait_recv()

                message_half(b, half, cols, packed, points, tokens, neighbours, scr)

                @pl.when(section == 0)
                def _():
                    rows = slice(half * part, (half + 1) * part)
                    scr.passed[b, rows, :] = scr.node[b, rows, :].astype(LOW)
                    pass_copy(n).start()

            if linked:

                @pl.when(b == 0)
                def _():
                    gather.middle(1)

                @pl.when(b == 1)
                def _():
                    gather.late(1)
                    gather.middle(2)

            return carry

        lax.fori_loop(0, count, forward, 0)
        if linked:
            gather.late(2)
            gather.finish(1)
            gather.middle(3)
            gather.finish(2)
            scatters = [
                Scatter(
                    place, grads, results[2], per, summed[n], (scr.scatter_send, scr.scatter_recv), n,
                    moved[6 * n : 6 * n + 6],
                )
                for n in range(len(summed))
            ]
        base = packed[:, cols.base].astype(WIDE).T
        scr.base_rows[...] = base
        unit, scale = normalised(base)
        scr.base_unit[...] = unit
        scr.base_scale[...] = scale
        scr.gain_row[...] = packed[:, cols.gain].astype(WIDE).T[:1]
        scr.modulation[...] = product(scr.condition[...].astype(LOW), packed[:, cols.mod])[:rows]

        def attention(b, carry):
            attend(b, cols, packed, segments, scr)
            if linked:

                @pl.when(b == 0)
                def _():
                    gather.late(3)
                    gather.middle(4)

                @pl.when(b == 1)
                def _():
                    gather.late(4)

            return carry

        lax.fori_loop(0, count, attention, 0)
        if linked:
            gather.finish(3)
            gather.finish(4)

        def feed(b, carry):
            feed_forward(b, cols, packed, cotangent, latents, grads, scr)
            return carry

        lax.fori_loop(0, count, feed, 0)
        if linked:
            scatters[3].begin()

        def token_step(b):
            return token_back(b, cols, packed, tokens, scr, grads)

        def attention_back(b, carry):
            attend_back(b, cols, packed, segments, grads, scr)

            @pl.when(section == 1)
            def _():
                scr.passed[b] = token_step(b).astype(LOW)
                back_copy(b).start()

            if linked:

                @pl.when(b == 0)
                def _():
                    scatters[3].middle()

            return carry

        lax.fori_loop(0, count, attention_back, 0)
        d_rows = normalised_back(scr.d_base_unit[...], scr.base_unit[...], scr.base_scale[...])
        grads[:, cols.base] = (d_rows + scr.d_base[...]).T
        grads[:, cols.gain] = jnp.broadcast_to(scr.d_gain[...], (128, width)).T
        if linked:
            packet = Packets(place, scr)
            scatters[2].begin()
            packet.begin()
            scatters[3].late()
        else:
            results[3][...] = trans_left(scr.condition[:rows].astype(LOW), scr.d_mod[...].astype(LOW))

        def backward(b, carry):
            point_sum[b] = jnp.zeros((length, width), WIDE)

            @pl.when(section == 0)
            def _():
                back_copy(b).wait_recv()
                scr.node[b] = scr.node[b] + scr.back_in[b].astype(WIDE)
                point_sum[b] = token_step(b)

            if linked:

                @pl.when(b == count - 1)
                def _():
                    scatters[1].begin()

            d_points = source_back(b, cols, packed, points, neighbours, scr, grads)
            scr.point_out[b] = (point_sum[b] + d_points).astype(LOW)
            point_copy(b).start()
            if linked:

                @pl.when(b == 0)
                def _():
                    scatters[2].middle()
                    packet.middle()

                @pl.when(b == 1)
                def _():
                    scatters[3].finish()
                    packet.late()

            return carry

        lax.fori_loop(0, count, backward, 0)
        if linked:
            scatters[0].begin()
            scatters[1].middle()
            scatters[0].middle()
            scatters[2].late()
            scatters[3].end()
            scatters[1].late()
            scatters[0].late()
            packet.finish(results[3], per)
            scatters[2].finish()
        for b in range(count):
            point_copy(b).wait_recv()
            point_sum[b] = scr.point_out[b].astype(WIDE) + scr.point_in[b].astype(WIDE)
        if linked:
            scatters[1].finish()
            scatters[0].finish()
            for n in (2, 1, 0):
                scatters[n].end()
            gather.drain()

        pltpu.make_async_copy(scr.lat_buf, latents.at[count - 1], scr.lat_sem).wait()

        @pl.when(section == 0)
        def _():
            for n in range(2 * count):
                pass_copy(n).wait_send()

        @pl.when(section == 1)
        def _():
            for b in range(count):
                back_copy(b).wait_send()

        for b in range(count):
            point_copy(b).wait_send()

    spec = pl.BlockSpec(memory_space=pltpu.VMEM)
    return pl.pallas_call(
        body,
        out_shape=outs,
        in_specs=[spec] * len(inputs),
        out_specs=[pl.BlockSpec(memory_space=pl.ANY)] + [spec] * (len(outs) - 1),
        scratch_shapes=list(scratch.values()) + bufs,
        compiler_params=pltpu.CompilerParams(
            vmem_limit_bytes=VMEM_BYTES, collective_id=0, has_side_effects=True
        ),
        cost_estimate=pl.CostEstimate(flops=10**10, bytes_accessed=1 << 24, transcendentals=0),
        name="layers",
    )(*inputs)


def finish_call(cols, latents, point_sum, share, mod_share):
    per, width = share.shape[0], point_sum.shape[-1]
    pieces = (cols.msg_out, cols.gain, cols.base, cols.q, cols.kv, cols.o, cols.up, cols.down)
    gain_at = 1

    def body(latents, point_sum, mod_share, share, latents_out, point_out, mod_out, msg_in_out, *rest):
        outs, (latents_buf, point_buf, mod_buf, sems) = rest[:-4], rest[-4:]
        arrays = ((latents, latents_buf, latents_out), (point_sum, point_buf, point_out), (mod_share, mod_buf, mod_out))
        arriving = [pltpu.make_async_copy(a, buf, sems.at[0, n]) for n, (a, buf, _) in enumerate(arrays)]
        leaving = [pltpu.make_async_copy(buf, a, sems.at[1, n]) for n, (_, buf, a) in enumerate(arrays)]
        for move in arriving:
            move.start()
        for first, then in zip(arriving, leaving):
            first.wait()
            then.start()
        msg_in_out[0, :, :width] = share[:, cols.source].astype(WIDE)
        msg_in_out[0, :, width:] = share[:, cols.target].astype(WIDE)
        for n, piece in enumerate(pieces):
            value = share[:, piece].astype(WIDE)
            if n == gain_at:
                outs[n][...] = value.T[:1]
            else:
                outs[n][0] = value
        for move in leaving:
            move.wait()

    shape = jax.ShapeDtypeStruct
    whole, local = pl.BlockSpec(memory_space=pl.ANY), pl.BlockSpec(memory_space=pltpu.VMEM)
    outs = [shape(latents.shape, LOW), shape(point_sum.shape, WIDE), shape(mod_share.shape, WIDE)]
    outs.append(shape((1, per, 2 * width), WIDE))
    for n, piece in enumerate(pieces):
        outs.append(shape((1, per) if n == gain_at else (1, per, piece.stop - piece.start), WIDE))
    latents, point_sum, mod, msg_in, msg_out, gain, base, q, kv, o, up, down = pl.pallas_call(
        body,
        out_shape=outs,
        in_specs=[whole, whole, whole, local],
        out_specs=[whole, whole, whole] + [local] * (1 + len(pieces)),
        scratch_shapes=[pltpu.VMEM(a.shape, a.dtype) for a in (latents, point_sum, mod_share)]
        + [pltpu.SemaphoreType.DMA((2, 3))],
        compiler_params=pltpu.CompilerParams(vmem_limit_bytes=VMEM_BYTES),
        cost_estimate=pl.CostEstimate(flops=10**6, bytes_accessed=1 << 23, transcendentals=0),
        name="finish",
    )(latents, point_sum, mod_share, share)
    turn = lambda array: jnp.swapaxes(array, 1, 2)
    return (latents[None], point_sum, turn(msg_in), msg_out, gain, mod[None], turn(base), q, kv, o, up, turn(down))


def on_device(
    points,
    segments,
    neighbours,
    condition,
    msg_in,
    msg_out,
    norm_gain,
    mod_weight,
    query_base,
    q_weight,
    kv_weight,
    o_weight,
    up_weight,
    down_weight,
    cotangent,
):
    count, length, width = points.shape
    per = q_weight.shape[1]
    hidden = up_weight.shape[2]
    per_sim = query_base.shape[1]
    cols = Columns(width, hidden, per_sim)
    sizes = {name: lax.axis_size(name) for name in (SECTION, DP, REP)}
    linked = per % 16 == 0 and sizes[DP] % 2 == 0 and sizes[REP] == 2
    raw = (
        jnp.swapaxes(msg_in, 1, 2),
        msg_out,
        norm_gain,
        mod_weight,
        jnp.swapaxes(query_base, 1, 2),
        q_weight,
        kv_weight,
        o_weight,
        up_weight,
        jnp.swapaxes(down_weight, 1, 2),
    )
    near_t = jnp.swapaxes(neighbours, 1, 2)
    if linked:
        outs = layer_call(cols, True, sizes, None, raw, points, segments, near_t, condition, cotangent[0], per)
        return finish_call(cols, *outs)
    turned = msg_in[0].T
    own = jnp.concatenate(
        [
            turned[:, :width],
            jnp.broadcast_to(norm_gain[0][:, None], (per, 128)),
            turned[:, width:],
            msg_out[0],
            kv_weight[0],
            q_weight[0],
            o_weight[0],
            query_base[0].T,
            up_weight[0],
            down_weight[0].T,
            mod_weight[0],
        ],
        axis=1,
    )
    packed = lax.all_gather(own, DP, axis=0, tiled=True)
    latents, point_sum, grads, mod_grads = layer_call(
        cols, False, sizes, packed, None, points, segments, near_t, condition, cotangent[0], per
    )
    grads = jnp.concatenate([grads, mod_grads], axis=1)
    share = lax.psum_scatter(grads, DP, scatter_dimension=0, tiled=True)
    share = lax.psum(share.astype(LOW), REP).astype(WIDE)
    return (
        latents[None],
        point_sum,
        jnp.concatenate([share[:, cols.source], share[:, cols.target]], axis=1).T[None],
        share[None, :, cols.msg_out],
        share[None, :, cols.gain.start],
        share[None, :, cols.mod],
        share[:, cols.base].T[None],
        share[None, :, cols.q],
        share[None, :, cols.kv],
        share[None, :, cols.o],
        share[None, :, cols.up],
        share[:, cols.down].T[None],
    )


def solution(mesh):
    placed = (
        P((DP, REP), None, None),
        P((DP, REP), None),
        P((DP, REP), None, None),
        P((DP, REP), None, None),
        P(SECTION, None, DP),
        P(SECTION, DP, None),
        P(SECTION, DP),
        P(SECTION, DP, None),
        P(SECTION, None, DP),
        P(SECTION, DP, None),
        P(SECTION, DP, None),
        P(SECTION, DP, None),
        P(SECTION, DP, None),
        P(SECTION, None, DP),
        P(SECTION, (DP, REP), None, None),
    )
    return jax.shard_map(
        on_device,
        mesh=mesh,
        in_specs=placed,
        out_specs=(
            P(SECTION, (DP, REP), None, None),
            P((DP, REP), None, None),
            P(SECTION, None, DP),
            P(SECTION, DP, None),
            P(SECTION, DP),
            P(SECTION, DP, None),
            P(SECTION, None, DP),
            P(SECTION, DP, None),
            P(SECTION, DP, None),
            P(SECTION, DP, None),
            P(SECTION, DP, None),
            P(SECTION, None, DP),
        ),
        check_vma=False,
    )
```

```python
import types

import jax
import jax.numpy as jnp
from jax import lax
from jax.experimental import pallas as pl
from jax.experimental.pallas import tpu as pltpu
from jax.sharding import PartitionSpec as P

HEADS = 6
HEAD_DIM = 64
EPSILON = 1e-05
TANH_ONE = 0.7978845608028654
TANH_THREE = 0.7978845608028654 * 0.044715
CUBE = TANH_THREE ** (1.0 / 3.0)
SECTION, DP, REP = "section", "dp", "rep"
CHUNKS = 3
LOW = jnp.bfloat16
WIDE = jnp.float32
VMEM_BYTES = 63 * 1024 * 1024


def product(left_op, right_op):
    return jnp.dot(left_op, right_op, preferred_element_type=WIDE)


def trans_left(left_op, right_op):
    return lax.dot_general(left_op, right_op, (((0,), (0,)), ((), ())), preferred_element_type=WIDE)


def trans_right(left_op, right_op):
    return lax.dot_general(left_op, right_op, (((1,), (1,)), ((), ())), preferred_element_type=WIDE)


def gelu_pair(inside):
    square = inside * inside
    half = 0.5 + 0.5 * jnp.tanh(inside * (TANH_ONE + TANH_THREE * square))
    value = inside * half
    slope = half + value * (1.0 - half) * (2.0 * TANH_ONE + 6.0 * TANH_THREE * square)
    return value, slope


def gelu_cubed(inside):
    kind = inside.dtype
    square = inside * inside
    bend = jnp.tanh(inside * (square + jnp.asarray(TANH_ONE / CUBE, kind)))
    upper = bend + jnp.asarray(1.0, kind)
    value = inside * upper
    steep = value * (jnp.asarray(1.0, kind) - bend) * (square + jnp.asarray(TANH_ONE / (3.0 * CUBE), kind))
    return value, upper * jnp.asarray(1.0 / 3.0, kind) + steep


def normalised(values):
    centre = values - jnp.mean(values, axis=-1, keepdims=True)
    spread = jnp.mean(centre * centre, axis=-1, keepdims=True)
    scale = lax.rsqrt(spread + EPSILON)
    return centre * scale, scale


def normalised_back(d_out, unit, scale):
    first = jnp.mean(d_out, axis=-1, keepdims=True)
    second = jnp.mean(d_out * unit, axis=-1, keepdims=True)
    return scale * (d_out - first - unit * second)


class Columns:
    def __init__(self, width, hidden, per_sim):
        self.pieces = (
            ("source", width),
            ("gain", 128),
            ("target", width),
            ("msg_out", width),
            ("kv", 2 * width),
            ("q", width),
            ("o", width),
            ("base", per_sim),
        )
        at = 0
        for name, extent in self.pieces:
            setattr(self, name, slice(at, at + extent))
            at += extent
        self.chunk = hidden // CHUNKS
        self.up, self.down = [], []
        for _ in range(CHUNKS):
            self.up.append(slice(at, at + self.chunk))
            self.down.append(slice(at + self.chunk, at + 2 * self.chunk))
            at += 2 * self.chunk
        self.mod = slice(at, at + 4 * width)
        at += 4 * width
        self.total = at


def evolution_masks(b, segments, length):
    second_count = jnp.sum(segments[pl.ds(b, 1), :], axis=1, keepdims=True)
    first_count = length - second_count
    own_col = (lax.broadcasted_iota(jnp.int32, (length, 1), 0) < first_count).astype(WIDE)
    own_row = (lax.broadcasted_iota(jnp.int32, (1, length), 1) < first_count).astype(WIDE)
    return own_col, own_row


def spread_heads(values, own_col):
    lane = lax.broadcasted_iota(jnp.int32, (1, values.shape[1]), 1)
    sims = (own_col.astype(LOW), (1.0 - own_col).astype(LOW))
    halves = ((lane < HEAD_DIM).astype(WIDE).astype(LOW), (lane >= HEAD_DIM).astype(WIDE).astype(LOW))
    return [jnp.concatenate([values * sims[0] * half, values * sims[1] * half], axis=1) for half in halves]


def by_sim(rows_in, pair):
    block = 2 * HEAD_DIM
    per_sim = rows_in.shape[0] // 2
    here = slice(pair * block, (pair + 1) * block)
    return jnp.concatenate([rows_in[:per_sim, here], rows_in[per_sim:, here]], axis=1)


def mod_rows(b, scr, width):
    return (
        [scr.modulation[pl.ds(2 * b + s, 1), width * n : width * (n + 1)] for s in range(2)] for n in range(4)
    )


def first_rows(b, scr, width):
    scale_one, shift_one, _, _ = mod_rows(b, scr, width)
    rows = [(1.0 + scale_one[s]) * scr.base_unit[...] + shift_one[s] for s in range(2)]
    return jnp.concatenate(rows, axis=0).astype(LOW)


def attend(b, cols, packed, segments, scr):
    length, width = scr.node.shape[1:]
    per_sim = scr.base_rows.shape[0]
    block = 2 * HEAD_DIM
    unit, _ = normalised(scr.node[b])
    normed = (unit * scr.gain_row[...]).astype(LOW)
    keyval = product(normed, packed[:, cols.kv]).astype(LOW)
    scr.values[b] = keyval[:, width:]
    scr.keyval_t[b] = keyval.T
    own_col, own_row = evolution_masks(b, segments, length)
    low_row = (own_row.astype(LOW), (1.0 - own_row).astype(LOW))
    query = (product(first_rows(b, scr, width), packed[:, cols.q]).astype(LOW) * 0.125).astype(LOW)
    scr.query[b] = query
    mask = own_col > 0.5
    for pair in range(HEADS // 2):
        keys = spread_heads(keyval[:, pair * block : (pair + 1) * block], own_col)
        query_pair = by_sim(query, pair)
        for h in range(2):
            head = 2 * pair + h
            raw = trans_right(keys[h], query_pair)
            top_first = jnp.max(jnp.where(mask, raw, -3e38), axis=0, keepdims=True)
            top_second = jnp.max(jnp.where(mask, -3e38, raw), axis=0, keepdims=True)
            grown = jnp.exp(raw - jnp.where(mask, top_first, top_second))
            sum_first = jnp.sum(jnp.where(mask, grown, 0.0), axis=0, keepdims=True)
            sum_second = jnp.sum(jnp.where(mask, 0.0, grown), axis=0, keepdims=True)
            share = (grown * jnp.where(mask, 1.0 / sum_first, 1.0 / sum_second)).astype(LOW)
            scr.weights_t[b, head] = share
            here = slice(head * HEAD_DIM, (head + 1) * HEAD_DIM)
            value_t = scr.keyval_t[b, width + here.start : width + here.stop, :]
            value_sims = jnp.concatenate([value_t * low_row[0], value_t * low_row[1]], axis=0)
            out_t = product(value_sims, share).astype(LOW)
            scr.attended_t[b, here, :per_sim] = out_t[:HEAD_DIM]
            scr.attended_t[b, here, per_sim:] = out_t[HEAD_DIM:]


def residual_of(b, cols, packed, scr):
    residual = trans_left(scr.attended_t[b], packed[:, cols.o])
    return residual + jnp.concatenate([scr.base_rows[...]] * 2, axis=0)


def feed_in(b, cols, packed, scr):
    width = scr.node.shape[-1]
    per_sim = scr.base_rows.shape[0]
    _, _, scale_two, shift_two = mod_rows(b, scr, width)
    unit, _ = normalised(residual_of(b, cols, packed, scr))
    second = jnp.concatenate(
        [(1.0 + scale_two[s]) * unit[s * per_sim : (s + 1) * per_sim] + shift_two[s] for s in range(2)], axis=0
    ).astype(LOW)
    scr.second[b] = second
    scr.second_t[:, pl.ds(pl.multiple_of(b * 2 * per_sim, 2 * per_sim), 2 * per_sim)] = second.T


def feed_chunk(b, at, cols, packed, cotangent, scr):
    up, down = cols.up[at], cols.down[at]
    queries = scr.second.shape[1]
    here = pl.ds(pl.multiple_of(b * queries, queries), queries)
    value, steep = gelu_cubed((product(scr.second[b], packed[:, up]) * CUBE).astype(LOW))
    hidden = value * jnp.asarray(0.5 / CUBE, LOW)
    d_up = (product(cotangent[b], packed[:, down]) * 1.5).astype(LOW) * steep
    scr.hidden[here, :] = hidden
    scr.d_up[here, :] = d_up
    if at == 0:
        scr.d_second[b] = trans_right(d_up, packed[:, up])
    else:
        scr.d_second[b] += trans_right(d_up, packed[:, up])
    if at == 0:
        scr.lat_sum[b] = trans_right(hidden, packed[:, down])
    elif at < CHUNKS - 1:
        scr.lat_sum[b] += trans_right(hidden, packed[:, down])


def feed_latents(b, cols, packed, latents, scr):
    queries = scr.second.shape[1]
    here = pl.ds(pl.multiple_of(b * queries, queries), queries)
    last = trans_right(scr.hidden[here, :], packed[:, cols.down[CHUNKS - 1]])
    scr.second[b] = (scr.lat_sum[b] + last).astype(LOW)
    pltpu.make_async_copy(scr.second.at[b], latents.at[b], scr.lat_sems.at[b]).start()


def feed_out(b, cols, packed, cotangent, grads, scr):
    width = scr.node.shape[-1]
    per_sim = scr.base_rows.shape[0]
    _, _, scale_two, _ = mod_rows(b, scr, width)
    attended_t = scr.attended_t[b]
    residual = residual_of(b, cols, packed, scr)
    res_unit, res_scale = normalised(residual)
    scr.lat_sum[b] += residual
    d_second = scr.d_second[b]
    d_res = []
    for s in range(2):
        rows_at = slice(s * per_sim, (s + 1) * per_sim)
        d_sim = d_second[rows_at]
        unit_sim = res_unit[rows_at]
        scr.d_mod[pl.ds(2 * b + s, 1), 2 * width : 3 * width] = jnp.sum(d_sim * unit_sim, axis=0, keepdims=True)
        scr.d_mod[pl.ds(2 * b + s, 1), 3 * width :] = jnp.sum(d_sim, axis=0, keepdims=True)
        d_res.append(
            cotangent[b, rows_at, :].astype(WIDE)
            + normalised_back(d_sim * (1.0 + scale_two[s]), unit_sim, res_scale[rows_at])
        )
    scr.d_base[...] += d_res[0] + d_res[1]
    res_low = jnp.concatenate(d_res, axis=0).astype(LOW)
    grads[:, cols.o] += product(attended_t, res_low)
    d_att = trans_right(packed[:, cols.o], res_low).astype(LOW)
    both = d_att.astype(WIDE) * attended_t.astype(WIDE)
    for head in range(HEADS):
        scr.overlap[b, head : head + 1, :] = jnp.sum(
            both[head * HEAD_DIM : (head + 1) * HEAD_DIM], axis=0, keepdims=True
        )
    scr.attended_t[b] = d_att


def attend_back(b, cols, packed, segments, grads, scr):
    length, width = scr.node.shape[1:]
    per_sim = scr.base_rows.shape[0]
    block = 2 * HEAD_DIM
    own_col, own_row = evolution_masks(b, segments, length)
    low_row = (own_row.astype(LOW), (1.0 - own_row).astype(LOW))
    mask = own_col > 0.5
    left_half = lax.broadcasted_iota(jnp.int32, (1, block), 1) < HEAD_DIM
    values_all = scr.values[b]
    query = scr.query[b]
    d_att = scr.attended_t[b]
    for pair in range(HEADS // 2):
        here = slice(pair * block, (pair + 1) * block)
        values = spread_heads(values_all[:, here], own_col)
        query_pair = by_sim(query, pair)
        d_att_pair = jnp.concatenate([d_att[here, :per_sim], d_att[here, per_sim:]], axis=0)
        d_keys, d_values = [], []
        for h in range(2):
            head = 2 * pair + h
            there = slice(head * HEAD_DIM, (head + 1) * HEAD_DIM)
            both = scr.overlap[b, head : head + 1, :]
            share = scr.weights_t[b, head]
            d_share = product(values[h], d_att_pair)
            d_raw = (
                share.astype(WIDE) * (d_share - jnp.where(mask, both[:, :per_sim], both[:, per_sim:]))
            ).astype(LOW)
            key_t = scr.keyval_t[b, there, :]
            key_sims = jnp.concatenate([key_t * low_row[0], key_t * low_row[1]], axis=0)
            d_q = (product(key_sims, d_raw) * 0.125).astype(LOW)
            scr.query_t[there, :per_sim] = d_q[:HEAD_DIM]
            scr.query_t[there, per_sim:] = d_q[HEAD_DIM:]
            full = trans_right(share, d_att_pair)
            d_values.append(jnp.where(mask, full[:, :block], full[:, block:]))
            full = product(d_raw, query_pair)
            d_keys.append(jnp.where(mask, full[:, :block], full[:, block:]))
        scr.d_keyval[:, here] = jnp.where(left_half, d_keys[0], d_keys[1]).astype(LOW)
        scr.d_keyval[:, width + here.start : width + here.stop] = jnp.where(
            left_half, d_values[0], d_values[1]
        ).astype(LOW)

    scale_one, shift_one, _, _ = mod_rows(b, scr, width)
    d_query = scr.query_t[...].T
    grads[:, cols.q] += trans_left(first_rows(b, scr, width), d_query)
    d_first = trans_right(d_query, packed[:, cols.q])
    for s in range(2):
        d_sim = d_first[s * per_sim : (s + 1) * per_sim]
        scr.d_mod[pl.ds(2 * b + s, 1), :width] = jnp.sum(d_sim * scr.base_unit[...], axis=0, keepdims=True)
        scr.d_mod[pl.ds(2 * b + s, 1), width : 2 * width] = jnp.sum(d_sim, axis=0, keepdims=True)
        scr.d_base_unit[...] += d_sim * (1.0 + scale_one[s])

    unit, node_scale = normalised(scr.node[b])
    gain = scr.gain_row[...]
    d_kv = scr.d_keyval[...]
    grads[:, cols.kv] += trans_left((unit * gain).astype(LOW), d_kv)
    d_normed = trans_right(d_kv, packed[:, cols.kv])
    scr.d_gain[...] += jnp.sum(d_normed * unit, axis=0, keepdims=True)
    scr.node[b] = normalised_back(d_normed * gain, unit, node_scale)


def perceiver_scratch(count, length, width, per_sim, chunk):
    queries = 2 * per_sim
    return dict(
        values=pltpu.VMEM((count, length, width), LOW),
        keyval_t=pltpu.VMEM((count, 2 * width, length), LOW),
        query=pltpu.VMEM((count, queries, width), LOW),
        weights_t=pltpu.VMEM((count, HEADS, length, per_sim), LOW),
        attended_t=pltpu.VMEM((count, width, queries), LOW),
        overlap=pltpu.VMEM((count, 8, queries), WIDE),
        second=pltpu.VMEM((count, queries, width), LOW),
        second_t=pltpu.VMEM((width, count * queries), LOW),
        cot_t=pltpu.VMEM((width, count * queries), LOW),
        hidden=pltpu.VMEM((count * queries, chunk), LOW),
        d_up=pltpu.VMEM((count * queries, chunk), LOW),
        lat_sum=pltpu.VMEM((count, queries, width), WIDE),
        d_second=pltpu.VMEM((count, queries, width), WIDE),
        query_t=pltpu.VMEM((width, queries), LOW),
        d_keyval=pltpu.VMEM((length, 2 * width), LOW),
    )


def one_hot(near_t, edges, columns, length):
    picks = []
    for k in edges:
        row = near_t[k : k + 1, columns].astype(jnp.int16)
        spot = lax.broadcasted_iota(jnp.int16, (length, row.shape[1]), 0)
        picks.append(jnp.where(row == spot, jnp.asarray(1.0, LOW), jnp.asarray(0.0, LOW)))
    return jnp.concatenate(picks, axis=1)


def message_half(b, half, cols, packed, points, tokens, neighbours, scr):
    length, width = points.shape[1:]
    count = neighbours.shape[1]
    part = length // 2
    here = slice(half * part, (half + 1) * part)
    if half == 0:
        scr.source_t[...] = (trans_right(packed[:, cols.source], points[b]) * CUBE).astype(LOW)
    target = (trans_right(packed[:, cols.target], tokens[b, here, :]) * CUBE).astype(LOW)
    target = jnp.concatenate([target, target], axis=1)
    near_t = neighbours[b]
    group = 8
    for at in range(0, count, group):
        value, steep = None, None
        for k in range(at, at + group, 2):
            inside = product(scr.source_t[...], one_hot(near_t, (k, k + 1), here, length)).astype(LOW) + target
            v, t = gelu_cubed(inside)
            scr.slope[b, k, :, here] = t[:, :part]
            scr.slope[b, k + 1, :, here] = t[:, part:]
            v, t = v[:, :part] + v[:, part:], t[:, :part] + t[:, part:]
            value, steep = (v, t) if value is None else (value + v, steep + t)
        if at == 0:
            scr.value_sum[...] = value.astype(WIDE)
            scr.slope_sum[b, :, here] = steep.astype(WIDE)
        else:
            scr.value_sum[...] += value.astype(WIDE)
            scr.slope_sum[b, :, here] += steep.astype(WIDE)
    mixed = (scr.value_sum[...] * (0.5 / (count * CUBE))).astype(LOW)
    scr.mixed_t[b, :, here] = mixed
    scr.node[b, here, :] = tokens[b, here, :].astype(WIDE) + trans_left(mixed, packed[:, cols.msg_out])


def token_back(b, cols, packed, tokens, scr, grads):
    count = scr.slope.shape[1]
    d_out = scr.node[b]
    node_low = d_out.astype(LOW)
    grads[:, cols.msg_out] += product(scr.mixed_t[b], node_low)
    d_mixed = trans_right(packed[:, cols.msg_out], node_low) * (1.5 / count)
    scr.mixed_t[b] = d_mixed.astype(LOW)
    d_target = (d_mixed * scr.slope_sum[b]).astype(LOW)
    grads[:, cols.target] += product(d_target, tokens[b])
    return d_out + trans_left(d_target, packed[:, cols.target])


def source_back(b, cols, packed, points, neighbours, scr, grads):
    length = points.shape[1]
    count = neighbours.shape[1]
    near_t = neighbours[b]
    group = 4
    low = scr.mixed_t[b]
    for at in range(0, count, group):
        edges = range(at, at + group)
        inside = jnp.concatenate([scr.slope[b, k] * low for k in edges], axis=1)
        part = trans_right(inside, one_hot(near_t, edges, slice(0, length), length))
        if at == 0:
            scr.total[...] = part
        else:
            scr.total[...] += part
    d_source = scr.total[...].astype(LOW)
    grads[:, cols.source] += product(d_source, points[b])
    return trans_left(d_source, packed[:, cols.source])


def remote(src, dst, send, recv, to):
    return pltpu.make_async_remote_copy(
        src_ref=src, dst_ref=dst, send_sem=send, recv_sem=recv, device_id=to, device_id_type=pl.DeviceIdType.MESH
    )


class Packed:
    def __init__(self, ref):
        self.ref = ref

    def __getitem__(self, index):
        piece = self.ref[:, :, :, index[1]]
        return piece.reshape(-1, piece.shape[-1])


class Gather:
    def __init__(self, place, ref, groups, sems):
        self.section, self.dp, self.rep, self.chips = place
        self.ref, self.groups = ref, groups
        self.core = lax.rem(self.dp, 2)
        self.chip = self.dp // 2
        self.send, self.recv = sems
        self.line = self.chips == 4

    def half(self, group, which):
        start, stop = self.groups[group]
        size = (stop - start) // 2
        return pl.ds(pl.multiple_of(start + which * size, 128), size)

    def whole(self, group):
        start, stop = self.groups[group]
        return pl.ds(start, stop - start)

    def source(self, k):
        return lax.rem(self.chip - k + self.chips, self.chips)

    def copy(self, spot, send, group, recv, to):
        return remote(spot, spot, self.send.at[send], self.recv.at[group, recv], to)

    def along(self, group, k, chip):
        spot = self.ref.at[chip, self.core, :, self.half(group, self.rep)]
        far = 2 * lax.rem(self.chip + k, self.chips) + self.core
        return self.copy(spot, k - 1, group, k - 1, (self.section, far, self.rep))

    def onward(self, group):
        to, k = 3 * (self.chip - 1), 2 * self.chip - 1
        spot = self.ref.at[self.source(2), self.core, :, self.half(group, self.rep)]
        return self.copy(spot, self.chips - 1, group, k - 1, (self.section, 2 * to + self.core, self.rep))

    def over_rep(self, group, chip):
        spot = self.ref.at[chip, self.core, :, self.half(group, self.rep)]
        return self.copy(spot, self.chips, group, self.chips - 1, (self.section, self.dp, 1 - self.rep))

    def from_rep(self, group):
        spot = self.ref.at[pl.ds(0, self.chips - 1), self.core, :, self.half(group, 1 - self.rep)]
        return self.copy(spot, self.chips, group, self.chips - 1, (self.section, self.dp, 1 - self.rep))

    def over_core(self, group, core):
        spot = self.ref.at[:, core, :, self.whole(group)]
        to = (self.section, 2 * self.chip + 1 - self.core, self.rep)
        return self.copy(spot, self.chips + 1, group, self.chips, to)

    def ends(self, k):
        return jnp.abs(lax.rem(self.chip + k, self.chips) - self.chip) == self.chips - 1

    def inner(self):
        return (self.chip == 1) | (self.chip == 2)

    def direct(self, k, act):
        if self.line:

            @pl.when(jnp.logical_not(self.ends(k)))
            def _():
                act()

        else:
            act()

    def begin(self, group):
        for k in range(1, self.chips):
            self.direct(k, lambda: self.along(group, k, self.chip).start())

    def arrived(self, group, n):
        last = jnp.where(self.chip == 0, 1, 3)
        k = [2, 4 - last, last][n] if self.line else n + 1
        chip = self.source(k)
        self.along(group, k, chip).wait_recv()
        if self.line and n == 0:

            @pl.when(self.inner())
            def _():
                self.onward(group).start()

        self.over_rep(group, chip).start()

    def near(self, group):
        for n in range(self.chips - 2):
            self.arrived(group, n)

    def far(self, group):
        self.arrived(group, self.chips - 2)

    def late(self, group):
        self.from_rep(group).wait_recv()
        self.over_core(group, self.core).start()

    def finish(self, group):
        self.over_core(group, 1 - self.core).wait_recv()

    def drain(self):
        total = self.ref.shape[-1]
        part = pl.ds(0, total // 2)
        home = (self.section, self.dp, 1 - self.rep)
        for k in range(1, self.chips):
            spot = self.ref.at[self.chip, self.core, :, part]
            self.direct(k, lambda: self.copy(spot, k - 1, 0, k - 1, home).wait_send())
        if self.line:

            @pl.when(self.inner())
            def _():
                self.copy(self.ref.at[self.chip, self.core, :, part], self.chips - 1, 0, 0, home).wait_send()

        spot = self.ref.at[pl.ds(0, self.chips - 1), self.core, :, part]
        self.copy(spot, self.chips, 0, 0, home).wait_send()
        self.copy(self.ref.at[:, self.core], self.chips + 1, 0, 0, home).wait_send()


class Scatter:
    def __init__(self, place, grads, share, per, columns, sems, at, bufs):
        self.section, self.dp, self.rep, self.chips = place
        self.grads, self.share, self.per, self.columns = grads, share, per, columns
        self.core = lax.rem(self.dp, 2)
        self.chip = self.dp // 2
        self.sems, self.at = sems, at
        self.core_out, self.core_in, self.rep_in, self.far_in, self.end_out, self.end_in = bufs
        self.size = (columns[1] - columns[0]) // 2
        self.rep_out = self.core_out.at[:, :, : self.size]
        self.far_out = self.core_out.at[:, :, self.size :]

    def rows(self, chip, core):
        return pl.ds(pl.multiple_of((2 * chip + core) * self.per, 16), self.per)

    def half(self, which):
        return pl.ds(pl.multiple_of(self.columns[0] + which * self.size, 128), self.size)

    def local(self, which):
        return pl.ds(pl.multiple_of(which * self.size, 128), self.size)

    def pair(self, kind):
        return self.sems[0].at[self.at, kind], self.sems[1].at[self.at, kind]

    def core_copy(self):
        to = (self.section, 2 * self.chip + 1 - self.core, self.rep)
        return remote(self.core_out, self.core_in, *self.pair(0), to)

    def rep_copy(self):
        return remote(self.rep_out, self.rep_in, *self.pair(1), (self.section, self.dp, 1 - self.rep))

    def far_copy(self, k):
        to = (self.section, 2 * lax.rem(self.chip + k, self.chips) + self.core, self.rep)
        return remote(self.far_out.at[k - 1], self.far_in.at[k - 1], *self.pair(3), to)

    def far_all(self):
        return remote(self.far_out.at[: self.chips - 1], self.far_in, *self.pair(3), (self.section, self.dp, 1 - self.rep))

    def end_copy(self):
        return remote(self.end_out, self.end_in, *self.pair(2), (self.section, self.dp, 1 - self.rep))

    def begin(self):
        start, stop = self.columns
        for chip in range(self.chips):
            self.core_out[chip] = self.grads[self.rows(chip, 1 - self.core), start:stop].astype(LOW)
        self.core_copy().start()

    def middle(self):
        self.core_copy().wait()
        for chip in range(self.chips):
            rows = self.rows(chip, self.core)
            other = self.grads[rows, self.half(1 - self.rep)]
            self.rep_out[chip] = (other + self.core_in[chip, :, self.local(1 - self.rep)].astype(WIDE)).astype(LOW)
        self.rep_copy().start()

    def late(self):
        self.rep_copy().wait_recv()
        for k in range(self.chips):
            chip = lax.rem(self.chip + k, self.chips)
            rows = self.rows(chip, self.core)
            mine = self.grads[rows, self.half(self.rep)]
            mine = mine + self.core_in[chip, :, self.local(self.rep)].astype(WIDE)
            mine = mine + self.rep_in[chip].astype(WIDE)
            if k == 0:
                self.grads[rows, self.half(self.rep)] = mine
            else:
                self.far_out[k - 1] = mine.astype(LOW)
                self.far_copy(k).start()

    def finish(self):
        total = self.grads[self.rows(self.chip, self.core), self.half(self.rep)]
        self.far_all().wait_recv()
        for k in range(1, self.chips):
            total = total + self.far_in[k - 1].astype(WIDE)
        low = total.astype(LOW)
        self.end_out[...] = low
        self.end_copy().start()
        self.share[:, self.half(self.rep)] = low

    def end(self):
        self.end_copy().wait_recv()
        self.share[:, self.half(1 - self.rep)] = self.end_in[...]
        self.rep_copy().wait_send()
        self.end_copy().wait_send()
        self.far_all().wait_send()


class Packets:
    def __init__(self, place, packets, sems, at):
        self.section, self.dp, self.rep, self.chips = place
        self.core, self.chip = lax.rem(self.dp, 2), self.dp // 2
        self.packets, self.sems, self.at = packets, sems, at

    def copy(self, spot, n, to):
        return remote(spot, spot, self.sems.at[0, self.at, n], self.sems.at[1, self.at, n], to)

    def along(self, k, chip):
        spot = self.packets.at[self.core, self.rep, chip]
        far = 2 * lax.rem(self.chip + k, self.chips) + self.core
        return self.copy(spot, k, (self.section, far, self.rep))

    def over_rep(self, rep):
        return self.copy(self.packets.at[self.core, rep], 0, (self.section, self.dp, 1 - self.rep))

    def over_core(self, core):
        to = (self.section, 2 * self.chip + 1 - self.core, self.rep)
        return self.copy(self.packets.at[core], self.chips, to)

    def begin(self, pieces):
        self.packets[self.core, self.rep, self.chip] = jnp.concatenate(pieces, axis=0).astype(LOW)
        for k in range(1, self.chips):
            self.along(k, self.chip).start()

    def middle(self):
        for k in range(1, self.chips):
            self.along(k, lax.rem(self.chip - k + self.chips, self.chips)).wait_recv()
        self.over_rep(self.rep).start()

    def late(self):
        self.over_rep(1 - self.rep).wait_recv()
        self.over_core(self.core).start()

    def finish(self):
        self.over_core(1 - self.core).wait_recv()
        for k in range(1, self.chips):
            self.along(k, self.chip).wait_send()
        self.over_rep(self.rep).wait_send()
        self.over_core(self.core).wait_send()
        width = self.packets.shape[-1]
        result = []
        for at in range(0, self.packets.shape[3], 16):
            part = self.packets[:, :, :, at : at + 16, :].astype(WIDE).reshape(4 * self.chips, 2, 8, width)
            result.append([part[:, m].reshape(32 * self.chips, width).astype(LOW) for m in range(2)])
        return result


def mod_share(scr, late, early, place, out, per):
    width = scr.node.shape[-1]
    second, condition = late.finish()
    (first,) = early.finish()
    scr.turned[...] = condition[0].T
    mine = scr.turned[pl.ds(pl.multiple_of(place[1] * per, 16), per), :]
    for at, part in enumerate(first + second):
        out[:, at * width : (at + 1) * width] = product(mine, part)


def layer_call(cols, linked, sizes, packed_in, raw, points, segments, neighbours, condition, cotangent, per):
    count, length, width = points.shape
    near = neighbours.shape[1]
    per_sim = cols.base.stop - cols.base.start
    chips = sizes[DP] // 2
    part = length // 2
    parts = tuple((cols.up[n].start, cols.down[n].stop) for n in range(CHUNKS))
    groups = (
        (0, cols.msg_out.stop),
        (cols.kv.start, cols.base.stop),
        (cols.mod.start, cols.mod.stop),
    ) + parts
    summed = (
        (0, cols.gain.stop),
        (cols.target.start, cols.msg_out.stop),
        (cols.kv.start, cols.kv.stop),
        (cols.q.start, cols.base.stop),
    ) + parts
    many = cols.mod.start
    rows = 8
    weights_in = list(raw) if linked else [packed_in]
    inputs = weights_in + [points, segments, neighbours, condition, cotangent]
    shape = jax.ShapeDtypeStruct
    outs = [
        shape((count, 2 * per_sim, width), LOW),
        shape((count, length, width), LOW),
        shape((count, length, width), LOW),
    ]
    outs.append(shape((per, many), LOW) if linked else shape((width, many), WIDE))
    outs.append(shape((per if linked else width, 4 * width), WIDE))
    scratch = dict(
        source_t=pltpu.VMEM((width, length), LOW),
        value_sum=pltpu.VMEM((width, part), WIDE),
        tokens=pltpu.VMEM((count, length, width), LOW),
        passed=pltpu.VMEM((count, length, width), LOW),
        mixed_t=pltpu.VMEM((count, width, length), LOW),
        slope=pltpu.VMEM((count, near, width, length), LOW),
        slope_sum=pltpu.VMEM((count, width, length), WIDE),
        node=pltpu.VMEM((count, length, width), WIDE),
        total=pltpu.VMEM((width, length), WIDE),
        point_out=pltpu.VMEM((count, length, width), LOW),
        point_in=pltpu.VMEM((count, length, width), LOW),
        back_in=pltpu.VMEM((count, length, width), LOW),
        modulation=pltpu.VMEM((rows, 4 * width), WIDE),
        condition=pltpu.VMEM((2 * rows, width), WIDE),
        base_unit=pltpu.VMEM((per_sim, width), WIDE),
        base_rows=pltpu.VMEM((per_sim, width), WIDE),
        base_scale=pltpu.VMEM((per_sim, 1), WIDE),
        gain_row=pltpu.VMEM((1, width), WIDE),
        d_gain=pltpu.VMEM((1, width), WIDE),
        d_base_unit=pltpu.VMEM((per_sim, width), WIDE),
        d_base=pltpu.VMEM((per_sim, width), WIDE),
        d_mod=pltpu.VMEM((rows, 4 * width), WIDE),
        lat_sems=pltpu.SemaphoreType.DMA((count,)),
        pass_sems=pltpu.SemaphoreType.DMA((2, 2 * count)),
        back_sems=pltpu.SemaphoreType.DMA((2, count)),
        point_local=pltpu.SemaphoreType.DMA((2,)),
        point_sems=pltpu.SemaphoreType.DMA((2, count)),
    )
    scratch.update(perceiver_scratch(count, length, width, per_sim, cols.chunk))
    bufs = []
    if linked:
        scratch.update(
            packed=pltpu.VMEM((chips, 2, per, cols.total), LOW),
            grads=pltpu.VMEM((width, many), WIDE),
            packets_two=pltpu.VMEM((2, 2, chips, 4 * rows, width), LOW),
            packets_one=pltpu.VMEM((2, 2, chips, 2 * rows, width), LOW),
            turned=pltpu.VMEM((width, 4 * chips * rows), LOW),
            packet_sems=pltpu.SemaphoreType.DMA((2, 2, chips + 1)),
            gather_send=pltpu.SemaphoreType.DMA((chips + 2,)),
            gather_recv=pltpu.SemaphoreType.DMA((len(groups), chips + 1)),
            scatter_send=pltpu.SemaphoreType.DMA((len(summed), 4)),
            scatter_recv=pltpu.SemaphoreType.DMA((len(summed), 4)),
        )
        for start, stop in summed:
            size = stop - start
            bufs += [
                pltpu.VMEM((chips, per, size), LOW),
                pltpu.VMEM((chips, per, size), LOW),
                pltpu.VMEM((chips, per, size // 2), LOW),
                pltpu.VMEM((chips - 1, per, size // 2), LOW),
                pltpu.VMEM((per, size // 2), LOW),
                pltpu.VMEM((per, size // 2), LOW),
            ]
    names = list(scratch)

    def body(*refs):
        ins, refs = refs[: len(inputs)], refs[len(inputs) :]
        results, refs = refs[: len(outs)], refs[len(outs) :]
        scr = types.SimpleNamespace(**dict(zip(names, refs)))
        moved = refs[len(names) :]
        points, segments, neighbours, condition, cotangent = ins[-5:]
        latents, point_mine, point_other = results[:3]
        section, dp, rep = (lax.axis_index(name) for name in (SECTION, DP, REP))
        other = (1 - section, dp, rep)
        if linked:
            packed, grads = Packed(scr.packed), scr.grads
            core, chip = lax.rem(dp, 2), dp // 2
            partners = [other, (section, dp, 1 - rep), (section, 2 * chip + 1 - core, rep)]
            partners += [(section, 2 * lax.rem(chip + k, chips) + core, rep) for k in range(1, chips)]
        else:
            packed, grads = ins[0], results[3]
            partners = [other]
        barrier = pltpu.get_barrier_semaphore()
        for to in partners:
            pl.semaphore_signal(barrier, inc=1, device_id=to, device_id_type=pl.DeviceIdType.MESH)
        if linked:
            place = (section, dp, rep, chips)
            gather = Gather(place, scr.packed, groups, (scr.gather_send, scr.gather_recv))
            msg_in, msg_out, norm_gain, mod_weight, query_base, q_weight, kv_weight, o_weight, up_weight, down_weight = ins[:10]
            mine = scr.packed.at[chip, core]
            mine[:, cols.source] = msg_in[0, :, :width]
            mine[:, cols.target] = msg_in[0, :, width:]
            mine[:, cols.msg_out] = msg_out[0]
            gain = jnp.broadcast_to(norm_gain[...].astype(WIDE), (128, per)).T
            mine[:, cols.gain] = gain.astype(LOW)
            mine[:, cols.kv] = kv_weight[0]
            mine[:, cols.q] = q_weight[0]
            mine[:, cols.o] = o_weight[0]
            mine[:, cols.base] = query_base[0]
            mine[:, cols.mod] = mod_weight[0]
            for n in range(CHUNKS):
                piece = slice(n * cols.chunk, (n + 1) * cols.chunk)
                mine[:, cols.up[n]] = up_weight[0, :, piece]
                mine[:, cols.down[n]] = down_weight[0, :, piece]
        pl.semaphore_wait(barrier, len(partners))
        if linked:
            gather.begin(0)
            gather.begin(1)
        first = grads.at[:, : cols.base.stop]
        first[...] = jnp.zeros_like(first)
        for total in (scr.d_gain, scr.d_base_unit, scr.d_base, scr.d_mod, scr.condition):
            total[...] = jnp.zeros_like(total)
        for b in range(count):
            scr.condition[2 * b : 2 * b + 2, :] = condition[b].astype(WIDE)
            scr.cot_t[:, b * 2 * per_sim : (b + 1) * 2 * per_sim] = cotangent[b].T

        tokens = scr.tokens

        @pl.when(section == 0)
        def _():
            tokens[...] = points[...]

        if linked:
            gather.near(0)
            gather.far(0)
            gather.begin(2)
            gather.late(0)
            gather.finish(0)
            gather.near(1)
            gather.begin(3)

        def pass_copy(n):
            b, half = n // 2, lax.rem(n, 2)
            rows = pl.ds(pl.multiple_of(half * part, part), part)
            return remote(
                scr.passed.at[b, rows, :], tokens.at[b, rows, :], scr.pass_sems.at[0, n], scr.pass_sems.at[1, n], other
            )

        def back_copy(b):
            return remote(scr.passed.at[b], scr.back_in.at[b], scr.back_sems.at[0, b], scr.back_sems.at[1, b], other)

        def point_copy(b):
            return remote(scr.point_out.at[b], scr.point_in.at[b], scr.point_sems.at[0, b], scr.point_sems.at[1, b], other)

        def forward(b):
            for half in range(2):
                n = 2 * b + half

                @pl.when(section == 1)
                def _():
                    pass_copy(n).wait_recv()

                message_half(b, half, cols, packed, points, tokens, neighbours, scr)

                @pl.when(section == 0)
                def _():
                    rows = slice(half * part, (half + 1) * part)
                    scr.passed[b, rows, :] = scr.node[b, rows, :].astype(LOW)
                    pass_copy(n).start()

                ahead = jnp.where(b == 2, 8 * half - 1, n + 2)
                gather_at(jnp.where(section == 0, n, ahead), (1, 3, 5, 7) if half else (0, 2, 4))

        def prepare():
            base = packed[:, cols.base].astype(WIDE).T
            scr.base_rows[...] = base
            unit, scale = normalised(base)
            scr.base_unit[...] = unit
            scr.base_scale[...] = scale
            scr.gain_row[...] = packed[:, cols.gain].astype(WIDE).T[:1]
            scr.modulation[...] = product(scr.condition[...].astype(LOW), packed[:, cols.mod])[:rows]

        def gather_step(n):
            if n == 0:
                gather.far(1)
            elif n == 1:
                gather.near(2)
                gather.begin(4)
            elif n == 2:
                gather.far(2)
            elif n == 3:
                gather.late(1)
                gather.near(3)
                gather.begin(5)
            elif n == 4:
                gather.far(3)
            elif n == 5:
                gather.late(2)
                gather.finish(1)
                gather.near(4)
                gather.finish(2)
                prepare()
            elif n == 6:
                gather.far(4)
                gather.late(3)
                gather.near(5)
            else:
                gather.far(5)
                gather.late(4)
                gather.finish(3)

        def gather_at(at, choices):
            if linked:
                for n in choices:

                    @pl.when(at == n)
                    def _():
                        gather_step(n)

        if linked:

            @pl.when(section == 1)
            def _():
                gather_step(0)
                gather_step(1)

        else:
            prepare()

        def early(step, carry):
            late_one = (step == 3) & (section == 1)
            early_one = (step == 2) & (section == 1)
            message = ((step < count) | late_one) & jnp.logical_not(early_one)
            b = jnp.where(message, jnp.minimum(step, count - 1), jnp.where(early_one, 0, step - count))

            @pl.when(message)
            def _():
                forward(b)

            @pl.when(jnp.logical_not(message))
            def _():
                attend(b, cols, packed, segments, scr)
                gather_at(jnp.where(section == 0, 6 + b, 6 + 2 * b), (6, 7))

            return carry

        lax.fori_loop(0, 2 * count, early, 0)
        if linked:
            scatters = [
                Scatter(
                    place, grads, results[3], per, summed[n], (scr.scatter_send, scr.scatter_recv), n,
                    moved[6 * n : 6 * n + 6],
                )
                for n in range(len(summed))
            ]

        def feed_first(b, carry):
            feed_in(b, cols, packed, scr)
            return carry

        lax.fori_loop(0, count, feed_first, 0)
        for at in range(CHUNKS):
            if linked and at > 0:
                gather.finish(3 + at)

            def feed_step(b, carry):
                feed_chunk(b, at, cols, packed, cotangent, scr)
                if linked and at == 0:

                    @pl.when(b == 0)
                    def _():
                        gather.late(5)

                return carry

            lax.fori_loop(0, count, feed_step, 0)
            grads[:, cols.down[at]] = product(scr.cot_t[...], scr.hidden[...])
            grads[:, cols.up[at]] = product(scr.second_t[...], scr.d_up[...])
            if linked:
                scatters[4 + at].begin()
                if at > 0:
                    scatters[3 + at].middle()
                if at > 1:
                    scatters[2 + at].late()

        if linked:
            halves = [slice(width * n, width * (n + 1)) for n in range(4)]
            packet_two = Packets(place, scr.packets_two, scr.packet_sems, 0)
            packet_one = Packets(place, scr.packets_one, scr.packet_sems, 1)

        def token_step(b):
            return token_back(b, cols, packed, tokens, scr, grads)

        def attention_back(b, carry):
            feed_out(b, cols, packed, cotangent, grads, scr)
            if linked:

                @pl.when(b == 0)
                def _():
                    scatters[6].middle()

                @pl.when(b == count - 1)
                def _():
                    packet_two.begin([scr.d_mod[:, halves[2]], scr.d_mod[:, halves[3]], scr.condition[...]])

            attend_back(b, cols, packed, segments, grads, scr)

            @pl.when(section == 1)
            def _():
                scr.passed[b] = token_step(b).astype(LOW)
                back_copy(b).start()

            if linked:

                @pl.when(b == 0)
                def _():
                    scatters[5].late()
                    scatters[4].finish()

                @pl.when(b == 1)
                def _():
                    scatters[6].late()
                    scatters[5].finish()

            return carry

        lax.fori_loop(0, count, attention_back, 0)
        if linked:
            scatters[2].begin()
        d_rows = normalised_back(scr.d_base_unit[...], scr.base_unit[...], scr.base_scale[...])
        grads[:, cols.base] = (d_rows + scr.d_base[...]).T
        grads[:, cols.gain] = jnp.broadcast_to(scr.d_gain[...], (128, width)).T
        if linked:
            scatters[3].begin()
            packet_one.begin([scr.d_mod[:, halves[0]], scr.d_mod[:, halves[1]]])
            packet_two.middle()

            @pl.when(section == 1)
            def _():
                scatters[1].begin()

            scatters[6].finish()
            scatters[2].middle()
        else:
            results[4][...] = trans_left(scr.condition[:rows].astype(LOW), scr.d_mod[...].astype(LOW))

        def backward(b, carry):
            @pl.when(section == 0)
            def _():
                back_copy(b).wait_recv()
                scr.node[b] = scr.node[b] + scr.back_in[b].astype(WIDE)
                scr.node[b] = token_step(b)

            @pl.when(section == 1)
            def _():
                scr.node[b] = jnp.zeros((length, width), WIDE)

            if linked:

                @pl.when((b == count - 1) & (section == 0))
                def _():
                    scatters[1].begin()

            d_points = source_back(b, cols, packed, points, neighbours, scr, grads)
            scr.point_out[b] = (scr.node[b] + d_points).astype(LOW)
            point_copy(b).start()
            if linked:

                @pl.when(b == 0)
                def _():
                    scatters[3].middle()
                    packet_one.middle()
                    packet_two.late()

                    @pl.when(section == 1)
                    def _():
                        scatters[1].middle()

                @pl.when(b == 1)
                def _():
                    packet_one.late()
                    scatters[2].late()

            return carry

        lax.fori_loop(0, count, backward, 0)
        if linked:
            scatters[0].begin()
            scatters[3].late()

            @pl.when(section == 0)
            def _():
                scatters[1].middle()

        feed_latents(0, cols, packed, latents, scr)
        if linked:
            scatters[0].middle()

            @pl.when(section == 1)
            def _():
                scatters[1].late()

        for b in range(1, count):
            feed_latents(b, cols, packed, latents, scr)
        if linked:
            scatters[2].finish()

            @pl.when(section == 0)
            def _():
                scatters[1].late()

            scatters[0].late()
            scatters[3].finish()
            for n in range(4, 4 + CHUNKS):
                scatters[n].end()
            mod_share(scr, packet_two, packet_one, place, results[4], per)
        for b in range(count):
            point_copy(b).wait_recv()
        point_moves = [
            pltpu.make_async_copy(scr.point_out, point_mine, scr.point_local.at[0]),
            pltpu.make_async_copy(scr.point_in, point_other, scr.point_local.at[1]),
        ]
        for move in point_moves:
            move.start()
        if linked:
            scatters[1].finish()
            scatters[0].finish()
            for n in (3, 2, 1, 0):
                scatters[n].end()
            gather.drain()
        for move in point_moves:
            move.wait()

        for b in range(count):
            pltpu.make_async_copy(scr.second.at[b], latents.at[b], scr.lat_sems.at[b]).wait()

        @pl.when(section == 0)
        def _():
            for n in range(2 * count):
                pass_copy(n).wait_send()

        @pl.when(section == 1)
        def _():
            for b in range(count):
                back_copy(b).wait_send()

        for b in range(count):
            point_copy(b).wait_send()

    spec = pl.BlockSpec(memory_space=pltpu.VMEM)
    return pl.pallas_call(
        body,
        out_shape=outs,
        in_specs=[spec] * len(inputs),
        out_specs=[pl.BlockSpec(memory_space=pl.ANY)] * 3 + [spec] * (len(outs) - 3),
        scratch_shapes=list(scratch.values()) + bufs,
        compiler_params=pltpu.CompilerParams(
            vmem_limit_bytes=VMEM_BYTES, collective_id=0, has_side_effects=True
        ),
        cost_estimate=pl.CostEstimate(flops=10**10, bytes_accessed=1 << 24, transcendentals=0),
        name="layers",
    )(*inputs)


def finish_call(cols, latents, point_mine, point_other, share, mod_share):
    per, width = share.shape[0], point_mine.shape[-1]
    pieces = ([cols.msg_out], [cols.gain], [cols.base], [cols.q], [cols.kv], [cols.o], cols.up, cols.down)
    gain_at = 1

    def body(latents, mod_share, point_mine, point_other, share, latents_out, mod_out, point_out, msg_in_out, *rest):
        outs, (latents_buf, mod_buf, sems) = rest[:-3], rest[-3:]
        arrays = ((latents, latents_buf, latents_out), (mod_share, mod_buf, mod_out))
        arriving = [pltpu.make_async_copy(a, buf, sems.at[0, n]) for n, (a, buf, _) in enumerate(arrays)]
        leaving = [pltpu.make_async_copy(buf, a, sems.at[1, n]) for n, (_, buf, a) in enumerate(arrays)]
        for move in arriving:
            move.start()
        for first, then in zip(arriving, leaving):
            first.wait()
            then.start()
        point_out[...] = point_mine[...].astype(WIDE) + point_other[...].astype(WIDE)
        msg_in_out[0, :, :width] = share[:, cols.source].astype(WIDE)
        msg_in_out[0, :, width:] = share[:, cols.target].astype(WIDE)
        for n, piece in enumerate(pieces):
            at = 0
            for place in piece:
                value = share[:, place].astype(WIDE)
                size = place.stop - place.start
                if n == gain_at:
                    outs[n][...] = value.T[:1]
                else:
                    outs[n][0, :, at : at + size] = value
                at += size
        for move in leaving:
            move.wait()

    shape = jax.ShapeDtypeStruct
    whole, local = pl.BlockSpec(memory_space=pl.ANY), pl.BlockSpec(memory_space=pltpu.VMEM)
    outs = [shape(latents.shape, LOW), shape(mod_share.shape, WIDE), shape(point_mine.shape, WIDE)]
    outs.append(shape((1, per, 2 * width), WIDE))
    for n, piece in enumerate(pieces):
        outs.append(shape((1, per) if n == gain_at else (1, per, sum(place.stop - place.start for place in piece)), WIDE))
    latents, mod, point_sum, msg_in, msg_out, gain, base, q, kv, o, up, down = pl.pallas_call(
        body,
        out_shape=outs,
        in_specs=[whole, whole, local, local, local],
        out_specs=[whole, whole] + [local] * (2 + len(pieces)),
        scratch_shapes=[pltpu.VMEM(a.shape, a.dtype) for a in (latents, mod_share)]
        + [pltpu.SemaphoreType.DMA((2, 2))],
        compiler_params=pltpu.CompilerParams(vmem_limit_bytes=VMEM_BYTES),
        cost_estimate=pl.CostEstimate(flops=10**6, bytes_accessed=1 << 23, transcendentals=0),
        name="finish",
    )(latents, mod_share, point_mine, point_other, share)
    turn = lambda array: jnp.swapaxes(array, 1, 2)
    return (latents[None], point_sum, turn(msg_in), msg_out, gain, mod[None], turn(base), q, kv, o, up, turn(down))


def on_device(
    points,
    segments,
    neighbours,
    condition,
    msg_in,
    msg_out,
    norm_gain,
    mod_weight,
    query_base,
    q_weight,
    kv_weight,
    o_weight,
    up_weight,
    down_weight,
    cotangent,
):
    count, length, width = points.shape
    per = q_weight.shape[1]
    hidden = up_weight.shape[2]
    per_sim = query_base.shape[1]
    cols = Columns(width, hidden, per_sim)
    sizes = {name: lax.axis_size(name) for name in (SECTION, DP, REP)}
    linked = per % 16 == 0 and sizes[DP] % 2 == 0 and sizes[REP] == 2
    raw = (
        jnp.swapaxes(msg_in, 1, 2),
        msg_out,
        norm_gain,
        mod_weight,
        jnp.swapaxes(query_base, 1, 2),
        q_weight,
        kv_weight,
        o_weight,
        up_weight,
        jnp.swapaxes(down_weight, 1, 2),
    )
    near_t = jnp.swapaxes(neighbours, 1, 2)
    if linked:
        outs = layer_call(cols, True, sizes, None, raw, points, segments, near_t, condition, cotangent[0], per)
        return finish_call(cols, *outs)
    turned = msg_in[0].T
    own = jnp.concatenate(
        [
            turned[:, :width],
            jnp.broadcast_to(norm_gain[0][:, None], (per, 128)),
            turned[:, width:],
            msg_out[0],
            kv_weight[0],
            q_weight[0],
            o_weight[0],
            query_base[0].T,
            *sum(
                (
                    [up_weight[0, :, n : n + cols.chunk], down_weight[0, n : n + cols.chunk].T]
                    for n in range(0, hidden, cols.chunk)
                ),
                [],
            ),
            mod_weight[0],
        ],
        axis=1,
    )
    packed = lax.all_gather(own, DP, axis=0, tiled=True)
    latents, point_mine, point_other, grads, mod_grads = layer_call(
        cols, False, sizes, packed, None, points, segments, near_t, condition, cotangent[0], per
    )
    grads = jnp.concatenate([grads, mod_grads], axis=1)
    share = lax.psum_scatter(grads, DP, scatter_dimension=0, tiled=True)
    share = lax.psum(share.astype(LOW), REP).astype(WIDE)
    return (
        latents[None],
        point_mine.astype(WIDE) + point_other.astype(WIDE),
        jnp.concatenate([share[:, cols.source], share[:, cols.target]], axis=1).T[None],
        share[None, :, cols.msg_out],
        share[None, :, cols.gain.start],
        share[None, :, cols.mod],
        share[:, cols.base].T[None],
        share[None, :, cols.q],
        share[None, :, cols.kv],
        share[None, :, cols.o],
        jnp.concatenate([share[None, :, piece] for piece in cols.up], axis=2),
        jnp.concatenate([share[:, piece] for piece in cols.down], axis=1).T[None],
    )


def solution(mesh):
    placed = (
        P((DP, REP), None, None),
        P((DP, REP), None),
        P((DP, REP), None, None),
        P((DP, REP), None, None),
        P(SECTION, None, DP),
        P(SECTION, DP, None),
        P(SECTION, DP),
        P(SECTION, DP, None),
        P(SECTION, None, DP),
        P(SECTION, DP, None),
        P(SECTION, DP, None),
        P(SECTION, DP, None),
        P(SECTION, DP, None),
        P(SECTION, None, DP),
        P(SECTION, (DP, REP), None, None),
    )
    return jax.shard_map(
        on_device,
        mesh=mesh,
        in_specs=placed,
        out_specs=(
            P(SECTION, (DP, REP), None, None),
            P((DP, REP), None, None),
            P(SECTION, None, DP),
            P(SECTION, DP, None),
            P(SECTION, DP),
            P(SECTION, DP, None),
            P(SECTION, None, DP),
            P(SECTION, DP, None),
            P(SECTION, DP, None),
            P(SECTION, DP, None),
            P(SECTION, DP, None),
            P(SECTION, None, DP),
        ),
        check_vma=False,
    )
```

```python
import types

import jax
import jax.numpy as jnp
from jax import lax
from jax.experimental import pallas as pl
from jax.experimental.pallas import tpu as pltpu
from jax.sharding import PartitionSpec as P

HEADS = 6
HEAD_DIM = 64
EPSILON = 1e-05
TANH_ONE = 0.7978845608028654
TANH_THREE = 0.7978845608028654 * 0.044715
CUBE = TANH_THREE ** (1.0 / 3.0)
SECTION, DP, REP = "section", "dp", "rep"
CHUNKS = 3
LOW = jnp.bfloat16
WIDE = jnp.float32
VMEM_BYTES = 63 * 1024 * 1024


def product(left_op, right_op):
    return jnp.dot(left_op, right_op, preferred_element_type=WIDE)


def trans_left(left_op, right_op):
    return lax.dot_general(left_op, right_op, (((0,), (0,)), ((), ())), preferred_element_type=WIDE)


def trans_right(left_op, right_op):
    return lax.dot_general(left_op, right_op, (((1,), (1,)), ((), ())), preferred_element_type=WIDE)


def gelu_pair(inside):
    square = inside * inside
    half = 0.5 + 0.5 * jnp.tanh(inside * (TANH_ONE + TANH_THREE * square))
    value = inside * half
    slope = half + value * (1.0 - half) * (2.0 * TANH_ONE + 6.0 * TANH_THREE * square)
    return value, slope


def gelu_cubed(inside):
    kind = inside.dtype
    square = inside * inside
    bend = jnp.tanh(inside * (square + jnp.asarray(TANH_ONE / CUBE, kind)))
    upper = bend + jnp.asarray(1.0, kind)
    value = inside * upper
    steep = value * (jnp.asarray(1.0, kind) - bend) * (square + jnp.asarray(TANH_ONE / (3.0 * CUBE), kind))
    return value, upper * jnp.asarray(1.0 / 3.0, kind) + steep


def normalised(values):
    centre = values - jnp.mean(values, axis=-1, keepdims=True)
    spread = jnp.mean(centre * centre, axis=-1, keepdims=True)
    scale = lax.rsqrt(spread + EPSILON)
    return centre * scale, scale


def normalised_back(d_out, unit, scale):
    first = jnp.mean(d_out, axis=-1, keepdims=True)
    second = jnp.mean(d_out * unit, axis=-1, keepdims=True)
    return scale * (d_out - first - unit * second)


class Columns:
    def __init__(self, width, hidden, per_sim):
        self.pieces = (
            ("source", width),
            ("gain", 128),
            ("target", width),
            ("msg_out", width),
            ("kv", 2 * width),
            ("q", width),
            ("o", width),
            ("base", per_sim),
        )
        at = 0
        for name, extent in self.pieces:
            setattr(self, name, slice(at, at + extent))
            at += extent
        self.chunk = hidden // CHUNKS
        self.up, self.down = [], []
        for _ in range(CHUNKS):
            self.up.append(slice(at, at + self.chunk))
            self.down.append(slice(at + self.chunk, at + 2 * self.chunk))
            at += 2 * self.chunk
        self.mod = slice(at, at + 4 * width)
        at += 4 * width
        self.total = at


def evolution_masks(b, segments, length):
    second_count = jnp.sum(segments[pl.ds(b, 1), :], axis=1, keepdims=True)
    first_count = length - second_count
    own_col = (lax.broadcasted_iota(jnp.int32, (length, 1), 0) < first_count).astype(WIDE)
    own_row = (lax.broadcasted_iota(jnp.int32, (1, length), 1) < first_count).astype(WIDE)
    return own_col, own_row


def spread_heads(values, own_col):
    lane = lax.broadcasted_iota(jnp.int32, (1, values.shape[1]), 1)
    sims = (own_col.astype(LOW), (1.0 - own_col).astype(LOW))
    halves = ((lane < HEAD_DIM).astype(WIDE).astype(LOW), (lane >= HEAD_DIM).astype(WIDE).astype(LOW))
    return [jnp.concatenate([values * sims[0] * half, values * sims[1] * half], axis=1) for half in halves]


def by_sim(rows_in, pair):
    block = 2 * HEAD_DIM
    per_sim = rows_in.shape[0] // 2
    here = slice(pair * block, (pair + 1) * block)
    return jnp.concatenate([rows_in[:per_sim, here], rows_in[per_sim:, here]], axis=1)


def mod_rows(b, scr, width):
    return (
        [scr.modulation[pl.ds(2 * b + s, 1), width * n : width * (n + 1)] for s in range(2)] for n in range(4)
    )


def first_rows(b, scr, width):
    scale_one, shift_one, _, _ = mod_rows(b, scr, width)
    rows = [(1.0 + scale_one[s]) * scr.base_unit[...] + shift_one[s] for s in range(2)]
    return jnp.concatenate(rows, axis=0).astype(LOW)


def attend(b, cols, packed, segments, scr):
    length, width = scr.node.shape[1:]
    per_sim = scr.base_rows.shape[0]
    block = 2 * HEAD_DIM
    unit, _ = normalised(scr.node[b])
    normed = (unit * scr.gain_row[...]).astype(LOW)
    keyval = product(normed, packed[:, cols.kv]).astype(LOW)
    scr.values[b] = keyval[:, width:]
    scr.keyval_t[b] = keyval.T
    own_col, own_row = evolution_masks(b, segments, length)
    low_row = (own_row.astype(LOW), (1.0 - own_row).astype(LOW))
    query = (product(first_rows(b, scr, width), packed[:, cols.q]).astype(LOW) * 0.125).astype(LOW)
    scr.query[b] = query
    mask = own_col > 0.5
    ones = jnp.concatenate([jnp.broadcast_to(own_row, (8, length)), jnp.broadcast_to(1.0 - own_row, (8, length))], axis=0)
    ones = ones.astype(LOW)
    for pair in range(HEADS // 2):
        keys = spread_heads(keyval[:, pair * block : (pair + 1) * block], own_col)
        raw_pair = trans_right(jnp.concatenate(keys, axis=0), by_sim(query, pair))
        for h in range(2):
            head = 2 * pair + h
            raw = raw_pair[h * length : (h + 1) * length]
            top_first = jnp.max(jnp.where(mask, raw, -3e38), axis=0, keepdims=True)
            top_second = jnp.max(jnp.where(mask, -3e38, raw), axis=0, keepdims=True)
            grown = jnp.exp(raw - jnp.where(mask, top_first, top_second)).astype(LOW)
            scr.weights_t[b, head] = grown
            here = slice(head * HEAD_DIM, (head + 1) * HEAD_DIM)
            value_t = scr.keyval_t[b, width + here.start : width + here.stop, :]
            value_sims = jnp.concatenate([value_t * low_row[0], value_t * low_row[1], ones], axis=0)
            out_t = product(value_sims, grown)
            inverse = 1.0 / out_t[2 * HEAD_DIM :]
            scr.inverse[b, head : head + 1, :per_sim] = inverse[:1]
            scr.inverse[b, head : head + 1, per_sim:] = inverse[8:9]
            scr.attended_t[b, here, :per_sim] = (out_t[:HEAD_DIM] * inverse[:1]).astype(LOW)
            scr.attended_t[b, here, per_sim:] = (out_t[HEAD_DIM : 2 * HEAD_DIM] * inverse[8:9]).astype(LOW)


def residual_of(b, cols, packed, scr):
    residual = trans_left(scr.attended_t[b], packed[:, cols.o])
    return residual + jnp.concatenate([scr.base_rows[...]] * 2, axis=0)


def feed_in(b, cols, packed, scr):
    width = scr.node.shape[-1]
    per_sim = scr.base_rows.shape[0]
    _, _, scale_two, shift_two = mod_rows(b, scr, width)
    unit, _ = normalised(residual_of(b, cols, packed, scr))
    second = jnp.concatenate(
        [(1.0 + scale_two[s]) * unit[s * per_sim : (s + 1) * per_sim] + shift_two[s] for s in range(2)], axis=0
    ).astype(LOW)
    scr.second[b] = second
    scr.second_t[:, pl.ds(pl.multiple_of(b * 2 * per_sim, 2 * per_sim), 2 * per_sim)] = second.T


def feed_chunk(b, at, cols, packed, cotangent, scr):
    up, down = cols.up[at], cols.down[at]
    queries = scr.second.shape[1]
    here = pl.ds(pl.multiple_of(b * queries, queries), queries)
    value, steep = gelu_cubed((product(scr.second[b], packed[:, up]) * CUBE).astype(LOW))
    hidden = value * jnp.asarray(0.5 / CUBE, LOW)
    d_up = (product(cotangent[b], packed[:, down]) * 1.5).astype(LOW) * steep
    scr.hidden[here, :] = hidden
    scr.d_up[here, :] = d_up
    if at == 0:
        scr.d_second[b] = trans_right(d_up, packed[:, up])
    else:
        scr.d_second[b] += trans_right(d_up, packed[:, up])
    if at == 0:
        scr.lat_sum[b] = trans_right(hidden, packed[:, down])
    elif at < CHUNKS - 1:
        scr.lat_sum[b] += trans_right(hidden, packed[:, down])


def feed_latents(b, cols, packed, latents, scr):
    queries = scr.second.shape[1]
    here = pl.ds(pl.multiple_of(b * queries, queries), queries)
    last = trans_right(scr.hidden[here, :], packed[:, cols.down[CHUNKS - 1]])
    scr.second[b] = (scr.lat_sum[b] + last).astype(LOW)
    pltpu.make_async_copy(scr.second.at[b], latents.at[b], scr.lat_sems.at[b]).start()


def feed_out(b, cols, packed, cotangent, grads, scr):
    width = scr.node.shape[-1]
    per_sim = scr.base_rows.shape[0]
    _, _, scale_two, _ = mod_rows(b, scr, width)
    attended_t = scr.attended_t[b]
    residual = residual_of(b, cols, packed, scr)
    res_unit, res_scale = normalised(residual)
    scr.lat_sum[b] += residual
    d_second = scr.d_second[b]
    d_res = []
    for s in range(2):
        rows_at = slice(s * per_sim, (s + 1) * per_sim)
        d_sim = d_second[rows_at]
        unit_sim = res_unit[rows_at]
        scr.d_mod[pl.ds(2 * b + s, 1), 2 * width : 3 * width] = jnp.sum(d_sim * unit_sim, axis=0, keepdims=True)
        scr.d_mod[pl.ds(2 * b + s, 1), 3 * width :] = jnp.sum(d_sim, axis=0, keepdims=True)
        d_res.append(
            cotangent[b, rows_at, :].astype(WIDE)
            + normalised_back(d_sim * (1.0 + scale_two[s]), unit_sim, res_scale[rows_at])
        )
    scr.d_base[...] += d_res[0] + d_res[1]
    res_low = jnp.concatenate(d_res, axis=0).astype(LOW)
    grads[:, cols.o] += product(attended_t, res_low)
    d_att = trans_right(packed[:, cols.o], res_low)
    for head in range(HEADS):
        there = slice(head * HEAD_DIM, (head + 1) * HEAD_DIM)
        scaled = d_att[there] * scr.inverse[b, head : head + 1, :]
        both = scaled * attended_t[there].astype(WIDE)
        scr.overlap[b, head : head + 1, :] = jnp.sum(both, axis=0, keepdims=True)
        scr.attended_t[b, there, :] = scaled.astype(LOW)


def attend_back(b, cols, packed, segments, grads, scr):
    length, width = scr.node.shape[1:]
    per_sim = scr.base_rows.shape[0]
    block = 2 * HEAD_DIM
    own_col, own_row = evolution_masks(b, segments, length)
    low_row = (own_row.astype(LOW), (1.0 - own_row).astype(LOW))
    mask = own_col > 0.5
    left_half = lax.broadcasted_iota(jnp.int32, (1, block), 1) < HEAD_DIM
    values_all = scr.values[b]
    query = scr.query[b]
    d_att = scr.attended_t[b]
    for pair in range(HEADS // 2):
        here = slice(pair * block, (pair + 1) * block)
        values = spread_heads(values_all[:, here], own_col)
        query_pair = by_sim(query, pair)
        d_att_pair = jnp.concatenate([d_att[here, :per_sim], d_att[here, per_sim:]], axis=0)
        d_share_pair = product(jnp.concatenate(values, axis=0), d_att_pair)
        d_raws = []
        for h in range(2):
            head = 2 * pair + h
            there = slice(head * HEAD_DIM, (head + 1) * HEAD_DIM)
            both = scr.overlap[b, head : head + 1, :]
            d_share = d_share_pair[h * length : (h + 1) * length]
            d_raw = (
                scr.weights_t[b, head].astype(WIDE)
                * (d_share - jnp.where(mask, both[:, :per_sim], both[:, per_sim:]))
            ).astype(LOW)
            d_raws.append(d_raw)
            key_t = scr.keyval_t[b, there, :]
            key_sims = jnp.concatenate([key_t * low_row[0], key_t * low_row[1]], axis=0)
            d_q = (product(key_sims, d_raw) * 0.125).astype(LOW)
            scr.query_t[there, :per_sim] = d_q[:HEAD_DIM]
            scr.query_t[there, per_sim:] = d_q[HEAD_DIM:]
        shares = scr.weights_t[b, 2 * pair : 2 * pair + 2].reshape(2 * length, per_sim)
        d_keys, d_values = [], []
        for full, parts in (
            (product(jnp.concatenate(d_raws, axis=0), query_pair), d_keys),
            (trans_right(shares, d_att_pair), d_values),
        ):
            for h in range(2):
                own = full[h * length : (h + 1) * length]
                parts.append(jnp.where(mask, own[:, :block], own[:, block:]))
        scr.d_keyval[:, here] = jnp.where(left_half, d_keys[0], d_keys[1]).astype(LOW)
        scr.d_keyval[:, width + here.start : width + here.stop] = jnp.where(
            left_half, d_values[0], d_values[1]
        ).astype(LOW)

    scale_one, shift_one, _, _ = mod_rows(b, scr, width)
    d_query = scr.query_t[...].T
    grads[:, cols.q] += trans_left(first_rows(b, scr, width), d_query)
    d_first = trans_right(d_query, packed[:, cols.q])
    for s in range(2):
        d_sim = d_first[s * per_sim : (s + 1) * per_sim]
        scr.d_mod[pl.ds(2 * b + s, 1), :width] = jnp.sum(d_sim * scr.base_unit[...], axis=0, keepdims=True)
        scr.d_mod[pl.ds(2 * b + s, 1), width : 2 * width] = jnp.sum(d_sim, axis=0, keepdims=True)
        scr.d_base_unit[...] += d_sim * (1.0 + scale_one[s])

    unit, node_scale = normalised(scr.node[b])
    gain = scr.gain_row[...]
    d_kv = scr.d_keyval[...]
    grads[:, cols.kv] += trans_left((unit * gain).astype(LOW), d_kv)
    d_normed = trans_right(d_kv, packed[:, cols.kv])
    scr.d_gain[...] += jnp.sum(d_normed * unit, axis=0, keepdims=True)
    scr.node[b] = normalised_back(d_normed * gain, unit, node_scale)


def perceiver_scratch(count, length, width, per_sim, chunk):
    queries = 2 * per_sim
    return dict(
        values=pltpu.VMEM((count, length, width), LOW),
        keyval_t=pltpu.VMEM((count, 2 * width, length), LOW),
        query=pltpu.VMEM((count, queries, width), LOW),
        weights_t=pltpu.VMEM((count, HEADS, length, per_sim), LOW),
        attended_t=pltpu.VMEM((count, width, queries), LOW),
        overlap=pltpu.VMEM((count, 8, queries), WIDE),
        inverse=pltpu.VMEM((count, 8, queries), WIDE),
        second=pltpu.VMEM((count, queries, width), LOW),
        second_t=pltpu.VMEM((width, count * queries), LOW),
        cot_t=pltpu.VMEM((width, count * queries), LOW),
        hidden=pltpu.VMEM((count * queries, chunk), LOW),
        d_up=pltpu.VMEM((count * queries, chunk), LOW),
        lat_sum=pltpu.VMEM((count, queries, width), WIDE),
        d_second=pltpu.VMEM((count, queries, width), WIDE),
        query_t=pltpu.VMEM((width, queries), LOW),
        d_keyval=pltpu.VMEM((length, 2 * width), LOW),
    )


def one_hot(near_t, edges, columns, length):
    picks = []
    for k in edges:
        row = near_t[k : k + 1, columns].astype(jnp.int16)
        spot = lax.broadcasted_iota(jnp.int16, (length, row.shape[1]), 0)
        picks.append(jnp.where(row == spot, jnp.asarray(1.0, LOW), jnp.asarray(0.0, LOW)))
    return jnp.concatenate(picks, axis=1)


def message_half(b, half, cols, packed, points, tokens, neighbours, scr):
    length, width = points.shape[1:]
    count = neighbours.shape[1]
    part = length // 2
    here = slice(half * part, (half + 1) * part)
    if half == 0:
        scr.source_t[...] = (trans_right(packed[:, cols.source], points[b]) * CUBE).astype(LOW)
    target = (trans_right(packed[:, cols.target], tokens[b, here, :]) * CUBE).astype(LOW)
    target = jnp.concatenate([target, target], axis=1)
    near_t = neighbours[b]
    group = 8
    for at in range(0, count, group):
        value, steep = None, None
        for k in range(at, at + group, 2):
            inside = product(scr.source_t[...], one_hot(near_t, (k, k + 1), here, length)).astype(LOW) + target
            v, t = gelu_cubed(inside)
            scr.slope[b, k, :, here] = t[:, :part]
            scr.slope[b, k + 1, :, here] = t[:, part:]
            v, t = v[:, :part] + v[:, part:], t[:, :part] + t[:, part:]
            value, steep = (v, t) if value is None else (value + v, steep + t)
        if at == 0:
            scr.value_sum[...] = value.astype(WIDE)
            scr.slope_sum[b, :, here] = steep.astype(WIDE)
        else:
            scr.value_sum[...] += value.astype(WIDE)
            scr.slope_sum[b, :, here] += steep.astype(WIDE)
    mixed = (scr.value_sum[...] * (0.5 / (count * CUBE))).astype(LOW)
    scr.mixed_t[b, :, here] = mixed
    scr.node[b, here, :] = tokens[b, here, :].astype(WIDE) + trans_left(mixed, packed[:, cols.msg_out])


def token_back(b, cols, packed, tokens, scr, grads):
    count = scr.slope.shape[1]
    d_out = scr.node[b]
    node_low = d_out.astype(LOW)
    grads[:, cols.msg_out] += product(scr.mixed_t[b], node_low)
    d_mixed = trans_right(packed[:, cols.msg_out], node_low) * (1.5 / count)
    scr.mixed_t[b] = d_mixed.astype(LOW)
    d_target = (d_mixed * scr.slope_sum[b]).astype(LOW)
    grads[:, cols.target] += product(d_target, tokens[b])
    return d_out + trans_left(d_target, packed[:, cols.target])


def source_back(b, cols, packed, points, neighbours, scr, grads):
    length = points.shape[1]
    count = neighbours.shape[1]
    near_t = neighbours[b]
    group = 4
    low = scr.mixed_t[b]
    for at in range(0, count, group):
        edges = range(at, at + group)
        inside = jnp.concatenate([scr.slope[b, k] * low for k in edges], axis=1)
        part = trans_right(inside, one_hot(near_t, edges, slice(0, length), length))
        if at == 0:
            scr.total[...] = part
        else:
            scr.total[...] += part
    d_source = scr.total[...].astype(LOW)
    grads[:, cols.source] += product(d_source, points[b])
    return trans_left(d_source, packed[:, cols.source])


def remote(src, dst, send, recv, to):
    return pltpu.make_async_remote_copy(
        src_ref=src, dst_ref=dst, send_sem=send, recv_sem=recv, device_id=to, device_id_type=pl.DeviceIdType.MESH
    )


class Packed:
    def __init__(self, ref):
        self.ref = ref

    def __getitem__(self, index):
        piece = self.ref[:, :, :, index[1]]
        return piece.reshape(-1, piece.shape[-1])


class Gather:
    def __init__(self, place, ref, groups, sems):
        self.section, self.dp, self.rep, self.chips = place
        self.ref, self.groups = ref, groups
        self.core = lax.rem(self.dp, 2)
        self.chip = self.dp // 2
        self.send, self.recv = sems
        self.line = self.chips == 4

    def half(self, group, which):
        start, stop = self.groups[group]
        size = (stop - start) // 2
        return pl.ds(pl.multiple_of(start + which * size, 128), size)

    def whole(self, group):
        start, stop = self.groups[group]
        return pl.ds(start, stop - start)

    def source(self, k):
        return lax.rem(self.chip - k + self.chips, self.chips)

    def copy(self, spot, send, group, recv, to):
        return remote(spot, spot, self.send.at[send], self.recv.at[group, recv], to)

    def along(self, group, k, chip):
        spot = self.ref.at[chip, self.core, :, self.half(group, self.rep)]
        far = 2 * lax.rem(self.chip + k, self.chips) + self.core
        return self.copy(spot, k - 1, group, k - 1, (self.section, far, self.rep))

    def onward(self, group):
        to, k = 3 * (self.chip - 1), 2 * self.chip - 1
        spot = self.ref.at[self.source(2), self.core, :, self.half(group, self.rep)]
        return self.copy(spot, self.chips - 1, group, k - 1, (self.section, 2 * to + self.core, self.rep))

    def over_rep(self, group, chip):
        spot = self.ref.at[chip, self.core, :, self.half(group, self.rep)]
        return self.copy(spot, self.chips, group, self.chips - 1, (self.section, self.dp, 1 - self.rep))

    def from_rep(self, group):
        spot = self.ref.at[pl.ds(0, self.chips - 1), self.core, :, self.half(group, 1 - self.rep)]
        return self.copy(spot, self.chips, group, self.chips - 1, (self.section, self.dp, 1 - self.rep))

    def over_core(self, group, core):
        spot = self.ref.at[:, core, :, self.whole(group)]
        to = (self.section, 2 * self.chip + 1 - self.core, self.rep)
        return self.copy(spot, self.chips + 1, group, self.chips, to)

    def ends(self, k):
        return jnp.abs(lax.rem(self.chip + k, self.chips) - self.chip) == self.chips - 1

    def inner(self):
        return (self.chip == 1) | (self.chip == 2)

    def direct(self, k, act):
        if self.line:

            @pl.when(jnp.logical_not(self.ends(k)))
            def _():
                act()

        else:
            act()

    def begin(self, group):
        for k in range(1, self.chips):
            self.direct(k, lambda: self.along(group, k, self.chip).start())

    def arrived(self, group, n):
        last = jnp.where(self.chip == 0, 1, 3)
        k = [2, 4 - last, last][n] if self.line else n + 1
        chip = self.source(k)
        self.along(group, k, chip).wait_recv()
        if self.line and n == 0:

            @pl.when(self.inner())
            def _():
                self.onward(group).start()

        self.over_rep(group, chip).start()

    def near(self, group):
        for n in range(self.chips - 2):
            self.arrived(group, n)

    def far(self, group):
        self.arrived(group, self.chips - 2)

    def late(self, group):
        self.from_rep(group).wait_recv()
        self.over_core(group, self.core).start()

    def finish(self, group):
        self.over_core(group, 1 - self.core).wait_recv()

    def drain(self):
        total = self.ref.shape[-1]
        part = pl.ds(0, total // 2)
        home = (self.section, self.dp, 1 - self.rep)
        for k in range(1, self.chips):
            spot = self.ref.at[self.chip, self.core, :, part]
            self.direct(k, lambda: self.copy(spot, k - 1, 0, k - 1, home).wait_send())
        if self.line:

            @pl.when(self.inner())
            def _():
                self.copy(self.ref.at[self.chip, self.core, :, part], self.chips - 1, 0, 0, home).wait_send()

        spot = self.ref.at[pl.ds(0, self.chips - 1), self.core, :, part]
        self.copy(spot, self.chips, 0, 0, home).wait_send()
        self.copy(self.ref.at[:, self.core], self.chips + 1, 0, 0, home).wait_send()


class Scatter:
    def __init__(self, place, grads, share, per, columns, sems, at, bufs):
        self.section, self.dp, self.rep, self.chips = place
        self.grads, self.share, self.per, self.columns = grads, share, per, columns
        self.core = lax.rem(self.dp, 2)
        self.chip = self.dp // 2
        self.sems, self.at = sems, at
        self.core_out, self.core_in, self.rep_in, self.far_in, self.end_out, self.end_in = bufs
        self.size = (columns[1] - columns[0]) // 2
        self.rep_out = self.core_out.at[:, :, : self.size]
        self.far_out = self.core_out.at[:, :, self.size :]

    def rows(self, chip, core):
        return pl.ds(pl.multiple_of((2 * chip + core) * self.per, 16), self.per)

    def half(self, which):
        return pl.ds(pl.multiple_of(self.columns[0] + which * self.size, 128), self.size)

    def local(self, which):
        return pl.ds(pl.multiple_of(which * self.size, 128), self.size)

    def pair(self, kind):
        return self.sems[0].at[self.at, kind], self.sems[1].at[self.at, kind]

    def core_copy(self):
        to = (self.section, 2 * self.chip + 1 - self.core, self.rep)
        return remote(self.core_out, self.core_in, *self.pair(0), to)

    def rep_copy(self):
        return remote(self.rep_out, self.rep_in, *self.pair(1), (self.section, self.dp, 1 - self.rep))

    def far_copy(self, k):
        to = (self.section, 2 * lax.rem(self.chip + k, self.chips) + self.core, self.rep)
        return remote(self.far_out.at[k - 1], self.far_in.at[k - 1], *self.pair(3), to)

    def far_all(self):
        return remote(self.far_out.at[: self.chips - 1], self.far_in, *self.pair(3), (self.section, self.dp, 1 - self.rep))

    def end_copy(self):
        return remote(self.end_out, self.end_in, *self.pair(2), (self.section, self.dp, 1 - self.rep))

    def begin(self):
        start, stop = self.columns
        for chip in range(self.chips):
            self.core_out[chip] = self.grads[self.rows(chip, 1 - self.core), start:stop].astype(LOW)
        self.core_copy().start()

    def middle(self):
        self.core_copy().wait()
        for chip in range(self.chips):
            rows = self.rows(chip, self.core)
            other = self.grads[rows, self.half(1 - self.rep)]
            self.rep_out[chip] = (other + self.core_in[chip, :, self.local(1 - self.rep)].astype(WIDE)).astype(LOW)
        self.rep_copy().start()

    def late(self):
        self.rep_copy().wait_recv()
        for k in range(self.chips):
            chip = lax.rem(self.chip + k, self.chips)
            rows = self.rows(chip, self.core)
            mine = self.grads[rows, self.half(self.rep)]
            mine = mine + self.core_in[chip, :, self.local(self.rep)].astype(WIDE)
            mine = mine + self.rep_in[chip].astype(WIDE)
            if k == 0:
                self.grads[rows, self.half(self.rep)] = mine
            else:
                self.far_out[k - 1] = mine.astype(LOW)
                self.far_copy(k).start()

    def finish(self):
        total = self.grads[self.rows(self.chip, self.core), self.half(self.rep)]
        self.far_all().wait_recv()
        for k in range(1, self.chips):
            total = total + self.far_in[k - 1].astype(WIDE)
        low = total.astype(LOW)
        self.end_out[...] = low
        self.end_copy().start()
        self.share[:, self.half(self.rep)] = low

    def end(self):
        self.end_copy().wait_recv()
        self.share[:, self.half(1 - self.rep)] = self.end_in[...]
        self.rep_copy().wait_send()
        self.end_copy().wait_send()
        self.far_all().wait_send()


class Packets:
    def __init__(self, place, packets, sems, at):
        self.section, self.dp, self.rep, self.chips = place
        self.core, self.chip = lax.rem(self.dp, 2), self.dp // 2
        self.packets, self.sems, self.at = packets, sems, at

    def copy(self, spot, n, to):
        return remote(spot, spot, self.sems.at[0, self.at, n], self.sems.at[1, self.at, n], to)

    def along(self, k, chip):
        spot = self.packets.at[self.core, self.rep, chip]
        far = 2 * lax.rem(self.chip + k, self.chips) + self.core
        return self.copy(spot, k, (self.section, far, self.rep))

    def over_rep(self, rep):
        return self.copy(self.packets.at[self.core, rep], 0, (self.section, self.dp, 1 - self.rep))

    def over_core(self, core):
        to = (self.section, 2 * self.chip + 1 - self.core, self.rep)
        return self.copy(self.packets.at[core], self.chips, to)

    def begin(self, pieces):
        self.packets[self.core, self.rep, self.chip] = jnp.concatenate(pieces, axis=0).astype(LOW)
        for k in range(1, self.chips):
            self.along(k, self.chip).start()

    def middle(self):
        for k in range(1, self.chips):
            self.along(k, lax.rem(self.chip - k + self.chips, self.chips)).wait_recv()
        self.over_rep(self.rep).start()

    def late(self):
        self.over_rep(1 - self.rep).wait_recv()
        self.over_core(self.core).start()

    def finish(self):
        self.over_core(1 - self.core).wait_recv()
        for k in range(1, self.chips):
            self.along(k, self.chip).wait_send()
        self.over_rep(self.rep).wait_send()
        self.over_core(self.core).wait_send()
        width = self.packets.shape[-1]
        result = []
        for at in range(0, self.packets.shape[3], 16):
            part = self.packets[:, :, :, at : at + 16, :].astype(WIDE).reshape(4 * self.chips, 2, 8, width)
            result.append([part[:, m].reshape(32 * self.chips, width).astype(LOW) for m in range(2)])
        return result


def mod_share(scr, late, early, place, out, per):
    width = scr.node.shape[-1]
    second, condition = late.finish()
    (first,) = early.finish()
    scr.turned[...] = condition[0].T
    mine = scr.turned[pl.ds(pl.multiple_of(place[1] * per, 16), per), :]
    for at, part in enumerate(first + second):
        out[:, at * width : (at + 1) * width] = product(mine, part)


def layer_call(cols, linked, sizes, packed_in, raw, points, segments, neighbours, condition, cotangent, per):
    count, length, width = points.shape
    near = neighbours.shape[1]
    per_sim = cols.base.stop - cols.base.start
    chips = sizes[DP] // 2
    part = length // 2
    parts = tuple((cols.up[n].start, cols.down[n].stop) for n in range(CHUNKS))
    groups = (
        (0, cols.msg_out.stop),
        (cols.kv.start, cols.base.stop),
        (cols.mod.start, cols.mod.stop),
    ) + parts
    summed = (
        (0, cols.gain.stop),
        (cols.target.start, cols.msg_out.stop),
        (cols.kv.start, cols.kv.stop),
        (cols.q.start, cols.base.stop),
    ) + parts
    many = cols.mod.start
    rows = 8
    weights_in = list(raw) if linked else [packed_in]
    inputs = weights_in + [points, segments, neighbours, condition, cotangent]
    shape = jax.ShapeDtypeStruct
    outs = [
        shape((count, 2 * per_sim, width), LOW),
        shape((count, length, width), LOW),
        shape((count, length, width), LOW),
    ]
    outs.append(shape((per, many), LOW) if linked else shape((width, many), WIDE))
    outs.append(shape((per if linked else width, 4 * width), WIDE))
    scratch = dict(
        source_t=pltpu.VMEM((width, length), LOW),
        value_sum=pltpu.VMEM((width, part), WIDE),
        tokens=pltpu.VMEM((count, length, width), LOW),
        passed=pltpu.VMEM((count, length, width), LOW),
        mixed_t=pltpu.VMEM((count, width, length), LOW),
        slope=pltpu.VMEM((count, near, width, length), LOW),
        slope_sum=pltpu.VMEM((count, width, length), WIDE),
        node=pltpu.VMEM((count, length, width), WIDE),
        total=pltpu.VMEM((width, length), WIDE),
        point_out=pltpu.VMEM((count, length, width), LOW),
        point_in=pltpu.VMEM((count, length, width), LOW),
        back_in=pltpu.VMEM((count, length, width), LOW),
        modulation=pltpu.VMEM((rows, 4 * width), WIDE),
        condition=pltpu.VMEM((2 * rows, width), WIDE),
        base_unit=pltpu.VMEM((per_sim, width), WIDE),
        base_rows=pltpu.VMEM((per_sim, width), WIDE),
        base_scale=pltpu.VMEM((per_sim, 1), WIDE),
        gain_row=pltpu.VMEM((1, width), WIDE),
        d_gain=pltpu.VMEM((1, width), WIDE),
        d_base_unit=pltpu.VMEM((per_sim, width), WIDE),
        d_base=pltpu.VMEM((per_sim, width), WIDE),
        d_mod=pltpu.VMEM((rows, 4 * width), WIDE),
        lat_sems=pltpu.SemaphoreType.DMA((count,)),
        pass_sems=pltpu.SemaphoreType.DMA((2, 2 * count)),
        back_sems=pltpu.SemaphoreType.DMA((2, count)),
        point_local=pltpu.SemaphoreType.DMA((2,)),
        point_sems=pltpu.SemaphoreType.DMA((2, count)),
    )
    scratch.update(perceiver_scratch(count, length, width, per_sim, cols.chunk))
    bufs = []
    if linked:
        scratch.update(
            packed=pltpu.VMEM((chips, 2, per, cols.total), LOW),
            grads=pltpu.VMEM((width, many), WIDE),
            packets_two=pltpu.VMEM((2, 2, chips, 4 * rows, width), LOW),
            packets_one=pltpu.VMEM((2, 2, chips, 2 * rows, width), LOW),
            turned=pltpu.VMEM((width, 4 * chips * rows), LOW),
            packet_sems=pltpu.SemaphoreType.DMA((2, 2, chips + 1)),
            gather_send=pltpu.SemaphoreType.DMA((chips + 2,)),
            gather_recv=pltpu.SemaphoreType.DMA((len(groups), chips + 1)),
            scatter_send=pltpu.SemaphoreType.DMA((len(summed), 4)),
            scatter_recv=pltpu.SemaphoreType.DMA((len(summed), 4)),
        )
        for start, stop in summed:
            size = stop - start
            bufs += [
                pltpu.VMEM((chips, per, size), LOW),
                pltpu.VMEM((chips, per, size), LOW),
                pltpu.VMEM((chips, per, size // 2), LOW),
                pltpu.VMEM((chips - 1, per, size // 2), LOW),
                pltpu.VMEM((per, size // 2), LOW),
                pltpu.VMEM((per, size // 2), LOW),
            ]
    names = list(scratch)

    def body(*refs):
        ins, refs = refs[: len(inputs)], refs[len(inputs) :]
        results, refs = refs[: len(outs)], refs[len(outs) :]
        scr = types.SimpleNamespace(**dict(zip(names, refs)))
        moved = refs[len(names) :]
        points, segments, neighbours, condition, cotangent = ins[-5:]
        latents, point_mine, point_other = results[:3]
        section, dp, rep = (lax.axis_index(name) for name in (SECTION, DP, REP))
        other = (1 - section, dp, rep)
        if linked:
            packed, grads = Packed(scr.packed), scr.grads
            core, chip = lax.rem(dp, 2), dp // 2
            partners = [other, (section, dp, 1 - rep), (section, 2 * chip + 1 - core, rep)]
            partners += [(section, 2 * lax.rem(chip + k, chips) + core, rep) for k in range(1, chips)]
        else:
            packed, grads = ins[0], results[3]
            partners = [other]
        barrier = pltpu.get_barrier_semaphore()
        for to in partners:
            pl.semaphore_signal(barrier, inc=1, device_id=to, device_id_type=pl.DeviceIdType.MESH)
        if linked:
            place = (section, dp, rep, chips)
            gather = Gather(place, scr.packed, groups, (scr.gather_send, scr.gather_recv))
            msg_in, msg_out, norm_gain, mod_weight, query_base, q_weight, kv_weight, o_weight, up_weight, down_weight = ins[:10]
            mine = scr.packed.at[chip, core]
            mine[:, cols.source] = msg_in[0, :, :width]
            mine[:, cols.target] = msg_in[0, :, width:]
            mine[:, cols.msg_out] = msg_out[0]
            gain = jnp.broadcast_to(norm_gain[...].astype(WIDE), (128, per)).T
            mine[:, cols.gain] = gain.astype(LOW)
            mine[:, cols.kv] = kv_weight[0]
            mine[:, cols.q] = q_weight[0]
            mine[:, cols.o] = o_weight[0]
            mine[:, cols.base] = query_base[0]
            mine[:, cols.mod] = mod_weight[0]
            for n in range(CHUNKS):
                piece = slice(n * cols.chunk, (n + 1) * cols.chunk)
                mine[:, cols.up[n]] = up_weight[0, :, piece]
                mine[:, cols.down[n]] = down_weight[0, :, piece]
        pl.semaphore_wait(barrier, len(partners))
        if linked:
            gather.begin(0)
            gather.begin(1)
        first = grads.at[:, : cols.base.stop]
        first[...] = jnp.zeros_like(first)
        for total in (scr.d_gain, scr.d_base_unit, scr.d_base, scr.d_mod, scr.condition):
            total[...] = jnp.zeros_like(total)
        for b in range(count):
            scr.condition[2 * b : 2 * b + 2, :] = condition[b].astype(WIDE)
            scr.cot_t[:, b * 2 * per_sim : (b + 1) * 2 * per_sim] = cotangent[b].T

        tokens = scr.tokens

        @pl.when(section == 0)
        def _():
            tokens[...] = points[...]

        if linked:
            gather.near(0)
            gather.far(0)
            gather.begin(2)
            gather.late(0)
            gather.finish(0)
            gather.near(1)
            gather.begin(3)

        def pass_copy(n):
            b, half = n // 2, lax.rem(n, 2)
            rows = pl.ds(pl.multiple_of(half * part, part), part)
            return remote(
                scr.passed.at[b, rows, :], tokens.at[b, rows, :], scr.pass_sems.at[0, n], scr.pass_sems.at[1, n], other
            )

        def back_copy(b):
            return remote(scr.passed.at[b], scr.back_in.at[b], scr.back_sems.at[0, b], scr.back_sems.at[1, b], other)

        def point_copy(b):
            return remote(scr.point_out.at[b], scr.point_in.at[b], scr.point_sems.at[0, b], scr.point_sems.at[1, b], other)

        def forward(b):
            for half in range(2):
                n = 2 * b + half

                @pl.when(section == 1)
                def _():
                    pass_copy(n).wait_recv()

                message_half(b, half, cols, packed, points, tokens, neighbours, scr)

                @pl.when(section == 0)
                def _():
                    rows = slice(half * part, (half + 1) * part)
                    scr.passed[b, rows, :] = scr.node[b, rows, :].astype(LOW)
                    pass_copy(n).start()

                ahead = jnp.where(b == 2, 8 * half - 1, n + 2)
                gather_at(jnp.where(section == 0, n, ahead), (1, 3, 5, 7) if half else (0, 2, 4))

        def prepare():
            base = packed[:, cols.base].astype(WIDE).T
            scr.base_rows[...] = base
            unit, scale = normalised(base)
            scr.base_unit[...] = unit
            scr.base_scale[...] = scale
            scr.gain_row[...] = packed[:, cols.gain].astype(WIDE).T[:1]
            scr.modulation[...] = product(scr.condition[...].astype(LOW), packed[:, cols.mod])[:rows]

        def gather_step(n):
            if n == 0:
                gather.far(1)
            elif n == 1:
                gather.near(2)
                gather.begin(4)
            elif n == 2:
                gather.far(2)
            elif n == 3:
                gather.late(1)
                gather.near(3)
                gather.begin(5)
            elif n == 4:
                gather.far(3)
            elif n == 5:
                gather.late(2)
                gather.finish(1)
                gather.near(4)
                gather.finish(2)
                prepare()
            elif n == 6:
                gather.far(4)
                gather.late(3)
                gather.near(5)
            else:
                gather.far(5)
                gather.late(4)
                gather.finish(3)

        def gather_at(at, choices):
            if linked:
                for n in choices:

                    @pl.when(at == n)
                    def _():
                        gather_step(n)

        if linked:

            @pl.when(section == 1)
            def _():
                gather_step(0)
                gather_step(1)

        else:
            prepare()

        def early(step, carry):
            late_one = (step == 3) & (section == 1)
            early_one = (step == 2) & (section == 1)
            message = ((step < count) | late_one) & jnp.logical_not(early_one)
            b = jnp.where(message, jnp.minimum(step, count - 1), jnp.where(early_one, 0, step - count))

            @pl.when(message)
            def _():
                forward(b)

            @pl.when(jnp.logical_not(message))
            def _():
                attend(b, cols, packed, segments, scr)
                gather_at(jnp.where(section == 0, 6 + b, 6 + 2 * b), (6, 7))

            return carry

        lax.fori_loop(0, 2 * count, early, 0)
        if linked:
            scatters = [
                Scatter(
                    place, grads, results[3], per, summed[n], (scr.scatter_send, scr.scatter_recv), n,
                    moved[6 * n : 6 * n + 6],
                )
                for n in range(len(summed))
            ]

        def feed_first(b, carry):
            feed_in(b, cols, packed, scr)
            return carry

        lax.fori_loop(0, count, feed_first, 0)
        for at in range(CHUNKS):
            if linked and at > 0:
                gather.finish(3 + at)

            def feed_step(b, carry):
                feed_chunk(b, at, cols, packed, cotangent, scr)
                if linked and at == 0:

                    @pl.when(b == 0)
                    def _():
                        gather.late(5)

                return carry

            lax.fori_loop(0, count, feed_step, 0)
            grads[:, cols.down[at]] = product(scr.cot_t[...], scr.hidden[...])
            grads[:, cols.up[at]] = product(scr.second_t[...], scr.d_up[...])
            if linked:
                scatters[4 + at].begin()
                if at > 0:
                    scatters[3 + at].middle()
                if at > 1:
                    scatters[2 + at].late()

        if linked:
            halves = [slice(width * n, width * (n + 1)) for n in range(4)]
            packet_two = Packets(place, scr.packets_two, scr.packet_sems, 0)
            packet_one = Packets(place, scr.packets_one, scr.packet_sems, 1)

        def token_step(b):
            return token_back(b, cols, packed, tokens, scr, grads)

        def attention_back(b, carry):
            feed_out(b, cols, packed, cotangent, grads, scr)
            if linked:

                @pl.when(b == 0)
                def _():
                    scatters[6].middle()

                @pl.when(b == count - 1)
                def _():
                    packet_two.begin([scr.d_mod[:, halves[2]], scr.d_mod[:, halves[3]], scr.condition[...]])

            attend_back(b, cols, packed, segments, grads, scr)

            @pl.when(section == 1)
            def _():
                scr.passed[b] = token_step(b).astype(LOW)
                back_copy(b).start()

            if linked:

                @pl.when(b == 0)
                def _():
                    scatters[5].late()
                    scatters[4].finish()

                @pl.when(b == 1)
                def _():
                    scatters[6].late()
                    scatters[5].finish()

            return carry

        lax.fori_loop(0, count, attention_back, 0)
        if linked:
            scatters[2].begin()
        d_rows = normalised_back(scr.d_base_unit[...], scr.base_unit[...], scr.base_scale[...])
        grads[:, cols.base] = (d_rows + scr.d_base[...]).T
        grads[:, cols.gain] = jnp.broadcast_to(scr.d_gain[...], (128, width)).T
        if linked:
            scatters[3].begin()
            packet_one.begin([scr.d_mod[:, halves[0]], scr.d_mod[:, halves[1]]])
            packet_two.middle()

            @pl.when(section == 1)
            def _():
                scatters[1].begin()

            scatters[6].finish()
            scatters[2].middle()
        else:
            results[4][...] = trans_left(scr.condition[:rows].astype(LOW), scr.d_mod[...].astype(LOW))

        def backward(b, carry):
            @pl.when(section == 0)
            def _():
                back_copy(b).wait_recv()
                scr.node[b] = scr.node[b] + scr.back_in[b].astype(WIDE)
                scr.node[b] = token_step(b)

            @pl.when(section == 1)
            def _():
                scr.node[b] = jnp.zeros((length, width), WIDE)

            if linked:

                @pl.when((b == count - 1) & (section == 0))
                def _():
                    scatters[1].begin()

            d_points = source_back(b, cols, packed, points, neighbours, scr, grads)
            scr.point_out[b] = (scr.node[b] + d_points).astype(LOW)
            point_copy(b).start()
            if linked:

                @pl.when(b == 0)
                def _():
                    scatters[3].middle()
                    packet_one.middle()
                    packet_two.late()

                    @pl.when(section == 1)
                    def _():
                        scatters[1].middle()

                @pl.when(b == 1)
                def _():
                    packet_one.late()
                    scatters[2].late()

            return carry

        lax.fori_loop(0, count, backward, 0)
        if linked:
            scatters[0].begin()
            scatters[3].late()

            @pl.when(section == 0)
            def _():
                scatters[1].middle()

        feed_latents(0, cols, packed, latents, scr)
        if linked:
            scatters[0].middle()

            @pl.when(section == 1)
            def _():
                scatters[1].late()

        for b in range(1, count):
            feed_latents(b, cols, packed, latents, scr)
        if linked:
            scatters[2].finish()

            @pl.when(section == 0)
            def _():
                scatters[1].late()

            scatters[0].late()
            scatters[3].finish()
            for n in range(4, 4 + CHUNKS):
                scatters[n].end()
            mod_share(scr, packet_two, packet_one, place, results[4], per)
        for b in range(count):
            point_copy(b).wait_recv()
        point_moves = [
            pltpu.make_async_copy(scr.point_out, point_mine, scr.point_local.at[0]),
            pltpu.make_async_copy(scr.point_in, point_other, scr.point_local.at[1]),
        ]
        for move in point_moves:
            move.start()
        if linked:
            scatters[1].finish()
            scatters[0].finish()
            for n in (3, 2, 1, 0):
                scatters[n].end()
            gather.drain()
        for move in point_moves:
            move.wait()

        for b in range(count):
            pltpu.make_async_copy(scr.second.at[b], latents.at[b], scr.lat_sems.at[b]).wait()

        @pl.when(section == 0)
        def _():
            for n in range(2 * count):
                pass_copy(n).wait_send()

        @pl.when(section == 1)
        def _():
            for b in range(count):
                back_copy(b).wait_send()

        for b in range(count):
            point_copy(b).wait_send()

    spec = pl.BlockSpec(memory_space=pltpu.VMEM)
    return pl.pallas_call(
        body,
        out_shape=outs,
        in_specs=[spec] * len(inputs),
        out_specs=[pl.BlockSpec(memory_space=pl.ANY)] * 3 + [spec] * (len(outs) - 3),
        scratch_shapes=list(scratch.values()) + bufs,
        compiler_params=pltpu.CompilerParams(
            vmem_limit_bytes=VMEM_BYTES, collective_id=0, has_side_effects=True
        ),
        cost_estimate=pl.CostEstimate(flops=10**10, bytes_accessed=1 << 24, transcendentals=0),
        name="layers",
    )(*inputs)


def finish_call(cols, latents, point_mine, point_other, share, mod_share):
    per, width = share.shape[0], point_mine.shape[-1]
    pieces = ([cols.msg_out], [cols.gain], [cols.base], [cols.q], [cols.kv], [cols.o], cols.up, cols.down)
    gain_at = 1

    shape = jax.ShapeDtypeStruct
    outs = [shape(latents.shape, LOW), shape(mod_share.shape, WIDE), shape(point_mine.shape, WIDE)]
    outs.append(shape((1, per, 2 * width), WIDE))
    for n, piece in enumerate(pieces):
        outs.append(shape((1, per) if n == gain_at else (1, per, sum(place.stop - place.start for place in piece)), WIDE))
    inputs = (share, point_mine, point_other, latents, mod_share)
    count = len(outs)

    def body(*refs):
        ins, refs = refs[: len(inputs)], refs[len(inputs) :]
        results, refs = refs[:count], refs[count:]
        held, refs = refs[: len(inputs)], refs[len(inputs) :]
        made, sems = refs[:-1], refs[-1]
        arriving = [pltpu.make_async_copy(a, b, sems.at[n]) for n, (a, b) in enumerate(zip(ins, held))]
        for move in arriving:
            move.start()
        share, point_mine, point_other, latents, mod_share = held
        sources = [latents, mod_share, *made]
        leaving = [
            pltpu.make_async_copy(a, b, sems.at[len(inputs) + n]) for n, (a, b) in enumerate(zip(sources, results))
        ]
        arriving[0].wait()
        msg_in, parts = made[1], made[2:]
        msg_in[0, :, :width] = share[:, cols.source].astype(WIDE)
        msg_in[0, :, width:] = share[:, cols.target].astype(WIDE)
        leaving[3].start()
        for n, piece in enumerate(pieces):
            at = 0
            for place in piece:
                value = share[:, place].astype(WIDE)
                size = place.stop - place.start
                if n == gain_at:
                    parts[n][...] = value.T[:1]
                else:
                    parts[n][0, :, at : at + size] = value
                at += size
            leaving[4 + n].start()
        arriving[1].wait()
        arriving[2].wait()
        made[0][...] = point_mine[...].astype(WIDE) + point_other[...].astype(WIDE)
        leaving[2].start()
        for n in (0, 1):
            arriving[3 + n].wait()
            leaving[n].start()
        for move in leaving:
            move.wait()

    whole = pl.BlockSpec(memory_space=pl.ANY)
    results = pl.pallas_call(
        body,
        out_shape=outs,
        in_specs=[whole] * len(inputs),
        out_specs=[whole] * count,
        scratch_shapes=[pltpu.VMEM(a.shape, a.dtype) for a in inputs]
        + [pltpu.VMEM(a.shape, a.dtype) for a in outs[2:]]
        + [pltpu.SemaphoreType.DMA((len(inputs) + count,))],
        compiler_params=pltpu.CompilerParams(vmem_limit_bytes=VMEM_BYTES),
        cost_estimate=pl.CostEstimate(flops=10**6, bytes_accessed=1 << 23, transcendentals=0),
        name="finish",
    )(*inputs)
    latents, mod, point_sum, msg_in, msg_out, gain, base, q, kv, o, up, down = results
    turn = lambda array: jnp.swapaxes(array, 1, 2)
    return (latents[None], point_sum, turn(msg_in), msg_out, gain, mod[None], turn(base), q, kv, o, up, turn(down))


def on_device(
    points,
    segments,
    neighbours,
    condition,
    msg_in,
    msg_out,
    norm_gain,
    mod_weight,
    query_base,
    q_weight,
    kv_weight,
    o_weight,
    up_weight,
    down_weight,
    cotangent,
):
    count, length, width = points.shape
    per = q_weight.shape[1]
    hidden = up_weight.shape[2]
    per_sim = query_base.shape[1]
    cols = Columns(width, hidden, per_sim)
    sizes = {name: lax.axis_size(name) for name in (SECTION, DP, REP)}
    linked = per % 16 == 0 and sizes[DP] % 2 == 0 and sizes[REP] == 2
    raw = (
        jnp.swapaxes(msg_in, 1, 2),
        msg_out,
        norm_gain,
        mod_weight,
        jnp.swapaxes(query_base, 1, 2),
        q_weight,
        kv_weight,
        o_weight,
        up_weight,
        jnp.swapaxes(down_weight, 1, 2),
    )
    near_t = jnp.swapaxes(neighbours, 1, 2)
    if linked:
        outs = layer_call(cols, True, sizes, None, raw, points, segments, near_t, condition, cotangent[0], per)
        return finish_call(cols, *outs)
    turned = msg_in[0].T
    own = jnp.concatenate(
        [
            turned[:, :width],
            jnp.broadcast_to(norm_gain[0][:, None], (per, 128)),
            turned[:, width:],
            msg_out[0],
            kv_weight[0],
            q_weight[0],
            o_weight[0],
            query_base[0].T,
            *sum(
                (
                    [up_weight[0, :, n : n + cols.chunk], down_weight[0, n : n + cols.chunk].T]
                    for n in range(0, hidden, cols.chunk)
                ),
                [],
            ),
            mod_weight[0],
        ],
        axis=1,
    )
    packed = lax.all_gather(own, DP, axis=0, tiled=True)
    latents, point_mine, point_other, grads, mod_grads = layer_call(
        cols, False, sizes, packed, None, points, segments, near_t, condition, cotangent[0], per
    )
    grads = jnp.concatenate([grads, mod_grads], axis=1)
    share = lax.psum_scatter(grads, DP, scatter_dimension=0, tiled=True)
    share = lax.psum(share.astype(LOW), REP).astype(WIDE)
    return (
        latents[None],
        point_mine.astype(WIDE) + point_other.astype(WIDE),
        jnp.concatenate([share[:, cols.source], share[:, cols.target]], axis=1).T[None],
        share[None, :, cols.msg_out],
        share[None, :, cols.gain.start],
        share[None, :, cols.mod],
        share[:, cols.base].T[None],
        share[None, :, cols.q],
        share[None, :, cols.kv],
        share[None, :, cols.o],
        jnp.concatenate([share[None, :, piece] for piece in cols.up], axis=2),
        jnp.concatenate([share[:, piece] for piece in cols.down], axis=1).T[None],
    )


def solution(mesh):
    placed = (
        P((DP, REP), None, None),
        P((DP, REP), None),
        P((DP, REP), None, None),
        P((DP, REP), None, None),
        P(SECTION, None, DP),
        P(SECTION, DP, None),
        P(SECTION, DP),
        P(SECTION, DP, None),
        P(SECTION, None, DP),
        P(SECTION, DP, None),
        P(SECTION, DP, None),
        P(SECTION, DP, None),
        P(SECTION, DP, None),
        P(SECTION, None, DP),
        P(SECTION, (DP, REP), None, None),
    )
    return jax.shard_map(
        on_device,
        mesh=mesh,
        in_specs=placed,
        out_specs=(
            P(SECTION, (DP, REP), None, None),
            P((DP, REP), None, None),
            P(SECTION, None, DP),
            P(SECTION, DP, None),
            P(SECTION, DP),
            P(SECTION, DP, None),
            P(SECTION, None, DP),
            P(SECTION, DP, None),
            P(SECTION, DP, None),
            P(SECTION, DP, None),
            P(SECTION, DP, None),
            P(SECTION, None, DP),
        ),
        check_vma=False,
    )
```

```python
import types

import jax
import jax.numpy as jnp
from jax import lax
from jax.experimental import pallas as pl
from jax.experimental.pallas import tpu as pltpu
from jax.sharding import PartitionSpec as P

HEADS = 6
HEAD_DIM = 64
EPSILON = 1e-05
TANH_ONE = 0.7978845608028654
TANH_THREE = 0.7978845608028654 * 0.044715
CUBE = TANH_THREE ** (1.0 / 3.0)
SECTION, DP, REP = "section", "dp", "rep"
CHUNKS = 3
LOW = jnp.bfloat16
WIDE = jnp.float32
VMEM_BYTES = 63 * 1024 * 1024


def product(left_op, right_op):
    return jnp.dot(left_op, right_op, preferred_element_type=WIDE)


def trans_left(left_op, right_op):
    return lax.dot_general(left_op, right_op, (((0,), (0,)), ((), ())), preferred_element_type=WIDE)


def trans_right(left_op, right_op):
    return lax.dot_general(left_op, right_op, (((1,), (1,)), ((), ())), preferred_element_type=WIDE)


def gelu_pair(inside):
    square = inside * inside
    half = 0.5 + 0.5 * jnp.tanh(inside * (TANH_ONE + TANH_THREE * square))
    value = inside * half
    slope = half + value * (1.0 - half) * (2.0 * TANH_ONE + 6.0 * TANH_THREE * square)
    return value, slope


def gelu_cubed(inside):
    kind = inside.dtype
    square = inside * inside
    bend = jnp.tanh(inside * (square + jnp.asarray(TANH_ONE / CUBE, kind)))
    upper = bend + jnp.asarray(1.0, kind)
    value = inside * upper
    steep = value * (jnp.asarray(1.0, kind) - bend) * (square + jnp.asarray(TANH_ONE / (3.0 * CUBE), kind))
    return value, upper * jnp.asarray(1.0 / 3.0, kind) + steep


def normalised(values):
    centre = values - jnp.mean(values, axis=-1, keepdims=True)
    spread = jnp.mean(centre * centre, axis=-1, keepdims=True)
    scale = lax.rsqrt(spread + EPSILON)
    return centre * scale, scale


def normalised_back(d_out, unit, scale):
    first = jnp.mean(d_out, axis=-1, keepdims=True)
    second = jnp.mean(d_out * unit, axis=-1, keepdims=True)
    return scale * (d_out - first - unit * second)


class Columns:
    def __init__(self, width, hidden, per_sim):
        self.pieces = (
            ("source", width),
            ("gain", 128),
            ("target", width),
            ("msg_out", width),
            ("kv", 2 * width),
            ("q", width),
            ("o", width),
            ("base", per_sim),
        )
        at = 0
        for name, extent in self.pieces:
            setattr(self, name, slice(at, at + extent))
            at += extent
        self.chunk = hidden // CHUNKS
        self.up, self.down = [], []
        for _ in range(CHUNKS):
            self.up.append(slice(at, at + self.chunk))
            self.down.append(slice(at + self.chunk, at + 2 * self.chunk))
            at += 2 * self.chunk
        self.mod = slice(at, at + 4 * width)
        at += 4 * width
        self.total = at


def evolution_masks(b, segments, length):
    second_count = jnp.sum(segments[pl.ds(b, 1), :], axis=1, keepdims=True)
    first_count = length - second_count
    own_col = (lax.broadcasted_iota(jnp.int32, (length, 1), 0) < first_count).astype(WIDE)
    own_row = (lax.broadcasted_iota(jnp.int32, (1, length), 1) < first_count).astype(WIDE)
    return own_col, own_row


def spread_heads(values, own_col):
    lane = lax.broadcasted_iota(jnp.int32, (1, values.shape[1]), 1)
    sims = (own_col.astype(LOW), (1.0 - own_col).astype(LOW))
    halves = ((lane < HEAD_DIM).astype(WIDE).astype(LOW), (lane >= HEAD_DIM).astype(WIDE).astype(LOW))
    return [jnp.concatenate([values * sims[0] * half, values * sims[1] * half], axis=1) for half in halves]


def by_sim(rows_in, pair):
    block = 2 * HEAD_DIM
    per_sim = rows_in.shape[0] // 2
    here = slice(pair * block, (pair + 1) * block)
    return jnp.concatenate([rows_in[:per_sim, here], rows_in[per_sim:, here]], axis=1)


def mod_rows(b, scr, width):
    return (
        [scr.modulation[pl.ds(2 * b + s, 1), width * n : width * (n + 1)] for s in range(2)] for n in range(4)
    )


def first_rows(b, scr, width):
    scale_one, shift_one, _, _ = mod_rows(b, scr, width)
    rows = [(1.0 + scale_one[s]) * scr.base_unit[...] + shift_one[s] for s in range(2)]
    return jnp.concatenate(rows, axis=0).astype(LOW)


def attend(b, cols, packed, segments, scr):
    length, width = scr.node.shape[1:]
    per_sim = scr.base_rows.shape[0]
    block = 2 * HEAD_DIM
    unit, _ = normalised(scr.node[b])
    normed = (unit * scr.gain_row[...]).astype(LOW)
    keyval = product(normed, packed[:, cols.kv]).astype(LOW)
    scr.values[b] = keyval[:, width:]
    scr.keyval_t[b] = keyval.T
    own_col, own_row = evolution_masks(b, segments, length)
    low_row = (own_row.astype(LOW), (1.0 - own_row).astype(LOW))
    query = (product(first_rows(b, scr, width), packed[:, cols.q]).astype(LOW) * 0.125).astype(LOW)
    scr.query[b] = query
    mask = own_col > 0.5
    ones = jnp.concatenate([jnp.broadcast_to(own_row, (8, length)), jnp.broadcast_to(1.0 - own_row, (8, length))], axis=0)
    ones = ones.astype(LOW)
    for pair in range(HEADS // 2):
        keys = spread_heads(keyval[:, pair * block : (pair + 1) * block], own_col)
        raw_pair = trans_right(jnp.concatenate(keys, axis=0), by_sim(query, pair))
        for h in range(2):
            head = 2 * pair + h
            raw = raw_pair[h * length : (h + 1) * length]
            top_first = jnp.max(jnp.where(mask, raw, -3e38), axis=0, keepdims=True)
            top_second = jnp.max(jnp.where(mask, -3e38, raw), axis=0, keepdims=True)
            grown = jnp.exp(raw - jnp.where(mask, top_first, top_second)).astype(LOW)
            scr.weights_t[b, head] = grown
            here = slice(head * HEAD_DIM, (head + 1) * HEAD_DIM)
            value_t = scr.keyval_t[b, width + here.start : width + here.stop, :]
            value_sims = jnp.concatenate([value_t * low_row[0], value_t * low_row[1], ones], axis=0)
            out_t = product(value_sims, grown)
            inverse = 1.0 / out_t[2 * HEAD_DIM :]
            scr.inverse[b, head : head + 1, :per_sim] = inverse[:1]
            scr.inverse[b, head : head + 1, per_sim:] = inverse[8:9]
            scr.attended_t[b, here, :per_sim] = (out_t[:HEAD_DIM] * inverse[:1]).astype(LOW)
            scr.attended_t[b, here, per_sim:] = (out_t[HEAD_DIM : 2 * HEAD_DIM] * inverse[8:9]).astype(LOW)


def residual_of(b, cols, packed, scr):
    residual = trans_left(scr.attended_t[b], packed[:, cols.o])
    return residual + jnp.concatenate([scr.base_rows[...]] * 2, axis=0)


def feed_in(b, cols, packed, scr):
    width = scr.node.shape[-1]
    per_sim = scr.base_rows.shape[0]
    _, _, scale_two, shift_two = mod_rows(b, scr, width)
    unit, _ = normalised(residual_of(b, cols, packed, scr))
    second = jnp.concatenate(
        [(1.0 + scale_two[s]) * unit[s * per_sim : (s + 1) * per_sim] + shift_two[s] for s in range(2)], axis=0
    ).astype(LOW)
    scr.second[b] = second
    scr.second_t[:, pl.ds(pl.multiple_of(b * 2 * per_sim, 2 * per_sim), 2 * per_sim)] = second.T


def feed_chunk(b, at, cols, packed, cotangent, scr):
    up, down = cols.up[at], cols.down[at]
    queries = scr.second.shape[1]
    here = pl.ds(pl.multiple_of(b * queries, queries), queries)
    value, steep = gelu_cubed((product(scr.second[b], packed[:, up]) * CUBE).astype(LOW))
    hidden = value * jnp.asarray(0.5 / CUBE, LOW)
    d_up = (product(cotangent[b], packed[:, down]) * 1.5).astype(LOW) * steep
    scr.hidden[here, :] = hidden
    scr.d_up[here, :] = d_up
    if at == 0:
        scr.d_second[b] = trans_right(d_up, packed[:, up])
    else:
        scr.d_second[b] += trans_right(d_up, packed[:, up])
    if at == 0:
        scr.lat_sum[b] = trans_right(hidden, packed[:, down])
    elif at < CHUNKS - 1:
        scr.lat_sum[b] += trans_right(hidden, packed[:, down])


def feed_latents(b, cols, packed, latents, scr):
    queries = scr.second.shape[1]
    here = pl.ds(pl.multiple_of(b * queries, queries), queries)
    last = trans_right(scr.hidden[here, :], packed[:, cols.down[CHUNKS - 1]])
    scr.second[b] = (scr.lat_sum[b] + last).astype(LOW)
    pltpu.make_async_copy(scr.second.at[b], latents.at[b], scr.lat_sems.at[b]).start()


def feed_out(b, cols, packed, cotangent, grads, scr):
    width = scr.node.shape[-1]
    per_sim = scr.base_rows.shape[0]
    _, _, scale_two, _ = mod_rows(b, scr, width)
    attended_t = scr.attended_t[b]
    residual = residual_of(b, cols, packed, scr)
    res_unit, res_scale = normalised(residual)
    scr.lat_sum[b] += residual
    d_second = scr.d_second[b]
    d_res = []
    for s in range(2):
        rows_at = slice(s * per_sim, (s + 1) * per_sim)
        d_sim = d_second[rows_at]
        unit_sim = res_unit[rows_at]
        scr.d_mod[pl.ds(2 * b + s, 1), 2 * width : 3 * width] = jnp.sum(d_sim * unit_sim, axis=0, keepdims=True)
        scr.d_mod[pl.ds(2 * b + s, 1), 3 * width :] = jnp.sum(d_sim, axis=0, keepdims=True)
        d_res.append(
            cotangent[b, rows_at, :].astype(WIDE)
            + normalised_back(d_sim * (1.0 + scale_two[s]), unit_sim, res_scale[rows_at])
        )
    scr.d_base[...] += d_res[0] + d_res[1]
    res_low = jnp.concatenate(d_res, axis=0).astype(LOW)
    grads[:, cols.o] += product(attended_t, res_low)
    d_att = trans_right(packed[:, cols.o], res_low)
    for head in range(HEADS):
        there = slice(head * HEAD_DIM, (head + 1) * HEAD_DIM)
        scaled = d_att[there] * scr.inverse[b, head : head + 1, :]
        both = scaled * attended_t[there].astype(WIDE)
        scr.overlap[b, head : head + 1, :] = jnp.sum(both, axis=0, keepdims=True)
        scr.attended_t[b, there, :] = scaled.astype(LOW)


def attend_back(b, cols, packed, segments, grads, scr):
    length, width = scr.node.shape[1:]
    per_sim = scr.base_rows.shape[0]
    block = 2 * HEAD_DIM
    own_col, own_row = evolution_masks(b, segments, length)
    low_row = (own_row.astype(LOW), (1.0 - own_row).astype(LOW))
    mask = own_col > 0.5
    left_half = lax.broadcasted_iota(jnp.int32, (1, block), 1) < HEAD_DIM
    values_all = scr.values[b]
    query = scr.query[b]
    d_att = scr.attended_t[b]
    for pair in range(HEADS // 2):
        here = slice(pair * block, (pair + 1) * block)
        values = spread_heads(values_all[:, here], own_col)
        query_pair = by_sim(query, pair)
        d_att_pair = jnp.concatenate([d_att[here, :per_sim], d_att[here, per_sim:]], axis=0)
        d_share_pair = product(jnp.concatenate(values, axis=0), d_att_pair)
        d_raws = []
        for h in range(2):
            head = 2 * pair + h
            there = slice(head * HEAD_DIM, (head + 1) * HEAD_DIM)
            both = scr.overlap[b, head : head + 1, :]
            d_share = d_share_pair[h * length : (h + 1) * length]
            d_raw = (
                scr.weights_t[b, head].astype(WIDE)
                * (d_share - jnp.where(mask, both[:, :per_sim], both[:, per_sim:]))
            ).astype(LOW)
            d_raws.append(d_raw)
            key_t = scr.keyval_t[b, there, :]
            key_sims = jnp.concatenate([key_t * low_row[0], key_t * low_row[1]], axis=0)
            d_q = (product(key_sims, d_raw) * 0.125).astype(LOW)
            scr.query_t[there, :per_sim] = d_q[:HEAD_DIM]
            scr.query_t[there, per_sim:] = d_q[HEAD_DIM:]
        shares = scr.weights_t[b, 2 * pair : 2 * pair + 2].reshape(2 * length, per_sim)
        d_keys, d_values = [], []
        for full, parts in (
            (product(jnp.concatenate(d_raws, axis=0), query_pair), d_keys),
            (trans_right(shares, d_att_pair), d_values),
        ):
            for h in range(2):
                own = full[h * length : (h + 1) * length]
                parts.append(jnp.where(mask, own[:, :block], own[:, block:]))
        scr.d_keyval[:, here] = jnp.where(left_half, d_keys[0], d_keys[1]).astype(LOW)
        scr.d_keyval[:, width + here.start : width + here.stop] = jnp.where(
            left_half, d_values[0], d_values[1]
        ).astype(LOW)

    scale_one, shift_one, _, _ = mod_rows(b, scr, width)
    d_query = scr.query_t[...].T
    grads[:, cols.q] += trans_left(first_rows(b, scr, width), d_query)
    d_first = trans_right(d_query, packed[:, cols.q])
    for s in range(2):
        d_sim = d_first[s * per_sim : (s + 1) * per_sim]
        scr.d_mod[pl.ds(2 * b + s, 1), :width] = jnp.sum(d_sim * scr.base_unit[...], axis=0, keepdims=True)
        scr.d_mod[pl.ds(2 * b + s, 1), width : 2 * width] = jnp.sum(d_sim, axis=0, keepdims=True)
        scr.d_base_unit[...] += d_sim * (1.0 + scale_one[s])

    unit, node_scale = normalised(scr.node[b])
    gain = scr.gain_row[...]
    d_kv = scr.d_keyval[...]
    grads[:, cols.kv] += trans_left((unit * gain).astype(LOW), d_kv)
    d_normed = trans_right(d_kv, packed[:, cols.kv])
    scr.d_gain[...] += jnp.sum(d_normed * unit, axis=0, keepdims=True)
    scr.node[b] = normalised_back(d_normed * gain, unit, node_scale)


def perceiver_scratch(count, length, width, per_sim, chunk):
    queries = 2 * per_sim
    return dict(
        values=pltpu.VMEM((count, length, width), LOW),
        keyval_t=pltpu.VMEM((count, 2 * width, length), LOW),
        query=pltpu.VMEM((count, queries, width), LOW),
        weights_t=pltpu.VMEM((count, HEADS, length, per_sim), LOW),
        attended_t=pltpu.VMEM((count, width, queries), LOW),
        overlap=pltpu.VMEM((count, 8, queries), WIDE),
        inverse=pltpu.VMEM((count, 8, queries), WIDE),
        second=pltpu.VMEM((count, queries, width), LOW),
        second_t=pltpu.VMEM((width, count * queries), LOW),
        cot_t=pltpu.VMEM((width, count * queries), LOW),
        hidden=pltpu.VMEM((count * queries, chunk), LOW),
        d_up=pltpu.VMEM((count * queries, chunk), LOW),
        lat_sum=pltpu.VMEM((count, queries, width), WIDE),
        d_second=pltpu.VMEM((count, queries, width), WIDE),
        query_t=pltpu.VMEM((width, queries), LOW),
        d_keyval=pltpu.VMEM((length, 2 * width), LOW),
    )


def one_hot(near_t, edges, columns, length):
    picks = []
    for k in edges:
        row = near_t[k : k + 1, columns].astype(jnp.int16)
        spot = lax.broadcasted_iota(jnp.int16, (length, row.shape[1]), 0)
        picks.append(jnp.where(row == spot, jnp.asarray(1.0, LOW), jnp.asarray(0.0, LOW)))
    return jnp.concatenate(picks, axis=1)


def message_half(b, half, cols, packed, points, tokens, neighbours, scr):
    length, width = points.shape[1:]
    count = neighbours.shape[1]
    part = length // 2
    here = slice(half * part, (half + 1) * part)
    if half == 0:
        scr.source_t[...] = (trans_right(packed[:, cols.source], points[b]) * CUBE).astype(LOW)
    target = (trans_right(packed[:, cols.target], tokens[b, here, :]) * CUBE).astype(LOW)
    target = jnp.concatenate([target, target], axis=1)
    near_t = neighbours[b]
    group = 8
    for at in range(0, count, group):
        value, steep = None, None
        for k in range(at, at + group, 2):
            inside = product(scr.source_t[...], one_hot(near_t, (k, k + 1), here, length)).astype(LOW) + target
            v, t = gelu_cubed(inside)
            scr.slope[b, k, :, here] = t[:, :part]
            scr.slope[b, k + 1, :, here] = t[:, part:]
            v, t = v[:, :part] + v[:, part:], t[:, :part] + t[:, part:]
            value, steep = (v, t) if value is None else (value + v, steep + t)
        if at == 0:
            scr.value_sum[...] = value.astype(WIDE)
            scr.slope_sum[b, :, here] = steep.astype(WIDE)
        else:
            scr.value_sum[...] += value.astype(WIDE)
            scr.slope_sum[b, :, here] += steep.astype(WIDE)
    mixed = (scr.value_sum[...] * (0.5 / (count * CUBE))).astype(LOW)
    scr.mixed_t[b, :, here] = mixed
    scr.node[b, here, :] = tokens[b, here, :].astype(WIDE) + trans_left(mixed, packed[:, cols.msg_out])


def token_back(b, cols, packed, tokens, scr, grads):
    count = scr.slope.shape[1]
    d_out = scr.node[b]
    node_low = d_out.astype(LOW)
    grads[:, cols.msg_out] += product(scr.mixed_t[b], node_low)
    d_mixed = trans_right(packed[:, cols.msg_out], node_low) * (1.5 / count)
    scr.mixed_t[b] = d_mixed.astype(LOW)
    d_target = (d_mixed * scr.slope_sum[b]).astype(LOW)
    grads[:, cols.target] += product(d_target, tokens[b])
    return d_out + trans_left(d_target, packed[:, cols.target])


def source_back(b, cols, packed, points, neighbours, scr, grads):
    length = points.shape[1]
    count = neighbours.shape[1]
    near_t = neighbours[b]
    group = 4
    low = scr.mixed_t[b]
    for at in range(0, count, group):
        edges = range(at, at + group)
        inside = jnp.concatenate([scr.slope[b, k] * low for k in edges], axis=1)
        part = trans_right(inside, one_hot(near_t, edges, slice(0, length), length))
        if at == 0:
            scr.total[...] = part
        else:
            scr.total[...] += part
    d_source = scr.total[...].astype(LOW)
    grads[:, cols.source] += product(d_source, points[b])
    return trans_left(d_source, packed[:, cols.source])


def remote(src, dst, send, recv, to):
    return pltpu.make_async_remote_copy(
        src_ref=src, dst_ref=dst, send_sem=send, recv_sem=recv, device_id=to, device_id_type=pl.DeviceIdType.MESH
    )


class Packed:
    def __init__(self, ref):
        self.ref = ref

    def __getitem__(self, index):
        piece = self.ref[:, :, :, index[1]]
        return piece.reshape(-1, piece.shape[-1])


class Gather:
    def __init__(self, place, ref, groups, sems):
        self.section, self.dp, self.rep, self.chips = place
        self.ref, self.groups = ref, groups
        self.core = lax.rem(self.dp, 2)
        self.chip = self.dp // 2
        self.send, self.recv = sems
        self.line = self.chips == 4

    def half(self, group, which):
        start, stop = self.groups[group]
        size = (stop - start) // 2
        return pl.ds(pl.multiple_of(start + which * size, 128), size)

    def whole(self, group):
        start, stop = self.groups[group]
        return pl.ds(start, stop - start)

    def source(self, k):
        return lax.rem(self.chip - k + self.chips, self.chips)

    def copy(self, spot, send, group, recv, to):
        return remote(spot, spot, self.send.at[send], self.recv.at[group, recv], to)

    def along(self, group, k, chip):
        spot = self.ref.at[chip, self.core, :, self.half(group, self.rep)]
        far = 2 * lax.rem(self.chip + k, self.chips) + self.core
        return self.copy(spot, k - 1, group, k - 1, (self.section, far, self.rep))

    def onward(self, group):
        to, k = 3 * (self.chip - 1), 2 * self.chip - 1
        spot = self.ref.at[self.source(2), self.core, :, self.half(group, self.rep)]
        return self.copy(spot, self.chips - 1, group, k - 1, (self.section, 2 * to + self.core, self.rep))

    def over_rep(self, group, chip):
        spot = self.ref.at[chip, self.core, :, self.half(group, self.rep)]
        return self.copy(spot, self.chips, group, self.chips - 1, (self.section, self.dp, 1 - self.rep))

    def from_rep(self, group):
        spot = self.ref.at[pl.ds(0, self.chips - 1), self.core, :, self.half(group, 1 - self.rep)]
        return self.copy(spot, self.chips, group, self.chips - 1, (self.section, self.dp, 1 - self.rep))

    def over_core(self, group, core):
        spot = self.ref.at[:, core, :, self.whole(group)]
        to = (self.section, 2 * self.chip + 1 - self.core, self.rep)
        return self.copy(spot, self.chips + 1, group, self.chips, to)

    def ends(self, k):
        return jnp.abs(lax.rem(self.chip + k, self.chips) - self.chip) == self.chips - 1

    def inner(self):
        return (self.chip == 1) | (self.chip == 2)

    def direct(self, k, act):
        if self.line:

            @pl.when(jnp.logical_not(self.ends(k)))
            def _():
                act()

        else:
            act()

    def begin(self, group):
        for k in range(1, self.chips):
            self.direct(k, lambda: self.along(group, k, self.chip).start())

    def arrived(self, group, n):
        last = jnp.where(self.chip == 0, 1, 3)
        k = [2, 4 - last, last][n] if self.line else n + 1
        chip = self.source(k)
        self.along(group, k, chip).wait_recv()
        if self.line and n == 0:

            @pl.when(self.inner())
            def _():
                self.onward(group).start()

        self.over_rep(group, chip).start()

    def near(self, group):
        for n in range(self.chips - 2):
            self.arrived(group, n)

    def far(self, group):
        self.arrived(group, self.chips - 2)

    def late(self, group):
        self.from_rep(group).wait_recv()
        self.over_core(group, self.core).start()

    def finish(self, group):
        self.over_core(group, 1 - self.core).wait_recv()

    def drain(self):
        total = self.ref.shape[-1]
        part = pl.ds(0, total // 2)
        home = (self.section, self.dp, 1 - self.rep)
        for k in range(1, self.chips):
            spot = self.ref.at[self.chip, self.core, :, part]
            self.direct(k, lambda: self.copy(spot, k - 1, 0, k - 1, home).wait_send())
        if self.line:

            @pl.when(self.inner())
            def _():
                self.copy(self.ref.at[self.chip, self.core, :, part], self.chips - 1, 0, 0, home).wait_send()

        spot = self.ref.at[pl.ds(0, self.chips - 1), self.core, :, part]
        self.copy(spot, self.chips, 0, 0, home).wait_send()
        self.copy(self.ref.at[:, self.core], self.chips + 1, 0, 0, home).wait_send()


class Scatter:
    def __init__(self, place, grads, share, per, columns, sems, at, bufs):
        self.section, self.dp, self.rep, self.chips = place
        self.grads, self.share, self.per, self.columns = grads, share, per, columns
        self.core = lax.rem(self.dp, 2)
        self.chip = self.dp // 2
        self.sems, self.at = sems, at
        self.core_out, self.core_in, self.rep_in, self.far_in, self.end_out, self.end_in = bufs
        self.size = (columns[1] - columns[0]) // 2
        self.rep_out = self.core_out.at[:, :, : self.size]
        self.far_out = self.core_out.at[:, :, self.size :]

    def rows(self, chip, core):
        return pl.ds(pl.multiple_of((2 * chip + core) * self.per, 16), self.per)

    def half(self, which):
        return pl.ds(pl.multiple_of(self.columns[0] + which * self.size, 128), self.size)

    def local(self, which):
        return pl.ds(pl.multiple_of(which * self.size, 128), self.size)

    def pair(self, kind):
        return self.sems[0].at[self.at, kind], self.sems[1].at[self.at, kind]

    def core_copy(self):
        to = (self.section, 2 * self.chip + 1 - self.core, self.rep)
        return remote(self.core_out, self.core_in, *self.pair(0), to)

    def rep_copy(self):
        return remote(self.rep_out, self.rep_in, *self.pair(1), (self.section, self.dp, 1 - self.rep))

    def far_copy(self, k):
        to = (self.section, 2 * lax.rem(self.chip + k, self.chips) + self.core, self.rep)
        return remote(self.far_out.at[k - 1], self.far_in.at[k - 1], *self.pair(3), to)

    def far_all(self):
        return remote(self.far_out.at[: self.chips - 1], self.far_in, *self.pair(3), (self.section, self.dp, 1 - self.rep))

    def end_copy(self):
        return remote(self.end_out, self.end_in, *self.pair(2), (self.section, self.dp, 1 - self.rep))

    def begin(self):
        start, stop = self.columns
        for chip in range(self.chips):
            self.core_out[chip] = self.grads[self.rows(chip, 1 - self.core), start:stop].astype(LOW)
        self.core_copy().start()

    def middle(self):
        self.core_copy().wait()
        for chip in range(self.chips):
            rows = self.rows(chip, self.core)
            other = self.grads[rows, self.half(1 - self.rep)]
            self.rep_out[chip] = (other + self.core_in[chip, :, self.local(1 - self.rep)].astype(WIDE)).astype(LOW)
        self.rep_copy().start()

    def late(self):
        self.rep_copy().wait_recv()
        for k in range(self.chips):
            chip = lax.rem(self.chip + k, self.chips)
            rows = self.rows(chip, self.core)
            mine = self.grads[rows, self.half(self.rep)]
            mine = mine + self.core_in[chip, :, self.local(self.rep)].astype(WIDE)
            mine = mine + self.rep_in[chip].astype(WIDE)
            if k == 0:
                self.grads[rows, self.half(self.rep)] = mine
            else:
                self.far_out[k - 1] = mine.astype(LOW)
                self.far_copy(k).start()

    def finish(self):
        total = self.grads[self.rows(self.chip, self.core), self.half(self.rep)]
        self.far_all().wait_recv()
        for k in range(1, self.chips):
            total = total + self.far_in[k - 1].astype(WIDE)
        low = total.astype(LOW)
        self.end_out[...] = low
        self.end_copy().start()
        self.share[:, self.half(self.rep)] = low

    def end(self):
        self.end_copy().wait_recv()
        self.share[:, self.half(1 - self.rep)] = self.end_in[...]
        self.rep_copy().wait_send()
        self.end_copy().wait_send()
        self.far_all().wait_send()


class Packets:
    def __init__(self, place, packets, sems, at):
        self.section, self.dp, self.rep, self.chips = place
        self.core, self.chip = lax.rem(self.dp, 2), self.dp // 2
        self.packets, self.sems, self.at = packets, sems, at

    def copy(self, spot, n, to):
        return remote(spot, spot, self.sems.at[0, self.at, n], self.sems.at[1, self.at, n], to)

    def along(self, k, chip):
        spot = self.packets.at[self.core, self.rep, chip]
        far = 2 * lax.rem(self.chip + k, self.chips) + self.core
        return self.copy(spot, k, (self.section, far, self.rep))

    def over_rep(self, rep):
        return self.copy(self.packets.at[self.core, rep], 0, (self.section, self.dp, 1 - self.rep))

    def over_core(self, core):
        to = (self.section, 2 * self.chip + 1 - self.core, self.rep)
        return self.copy(self.packets.at[core], self.chips, to)

    def begin(self, pieces):
        self.packets[self.core, self.rep, self.chip] = jnp.concatenate(pieces, axis=0).astype(LOW)
        for k in range(1, self.chips):
            self.along(k, self.chip).start()

    def middle(self):
        for k in range(1, self.chips):
            self.along(k, lax.rem(self.chip - k + self.chips, self.chips)).wait_recv()
        self.over_rep(self.rep).start()

    def late(self):
        self.over_rep(1 - self.rep).wait_recv()
        self.over_core(self.core).start()

    def finish(self):
        self.over_core(1 - self.core).wait_recv()
        for k in range(1, self.chips):
            self.along(k, self.chip).wait_send()
        self.over_rep(self.rep).wait_send()
        self.over_core(self.core).wait_send()
        width = self.packets.shape[-1]
        result = []
        for at in range(0, self.packets.shape[3], 16):
            part = self.packets[:, :, :, at : at + 16, :].astype(WIDE).reshape(4 * self.chips, 2, 8, width)
            result.append([part[:, m].reshape(32 * self.chips, width).astype(LOW) for m in range(2)])
        return result


def mod_share(scr, late, early, place, out, per):
    width = scr.node.shape[-1]
    second, condition = late.finish()
    (first,) = early.finish()
    scr.turned[...] = condition[0].T
    mine = scr.turned[pl.ds(pl.multiple_of(place[1] * per, 16), per), :]
    for at, part in enumerate(first + second):
        out[:, at * width : (at + 1) * width] = product(mine, part)


def layer_call(cols, linked, sizes, packed_in, raw, points, segments, neighbours, condition, cotangent, per):
    count, length, width = points.shape
    near = neighbours.shape[1]
    per_sim = cols.base.stop - cols.base.start
    chips = sizes[DP] // 2
    part = length // 2
    parts = tuple((cols.up[n].start, cols.down[n].stop) for n in range(CHUNKS))
    groups = (
        (0, cols.msg_out.stop),
        (cols.kv.start, cols.base.stop),
        (cols.mod.start, cols.mod.stop),
    ) + parts
    summed = (
        (0, cols.gain.stop),
        (cols.target.start, cols.msg_out.stop),
        (cols.kv.start, cols.kv.stop),
        (cols.q.start, cols.base.stop),
    ) + parts
    many = cols.mod.start
    rows = 8
    weights_in = list(raw) if linked else [packed_in]
    inputs = weights_in + [points, segments, neighbours, condition, cotangent]
    shape = jax.ShapeDtypeStruct
    outs = [
        shape((count, 2 * per_sim, width), LOW),
        shape((count, length, width), LOW),
        shape((count, length, width), LOW),
    ]
    outs.append(shape((per, many), LOW) if linked else shape((width, many), WIDE))
    outs.append(shape((per if linked else width, 4 * width), WIDE))
    scratch = dict(
        source_t=pltpu.VMEM((width, length), LOW),
        value_sum=pltpu.VMEM((width, part), WIDE),
        tokens=pltpu.VMEM((count, length, width), LOW),
        passed=pltpu.VMEM((count, length, width), LOW),
        mixed_t=pltpu.VMEM((count, width, length), LOW),
        slope=pltpu.VMEM((count, near, width, length), LOW),
        slope_sum=pltpu.VMEM((count, width, length), WIDE),
        node=pltpu.VMEM((count, length, width), WIDE),
        total=pltpu.VMEM((width, length), WIDE),
        point_out=pltpu.VMEM((count, length, width), LOW),
        point_in=pltpu.VMEM((count, length, width), LOW),
        back_in=pltpu.VMEM((count, length, width), LOW),
        modulation=pltpu.VMEM((rows, 4 * width), WIDE),
        condition=pltpu.VMEM((2 * rows, width), WIDE),
        base_unit=pltpu.VMEM((per_sim, width), WIDE),
        base_rows=pltpu.VMEM((per_sim, width), WIDE),
        base_scale=pltpu.VMEM((per_sim, 1), WIDE),
        gain_row=pltpu.VMEM((1, width), WIDE),
        d_gain=pltpu.VMEM((1, width), WIDE),
        d_base_unit=pltpu.VMEM((per_sim, width), WIDE),
        d_base=pltpu.VMEM((per_sim, width), WIDE),
        d_mod=pltpu.VMEM((rows, 4 * width), WIDE),
        lat_sems=pltpu.SemaphoreType.DMA((count,)),
        pass_sems=pltpu.SemaphoreType.DMA((2, 2 * count)),
        back_sems=pltpu.SemaphoreType.DMA((2, count)),
        point_local=pltpu.SemaphoreType.DMA((2,)),
        point_sems=pltpu.SemaphoreType.DMA((2, count)),
    )
    scratch.update(perceiver_scratch(count, length, width, per_sim, cols.chunk))
    bufs = []
    if linked:
        scratch.update(
            packed=pltpu.VMEM((chips, 2, per, cols.total), LOW),
            grads=pltpu.VMEM((width, many), WIDE),
            packets_two=pltpu.VMEM((2, 2, chips, 4 * rows, width), LOW),
            packets_one=pltpu.VMEM((2, 2, chips, 2 * rows, width), LOW),
            turned=pltpu.VMEM((width, 4 * chips * rows), LOW),
            packet_sems=pltpu.SemaphoreType.DMA((2, 2, chips + 1)),
            gather_send=pltpu.SemaphoreType.DMA((chips + 2,)),
            gather_recv=pltpu.SemaphoreType.DMA((len(groups), chips + 1)),
            scatter_send=pltpu.SemaphoreType.DMA((len(summed), 4)),
            scatter_recv=pltpu.SemaphoreType.DMA((len(summed), 4)),
        )
        for start, stop in summed:
            size = stop - start
            bufs += [
                pltpu.VMEM((chips, per, size), LOW),
                pltpu.VMEM((chips, per, size), LOW),
                pltpu.VMEM((chips, per, size // 2), LOW),
                pltpu.VMEM((chips - 1, per, size // 2), LOW),
                pltpu.VMEM((per, size // 2), LOW),
                pltpu.VMEM((per, size // 2), LOW),
            ]
    names = list(scratch)

    def body(*refs):
        ins, refs = refs[: len(inputs)], refs[len(inputs) :]
        results, refs = refs[: len(outs)], refs[len(outs) :]
        scr = types.SimpleNamespace(**dict(zip(names, refs)))
        moved = refs[len(names) :]
        points, segments, neighbours, condition, cotangent = ins[-5:]
        latents, point_mine, point_other = results[:3]
        section, dp, rep = (lax.axis_index(name) for name in (SECTION, DP, REP))
        other = (1 - section, dp, rep)
        if linked:
            packed, grads = Packed(scr.packed), scr.grads
            core, chip = lax.rem(dp, 2), dp // 2
            partners = [other, (section, dp, 1 - rep), (section, 2 * chip + 1 - core, rep)]
            partners += [(section, 2 * lax.rem(chip + k, chips) + core, rep) for k in range(1, chips)]
        else:
            packed, grads = ins[0], results[3]
            partners = [other]
        barrier = pltpu.get_barrier_semaphore()
        for to in partners:
            pl.semaphore_signal(barrier, inc=1, device_id=to, device_id_type=pl.DeviceIdType.MESH)
        if linked:
            place = (section, dp, rep, chips)
            gather = Gather(place, scr.packed, groups, (scr.gather_send, scr.gather_recv))
            msg_in, msg_out, norm_gain, mod_weight, query_base, q_weight, kv_weight, o_weight, up_weight, down_weight = ins[:10]
            mine = scr.packed.at[chip, core]
            mine[:, cols.source] = msg_in[0, :, :width]
            mine[:, cols.target] = msg_in[0, :, width:]
            mine[:, cols.msg_out] = msg_out[0]
            gain = jnp.broadcast_to(norm_gain[...].astype(WIDE), (128, per)).T
            mine[:, cols.gain] = gain.astype(LOW)
            mine[:, cols.kv] = kv_weight[0]
            mine[:, cols.q] = q_weight[0]
            mine[:, cols.o] = o_weight[0]
            mine[:, cols.base] = query_base[0]
            mine[:, cols.mod] = mod_weight[0]
            for n in range(CHUNKS):
                piece = slice(n * cols.chunk, (n + 1) * cols.chunk)
                mine[:, cols.up[n]] = up_weight[0, :, piece]
                mine[:, cols.down[n]] = down_weight[0, :, piece]
        pl.semaphore_wait(barrier, len(partners))
        if linked:
            gather.begin(0)
            gather.begin(1)
        first = grads.at[:, : cols.base.stop]
        first[...] = jnp.zeros_like(first)
        for total in (scr.d_gain, scr.d_base_unit, scr.d_base, scr.d_mod, scr.condition):
            total[...] = jnp.zeros_like(total)
        for b in range(count):
            scr.condition[2 * b : 2 * b + 2, :] = condition[b].astype(WIDE)
            scr.cot_t[:, b * 2 * per_sim : (b + 1) * 2 * per_sim] = cotangent[b].T

        tokens = scr.tokens

        @pl.when(section == 0)
        def _():
            tokens[...] = points[...]

        if linked:
            gather.near(0)
            gather.far(0)
            gather.begin(2)
            gather.late(0)
            gather.finish(0)
            gather.near(1)
            gather.begin(3)

        def pass_copy(n):
            b, half = n // 2, lax.rem(n, 2)
            rows = pl.ds(pl.multiple_of(half * part, part), part)
            return remote(
                scr.passed.at[b, rows, :], tokens.at[b, rows, :], scr.pass_sems.at[0, n], scr.pass_sems.at[1, n], other
            )

        def back_copy(b):
            return remote(scr.passed.at[b], scr.back_in.at[b], scr.back_sems.at[0, b], scr.back_sems.at[1, b], other)

        def point_copy(b):
            return remote(scr.point_out.at[b], scr.point_in.at[b], scr.point_sems.at[0, b], scr.point_sems.at[1, b], other)

        def forward(b):
            for half in range(2):
                n = 2 * b + half

                @pl.when(section == 1)
                def _():
                    pass_copy(n).wait_recv()

                message_half(b, half, cols, packed, points, tokens, neighbours, scr)

                @pl.when(section == 0)
                def _():
                    rows = slice(half * part, (half + 1) * part)
                    scr.passed[b, rows, :] = scr.node[b, rows, :].astype(LOW)
                    pass_copy(n).start()

                ahead = jnp.where(b == 2, 8 * half - 1, n + 2)
                gather_at(jnp.where(section == 0, n, ahead), (1, 3, 5, 7) if half else (0, 2, 4))

        def prepare():
            base = packed[:, cols.base].astype(WIDE).T
            scr.base_rows[...] = base
            unit, scale = normalised(base)
            scr.base_unit[...] = unit
            scr.base_scale[...] = scale
            scr.gain_row[...] = packed[:, cols.gain].astype(WIDE).T[:1]
            scr.modulation[...] = product(scr.condition[...].astype(LOW), packed[:, cols.mod])[:rows]

        def gather_step(n):
            if n == 0:
                gather.far(1)
            elif n == 1:
                gather.near(2)
                gather.begin(4)
            elif n == 2:
                gather.far(2)
            elif n == 3:
                gather.late(1)
                gather.near(3)
                gather.begin(5)
            elif n == 4:
                gather.far(3)
            elif n == 5:
                gather.late(2)
                gather.finish(1)
                gather.near(4)
                gather.finish(2)
                prepare()
            elif n == 6:
                gather.far(4)
                gather.late(3)
                gather.near(5)
            else:
                gather.far(5)
                gather.late(4)
                gather.finish(3)

        def gather_at(at, choices):
            if linked:
                for n in choices:

                    @pl.when(at == n)
                    def _():
                        gather_step(n)

        if linked:

            @pl.when(section == 1)
            def _():
                gather_step(0)
                gather_step(1)

        else:
            prepare()

        def early(step, carry):
            late_one = (step == 3) & (section == 1)
            early_one = (step == 2) & (section == 1)
            message = ((step < count) | late_one) & jnp.logical_not(early_one)
            b = jnp.where(message, jnp.minimum(step, count - 1), jnp.where(early_one, 0, step - count))

            @pl.when(message)
            def _():
                forward(b)

            @pl.when(jnp.logical_not(message))
            def _():
                attend(b, cols, packed, segments, scr)
                gather_at(jnp.where(section == 0, 6 + b, 6 + 2 * b), (6, 7))

            return carry

        lax.fori_loop(0, 2 * count, early, 0)
        if linked:
            scatters = [
                Scatter(
                    place, grads, results[3], per, summed[n], (scr.scatter_send, scr.scatter_recv), n,
                    moved[6 * n : 6 * n + 6],
                )
                for n in range(len(summed))
            ]

        def feed_first(b, carry):
            feed_in(b, cols, packed, scr)
            return carry

        lax.fori_loop(0, count, feed_first, 0, unroll=True)
        for at in range(CHUNKS):
            if linked and at > 0:
                gather.finish(3 + at)

            def feed_step(b, carry):
                feed_chunk(b, at, cols, packed, cotangent, scr)
                if linked and at == 0:

                    @pl.when(b == 0)
                    def _():
                        gather.late(5)

                return carry

            lax.fori_loop(0, count, feed_step, 0, unroll=True)
            grads[:, cols.down[at]] = product(scr.cot_t[...], scr.hidden[...])
            grads[:, cols.up[at]] = product(scr.second_t[...], scr.d_up[...])
            if linked:
                scatters[4 + at].begin()
                if at > 0:
                    scatters[3 + at].middle()
                if at > 1:
                    scatters[2 + at].late()

        if linked:
            halves = [slice(width * n, width * (n + 1)) for n in range(4)]
            packet_two = Packets(place, scr.packets_two, scr.packet_sems, 0)
            packet_one = Packets(place, scr.packets_one, scr.packet_sems, 1)

        def token_step(b):
            return token_back(b, cols, packed, tokens, scr, grads)

        def attention_back(b, carry):
            feed_out(b, cols, packed, cotangent, grads, scr)
            if linked:

                @pl.when(b == 0)
                def _():
                    scatters[6].middle()

                @pl.when(b == count - 1)
                def _():
                    packet_two.begin([scr.d_mod[:, halves[2]], scr.d_mod[:, halves[3]], scr.condition[...]])

            attend_back(b, cols, packed, segments, grads, scr)

            @pl.when(section == 1)
            def _():
                scr.passed[b] = token_step(b).astype(LOW)
                back_copy(b).start()

            if linked:

                @pl.when(b == 0)
                def _():
                    scatters[5].late()
                    scatters[4].finish()

                @pl.when(b == 1)
                def _():
                    scatters[6].late()
                    scatters[5].finish()

            return carry

        lax.fori_loop(0, count, attention_back, 0)
        if linked:
            scatters[2].begin()
        d_rows = normalised_back(scr.d_base_unit[...], scr.base_unit[...], scr.base_scale[...])
        grads[:, cols.base] = (d_rows + scr.d_base[...]).T
        grads[:, cols.gain] = jnp.broadcast_to(scr.d_gain[...], (128, width)).T
        if linked:
            scatters[3].begin()
            packet_one.begin([scr.d_mod[:, halves[0]], scr.d_mod[:, halves[1]]])
            packet_two.middle()

            @pl.when(section == 1)
            def _():
                scatters[1].begin()

            scatters[6].finish()
            scatters[2].middle()
        else:
            results[4][...] = trans_left(scr.condition[:rows].astype(LOW), scr.d_mod[...].astype(LOW))

        def backward(b, carry):
            @pl.when(section == 0)
            def _():
                back_copy(b).wait_recv()
                scr.node[b] = scr.node[b] + scr.back_in[b].astype(WIDE)
                scr.node[b] = token_step(b)

            @pl.when(section == 1)
            def _():
                scr.node[b] = jnp.zeros((length, width), WIDE)

            if linked:

                @pl.when((b == count - 1) & (section == 0))
                def _():
                    scatters[1].begin()

            d_points = source_back(b, cols, packed, points, neighbours, scr, grads)
            scr.point_out[b] = (scr.node[b] + d_points).astype(LOW)
            point_copy(b).start()
            if linked:

                @pl.when(b == 0)
                def _():
                    scatters[3].middle()
                    packet_one.middle()
                    packet_two.late()

                    @pl.when(section == 1)
                    def _():
                        scatters[1].middle()

                @pl.when(b == 1)
                def _():
                    packet_one.late()
                    scatters[2].late()

            return carry

        lax.fori_loop(0, count, backward, 0)
        if linked:
            scatters[0].begin()
            scatters[3].late()

            @pl.when(section == 0)
            def _():
                scatters[1].middle()

        feed_latents(0, cols, packed, latents, scr)
        if linked:
            scatters[0].middle()

            @pl.when(section == 1)
            def _():
                scatters[1].late()

        for b in range(1, count):
            feed_latents(b, cols, packed, latents, scr)
        if linked:
            scatters[2].finish()

            @pl.when(section == 0)
            def _():
                scatters[1].late()

            scatters[0].late()
            scatters[3].finish()
            for n in range(4, 4 + CHUNKS):
                scatters[n].end()
            mod_share(scr, packet_two, packet_one, place, results[4], per)
        for b in range(count):
            point_copy(b).wait_recv()
        point_moves = [
            pltpu.make_async_copy(scr.point_out, point_mine, scr.point_local.at[0]),
            pltpu.make_async_copy(scr.point_in, point_other, scr.point_local.at[1]),
        ]
        for move in point_moves:
            move.start()
        if linked:
            scatters[1].finish()
            scatters[0].finish()
            for n in (3, 2, 1, 0):
                scatters[n].end()
            gather.drain()
        for move in point_moves:
            move.wait()

        for b in range(count):
            pltpu.make_async_copy(scr.second.at[b], latents.at[b], scr.lat_sems.at[b]).wait()

        @pl.when(section == 0)
        def _():
            for n in range(2 * count):
                pass_copy(n).wait_send()

        @pl.when(section == 1)
        def _():
            for b in range(count):
                back_copy(b).wait_send()

        for b in range(count):
            point_copy(b).wait_send()

    spec = pl.BlockSpec(memory_space=pltpu.VMEM)
    return pl.pallas_call(
        body,
        out_shape=outs,
        in_specs=[spec] * len(inputs),
        out_specs=[pl.BlockSpec(memory_space=pl.ANY)] * 3 + [spec] * (len(outs) - 3),
        scratch_shapes=list(scratch.values()) + bufs,
        compiler_params=pltpu.CompilerParams(
            vmem_limit_bytes=VMEM_BYTES, collective_id=0, has_side_effects=True
        ),
        cost_estimate=pl.CostEstimate(flops=10**10, bytes_accessed=1 << 24, transcendentals=0),
        name="layers",
    )(*inputs)


def finish_call(cols, latents, point_mine, point_other, share, mod_share):
    per, width = share.shape[0], point_mine.shape[-1]
    pieces = ([cols.msg_out], [cols.gain], [cols.base], [cols.q], [cols.kv], [cols.o], cols.up, cols.down)
    gain_at = 1

    shape = jax.ShapeDtypeStruct
    outs = [shape(latents.shape, LOW), shape(mod_share.shape, WIDE), shape(point_mine.shape, WIDE)]
    outs.append(shape((1, per, 2 * width), WIDE))
    for n, piece in enumerate(pieces):
        outs.append(shape((1, per) if n == gain_at else (1, per, sum(place.stop - place.start for place in piece)), WIDE))
    inputs = (share, point_mine, point_other, latents, mod_share)
    count = len(outs)

    def body(*refs):
        ins, refs = refs[: len(inputs)], refs[len(inputs) :]
        results, refs = refs[:count], refs[count:]
        held, refs = refs[: len(inputs)], refs[len(inputs) :]
        made, sems = refs[:-1], refs[-1]
        arriving = [pltpu.make_async_copy(a, b, sems.at[n]) for n, (a, b) in enumerate(zip(ins, held))]
        for move in arriving:
            move.start()
        share, point_mine, point_other, latents, mod_share = held
        sources = [latents, mod_share, *made]
        leaving = [
            pltpu.make_async_copy(a, b, sems.at[len(inputs) + n]) for n, (a, b) in enumerate(zip(sources, results))
        ]
        arriving[0].wait()
        msg_in, parts = made[1], made[2:]
        msg_in[0, :, :width] = share[:, cols.source].astype(WIDE)
        msg_in[0, :, width:] = share[:, cols.target].astype(WIDE)
        leaving[3].start()
        for n, piece in enumerate(pieces):
            at = 0
            for place in piece:
                value = share[:, place].astype(WIDE)
                size = place.stop - place.start
                if n == gain_at:
                    parts[n][...] = value.T[:1]
                else:
                    parts[n][0, :, at : at + size] = value
                at += size
            leaving[4 + n].start()
        arriving[1].wait()
        arriving[2].wait()
        made[0][...] = point_mine[...].astype(WIDE) + point_other[...].astype(WIDE)
        leaving[2].start()
        for n in (0, 1):
            arriving[3 + n].wait()
            leaving[n].start()
        for move in leaving:
            move.wait()

    whole = pl.BlockSpec(memory_space=pl.ANY)
    results = pl.pallas_call(
        body,
        out_shape=outs,
        in_specs=[whole] * len(inputs),
        out_specs=[whole] * count,
        scratch_shapes=[pltpu.VMEM(a.shape, a.dtype) for a in inputs]
        + [pltpu.VMEM(a.shape, a.dtype) for a in outs[2:]]
        + [pltpu.SemaphoreType.DMA((len(inputs) + count,))],
        compiler_params=pltpu.CompilerParams(vmem_limit_bytes=VMEM_BYTES),
        cost_estimate=pl.CostEstimate(flops=10**6, bytes_accessed=1 << 23, transcendentals=0),
        name="finish",
    )(*inputs)
    latents, mod, point_sum, msg_in, msg_out, gain, base, q, kv, o, up, down = results
    turn = lambda array: jnp.swapaxes(array, 1, 2)
    return (latents[None], point_sum, turn(msg_in), msg_out, gain, mod[None], turn(base), q, kv, o, up, turn(down))


def on_device(
    points,
    segments,
    neighbours,
    condition,
    msg_in,
    msg_out,
    norm_gain,
    mod_weight,
    query_base,
    q_weight,
    kv_weight,
    o_weight,
    up_weight,
    down_weight,
    cotangent,
):
    count, length, width = points.shape
    per = q_weight.shape[1]
    hidden = up_weight.shape[2]
    per_sim = query_base.shape[1]
    cols = Columns(width, hidden, per_sim)
    sizes = {name: lax.axis_size(name) for name in (SECTION, DP, REP)}
    linked = per % 16 == 0 and sizes[DP] % 2 == 0 and sizes[REP] == 2
    raw = (
        jnp.swapaxes(msg_in, 1, 2),
        msg_out,
        norm_gain,
        mod_weight,
        jnp.swapaxes(query_base, 1, 2),
        q_weight,
        kv_weight,
        o_weight,
        up_weight,
        jnp.swapaxes(down_weight, 1, 2),
    )
    near_t = jnp.swapaxes(neighbours, 1, 2)
    if linked:
        outs = layer_call(cols, True, sizes, None, raw, points, segments, near_t, condition, cotangent[0], per)
        return finish_call(cols, *outs)
    turned = msg_in[0].T
    own = jnp.concatenate(
        [
            turned[:, :width],
            jnp.broadcast_to(norm_gain[0][:, None], (per, 128)),
            turned[:, width:],
            msg_out[0],
            kv_weight[0],
            q_weight[0],
            o_weight[0],
            query_base[0].T,
            *sum(
                (
                    [up_weight[0, :, n : n + cols.chunk], down_weight[0, n : n + cols.chunk].T]
                    for n in range(0, hidden, cols.chunk)
                ),
                [],
            ),
            mod_weight[0],
        ],
        axis=1,
    )
    packed = lax.all_gather(own, DP, axis=0, tiled=True)
    latents, point_mine, point_other, grads, mod_grads = layer_call(
        cols, False, sizes, packed, None, points, segments, near_t, condition, cotangent[0], per
    )
    grads = jnp.concatenate([grads, mod_grads], axis=1)
    share = lax.psum_scatter(grads, DP, scatter_dimension=0, tiled=True)
    share = lax.psum(share.astype(LOW), REP).astype(WIDE)
    return (
        latents[None],
        point_mine.astype(WIDE) + point_other.astype(WIDE),
        jnp.concatenate([share[:, cols.source], share[:, cols.target]], axis=1).T[None],
        share[None, :, cols.msg_out],
        share[None, :, cols.gain.start],
        share[None, :, cols.mod],
        share[:, cols.base].T[None],
        share[None, :, cols.q],
        share[None, :, cols.kv],
        share[None, :, cols.o],
        jnp.concatenate([share[None, :, piece] for piece in cols.up], axis=2),
        jnp.concatenate([share[:, piece] for piece in cols.down], axis=1).T[None],
    )


def solution(mesh):
    placed = (
        P((DP, REP), None, None),
        P((DP, REP), None),
        P((DP, REP), None, None),
        P((DP, REP), None, None),
        P(SECTION, None, DP),
        P(SECTION, DP, None),
        P(SECTION, DP),
        P(SECTION, DP, None),
        P(SECTION, None, DP),
        P(SECTION, DP, None),
        P(SECTION, DP, None),
        P(SECTION, DP, None),
        P(SECTION, DP, None),
        P(SECTION, None, DP),
        P(SECTION, (DP, REP), None, None),
    )
    return jax.shard_map(
        on_device,
        mesh=mesh,
        in_specs=placed,
        out_specs=(
            P(SECTION, (DP, REP), None, None),
            P((DP, REP), None, None),
            P(SECTION, None, DP),
            P(SECTION, DP, None),
            P(SECTION, DP),
            P(SECTION, DP, None),
            P(SECTION, None, DP),
            P(SECTION, DP, None),
            P(SECTION, DP, None),
            P(SECTION, DP, None),
            P(SECTION, DP, None),
            P(SECTION, None, DP),
        ),
        check_vma=False,
    )
```

```python
import types

import jax
import jax.numpy as jnp
from jax import lax
from jax.experimental import pallas as pl
from jax.experimental.pallas import tpu as pltpu
from jax.sharding import PartitionSpec as P

HEADS = 6
HEAD_DIM = 64
EPSILON = 1e-05
TANH_ONE = 0.7978845608028654
TANH_THREE = 0.7978845608028654 * 0.044715
CUBE = TANH_THREE ** (1.0 / 3.0)
SECTION, DP, REP = "section", "dp", "rep"
CHUNKS = 3
LOW = jnp.bfloat16
WIDE = jnp.float32
VMEM_BYTES = 63 * 1024 * 1024


def product(left_op, right_op):
    return jnp.dot(left_op, right_op, preferred_element_type=WIDE)


def trans_left(left_op, right_op):
    return lax.dot_general(left_op, right_op, (((0,), (0,)), ((), ())), preferred_element_type=WIDE)


def trans_right(left_op, right_op):
    return lax.dot_general(left_op, right_op, (((1,), (1,)), ((), ())), preferred_element_type=WIDE)


def gelu_pair(inside):
    square = inside * inside
    half = 0.5 + 0.5 * jnp.tanh(inside * (TANH_ONE + TANH_THREE * square))
    value = inside * half
    slope = half + value * (1.0 - half) * (2.0 * TANH_ONE + 6.0 * TANH_THREE * square)
    return value, slope


def gelu_cubed(inside):
    kind = inside.dtype
    square = inside * inside
    bend = jnp.tanh(inside * (square + jnp.asarray(TANH_ONE / CUBE, kind)))
    upper = bend + jnp.asarray(1.0, kind)
    value = inside * upper
    steep = value * (jnp.asarray(1.0, kind) - bend) * (square + jnp.asarray(TANH_ONE / (3.0 * CUBE), kind))
    return value, upper * jnp.asarray(1.0 / 3.0, kind) + steep


def normalised(values):
    centre = values - jnp.mean(values, axis=-1, keepdims=True)
    spread = jnp.mean(centre * centre, axis=-1, keepdims=True)
    scale = lax.rsqrt(spread + EPSILON)
    return centre * scale, scale


def normalised_back(d_out, unit, scale):
    first = jnp.mean(d_out, axis=-1, keepdims=True)
    second = jnp.mean(d_out * unit, axis=-1, keepdims=True)
    return scale * (d_out - first - unit * second)


class Columns:
    def __init__(self, width, hidden, per_sim):
        self.pieces = (
            ("source", width),
            ("gain", 128),
            ("target", width),
            ("msg_out", width),
            ("kv", 2 * width),
            ("q", width),
            ("o", width),
            ("base", per_sim),
        )
        at = 0
        for name, extent in self.pieces:
            setattr(self, name, slice(at, at + extent))
            at += extent
        self.chunk = hidden // CHUNKS
        self.order = (*range(1, CHUNKS), 0)
        self.up, self.down = [None] * CHUNKS, [None] * CHUNKS
        for n in self.order:
            self.up[n] = slice(at, at + self.chunk)
            self.down[n] = slice(at + self.chunk, at + 2 * self.chunk)
            at += 2 * self.chunk
        self.mod_two = slice(at, at + 2 * width)
        self.mod_one = slice(at + 2 * width, at + 4 * width)
        at += 4 * width
        self.total = at


def evolution_masks(b, segments, length):
    second_count = jnp.sum(segments[pl.ds(b, 1), :], axis=1, keepdims=True)
    first_count = length - second_count
    own_col = (lax.broadcasted_iota(jnp.int32, (length, 1), 0) < first_count).astype(WIDE)
    own_row = (lax.broadcasted_iota(jnp.int32, (1, length), 1) < first_count).astype(WIDE)
    return own_col, own_row


def spread_heads(values, own_col):
    lane = lax.broadcasted_iota(jnp.int32, (1, values.shape[1]), 1)
    sims = (own_col.astype(LOW), (1.0 - own_col).astype(LOW))
    halves = ((lane < HEAD_DIM).astype(WIDE).astype(LOW), (lane >= HEAD_DIM).astype(WIDE).astype(LOW))
    return [jnp.concatenate([values * sims[0] * half, values * sims[1] * half], axis=1) for half in halves]


def by_sim(rows_in, pair):
    block = 2 * HEAD_DIM
    per_sim = rows_in.shape[0] // 2
    here = slice(pair * block, (pair + 1) * block)
    return jnp.concatenate([rows_in[:per_sim, here], rows_in[per_sim:, here]], axis=1)


def mod_rows(b, scr, width):
    return (
        [scr.modulation[pl.ds(2 * b + s, 1), width * n : width * (n + 1)] for s in range(2)] for n in range(4)
    )


def first_rows(b, scr, width):
    scale_one, shift_one, _, _ = mod_rows(b, scr, width)
    rows = [(1.0 + scale_one[s]) * scr.base_unit[...] + shift_one[s] for s in range(2)]
    return jnp.concatenate(rows, axis=0).astype(LOW)


def attend(b, cols, packed, segments, scr):
    length, width = scr.node.shape[1:]
    per_sim = scr.base_rows.shape[0]
    block = 2 * HEAD_DIM
    unit, _ = normalised(scr.node[b])
    normed = (unit * scr.gain_row[...]).astype(LOW)
    keyval = product(normed, packed[:, cols.kv]).astype(LOW)
    scr.values[b] = keyval[:, width:]
    scr.keyval_t[b] = keyval.T
    own_col, own_row = evolution_masks(b, segments, length)
    low_row = (own_row.astype(LOW), (1.0 - own_row).astype(LOW))
    query = (product(first_rows(b, scr, width), packed[:, cols.q]).astype(LOW) * 0.125).astype(LOW)
    scr.query[b] = query
    mask = own_col > 0.5
    ones = jnp.concatenate([jnp.broadcast_to(own_row, (8, length)), jnp.broadcast_to(1.0 - own_row, (8, length))], axis=0)
    ones = ones.astype(LOW)
    for pair in range(HEADS // 2):
        keys = spread_heads(keyval[:, pair * block : (pair + 1) * block], own_col)
        raw_pair = trans_right(jnp.concatenate(keys, axis=0), by_sim(query, pair))
        for h in range(2):
            head = 2 * pair + h
            raw = raw_pair[h * length : (h + 1) * length]
            top_first = jnp.max(jnp.where(mask, raw, -3e38), axis=0, keepdims=True)
            top_second = jnp.max(jnp.where(mask, -3e38, raw), axis=0, keepdims=True)
            grown = jnp.exp(raw - jnp.where(mask, top_first, top_second)).astype(LOW)
            scr.weights_t[b, head] = grown
            here = slice(head * HEAD_DIM, (head + 1) * HEAD_DIM)
            value_t = scr.keyval_t[b, width + here.start : width + here.stop, :]
            value_sims = jnp.concatenate([value_t * low_row[0], value_t * low_row[1], ones], axis=0)
            out_t = product(value_sims, grown)
            inverse = 1.0 / out_t[2 * HEAD_DIM :]
            scr.inverse[b, head : head + 1, :per_sim] = inverse[:1]
            scr.inverse[b, head : head + 1, per_sim:] = inverse[8:9]
            scr.attended_t[b, here, :per_sim] = (out_t[:HEAD_DIM] * inverse[:1]).astype(LOW)
            scr.attended_t[b, here, per_sim:] = (out_t[HEAD_DIM : 2 * HEAD_DIM] * inverse[8:9]).astype(LOW)


def residual_of(b, cols, packed, scr):
    residual = trans_left(scr.attended_t[b], packed[:, cols.o])
    return residual + jnp.concatenate([scr.base_rows[...]] * 2, axis=0)


def feed_in(b, cols, packed, scr):
    width = scr.node.shape[-1]
    per_sim = scr.base_rows.shape[0]
    _, _, scale_two, shift_two = mod_rows(b, scr, width)
    unit, _ = normalised(residual_of(b, cols, packed, scr))
    second = jnp.concatenate(
        [(1.0 + scale_two[s]) * unit[s * per_sim : (s + 1) * per_sim] + shift_two[s] for s in range(2)], axis=0
    ).astype(LOW)
    scr.second[b] = second
    scr.second_t[:, pl.ds(pl.multiple_of(b * 2 * per_sim, 2 * per_sim), 2 * per_sim)] = second.T


def feed_chunk(b, at, cols, packed, cotangent, scr):
    up, down = cols.up[at], cols.down[at]
    queries = scr.second.shape[1]
    here = pl.ds(pl.multiple_of(b * queries, queries), queries)
    value, steep = gelu_cubed((product(scr.second[b], packed[:, up]) * CUBE).astype(LOW))
    hidden = value * jnp.asarray(0.5 / CUBE, LOW)
    d_up = (product(cotangent[b], packed[:, down]) * 1.5).astype(LOW) * steep
    scr.hidden[here, :] = hidden
    scr.d_up[here, :] = d_up
    if at == 0:
        scr.d_second[b] = trans_right(d_up, packed[:, up])
    else:
        scr.d_second[b] += trans_right(d_up, packed[:, up])
    if at == 0:
        scr.lat_sum[b] = trans_right(hidden, packed[:, down])
    elif at < CHUNKS - 1:
        scr.lat_sum[b] += trans_right(hidden, packed[:, down])


def feed_latents(b, cols, packed, latents, scr):
    queries = scr.second.shape[1]
    here = pl.ds(pl.multiple_of(b * queries, queries), queries)
    last = trans_right(scr.hidden[here, :], packed[:, cols.down[CHUNKS - 1]])
    scr.second[b] = (scr.lat_sum[b] + last).astype(LOW)
    pltpu.make_async_copy(scr.second.at[b], latents.at[b], scr.lat_sems.at[b]).start()


def feed_out(b, cols, packed, cotangent, grads, scr):
    width = scr.node.shape[-1]
    per_sim = scr.base_rows.shape[0]
    _, _, scale_two, _ = mod_rows(b, scr, width)
    attended_t = scr.attended_t[b]
    residual = residual_of(b, cols, packed, scr)
    res_unit, res_scale = normalised(residual)
    scr.lat_sum[b] += residual
    d_second = scr.d_second[b]
    d_res = []
    for s in range(2):
        rows_at = slice(s * per_sim, (s + 1) * per_sim)
        d_sim = d_second[rows_at]
        unit_sim = res_unit[rows_at]
        scr.d_mod[pl.ds(2 * b + s, 1), 2 * width : 3 * width] = jnp.sum(d_sim * unit_sim, axis=0, keepdims=True)
        scr.d_mod[pl.ds(2 * b + s, 1), 3 * width :] = jnp.sum(d_sim, axis=0, keepdims=True)
        d_res.append(
            cotangent[b, rows_at, :].astype(WIDE)
            + normalised_back(d_sim * (1.0 + scale_two[s]), unit_sim, res_scale[rows_at])
        )
    scr.d_base[...] += d_res[0] + d_res[1]
    res_low = jnp.concatenate(d_res, axis=0).astype(LOW)
    grads[:, cols.o] += product(attended_t, res_low)
    d_att = trans_right(packed[:, cols.o], res_low)
    for head in range(HEADS):
        there = slice(head * HEAD_DIM, (head + 1) * HEAD_DIM)
        scaled = d_att[there] * scr.inverse[b, head : head + 1, :]
        both = scaled * attended_t[there].astype(WIDE)
        scr.overlap[b, head : head + 1, :] = jnp.sum(both, axis=0, keepdims=True)
        scr.attended_t[b, there, :] = scaled.astype(LOW)


def attend_back(b, cols, packed, segments, grads, scr):
    length, width = scr.node.shape[1:]
    per_sim = scr.base_rows.shape[0]
    block = 2 * HEAD_DIM
    own_col, own_row = evolution_masks(b, segments, length)
    low_row = (own_row.astype(LOW), (1.0 - own_row).astype(LOW))
    mask = own_col > 0.5
    left_half = lax.broadcasted_iota(jnp.int32, (1, block), 1) < HEAD_DIM
    values_all = scr.values[b]
    query = scr.query[b]
    d_att = scr.attended_t[b]
    for pair in range(HEADS // 2):
        here = slice(pair * block, (pair + 1) * block)
        values = spread_heads(values_all[:, here], own_col)
        query_pair = by_sim(query, pair)
        d_att_pair = jnp.concatenate([d_att[here, :per_sim], d_att[here, per_sim:]], axis=0)
        d_share_pair = product(jnp.concatenate(values, axis=0), d_att_pair)
        d_raws = []
        for h in range(2):
            head = 2 * pair + h
            there = slice(head * HEAD_DIM, (head + 1) * HEAD_DIM)
            both = scr.overlap[b, head : head + 1, :]
            d_share = d_share_pair[h * length : (h + 1) * length]
            d_raw = (
                scr.weights_t[b, head].astype(WIDE)
                * (d_share - jnp.where(mask, both[:, :per_sim], both[:, per_sim:]))
            ).astype(LOW)
            d_raws.append(d_raw)
            key_t = scr.keyval_t[b, there, :]
            key_sims = jnp.concatenate([key_t * low_row[0], key_t * low_row[1]], axis=0)
            d_q = (product(key_sims, d_raw) * 0.125).astype(LOW)
            scr.query_t[there, :per_sim] = d_q[:HEAD_DIM]
            scr.query_t[there, per_sim:] = d_q[HEAD_DIM:]
        shares = scr.weights_t[b, 2 * pair : 2 * pair + 2].reshape(2 * length, per_sim)
        d_keys, d_values = [], []
        for full, parts in (
            (product(jnp.concatenate(d_raws, axis=0), query_pair), d_keys),
            (trans_right(shares, d_att_pair), d_values),
        ):
            for h in range(2):
                own = full[h * length : (h + 1) * length]
                parts.append(jnp.where(mask, own[:, :block], own[:, block:]))
        scr.d_keyval[:, here] = jnp.where(left_half, d_keys[0], d_keys[1]).astype(LOW)
        scr.d_keyval[:, width + here.start : width + here.stop] = jnp.where(
            left_half, d_values[0], d_values[1]
        ).astype(LOW)

    scale_one, shift_one, _, _ = mod_rows(b, scr, width)
    d_query = scr.query_t[...].T
    grads[:, cols.q] += trans_left(first_rows(b, scr, width), d_query)
    d_first = trans_right(d_query, packed[:, cols.q])
    for s in range(2):
        d_sim = d_first[s * per_sim : (s + 1) * per_sim]
        scr.d_mod[pl.ds(2 * b + s, 1), :width] = jnp.sum(d_sim * scr.base_unit[...], axis=0, keepdims=True)
        scr.d_mod[pl.ds(2 * b + s, 1), width : 2 * width] = jnp.sum(d_sim, axis=0, keepdims=True)
        scr.d_base_unit[...] += d_sim * (1.0 + scale_one[s])

    unit, node_scale = normalised(scr.node[b])
    gain = scr.gain_row[...]
    d_kv = scr.d_keyval[...]
    grads[:, cols.kv] += trans_left((unit * gain).astype(LOW), d_kv)
    d_normed = trans_right(d_kv, packed[:, cols.kv])
    scr.d_gain[...] += jnp.sum(d_normed * unit, axis=0, keepdims=True)
    scr.node[b] = normalised_back(d_normed * gain, unit, node_scale)


def perceiver_scratch(count, length, width, per_sim, chunk):
    queries = 2 * per_sim
    return dict(
        values=pltpu.VMEM((count, length, width), LOW),
        keyval_t=pltpu.VMEM((count, 2 * width, length), LOW),
        query=pltpu.VMEM((count, queries, width), LOW),
        weights_t=pltpu.VMEM((count, HEADS, length, per_sim), LOW),
        attended_t=pltpu.VMEM((count, width, queries), LOW),
        overlap=pltpu.VMEM((count, 8, queries), WIDE),
        inverse=pltpu.VMEM((count, 8, queries), WIDE),
        second=pltpu.VMEM((count, queries, width), LOW),
        second_t=pltpu.VMEM((width, count * queries), LOW),
        cot_t=pltpu.VMEM((width, count * queries), LOW),
        hidden=pltpu.VMEM((count * queries, chunk), LOW),
        d_up=pltpu.VMEM((count * queries, chunk), LOW),
        lat_sum=pltpu.VMEM((count, queries, width), WIDE),
        d_second=pltpu.VMEM((count, queries, width), WIDE),
        query_t=pltpu.VMEM((width, queries), LOW),
        d_keyval=pltpu.VMEM((length, 2 * width), LOW),
    )


def one_hot(near_t, edges, columns, length):
    picks = []
    for k in edges:
        row = near_t[k : k + 1, columns].astype(jnp.int16)
        spot = lax.broadcasted_iota(jnp.int16, (length, row.shape[1]), 0)
        picks.append(jnp.where(row == spot, jnp.asarray(1.0, LOW), jnp.asarray(0.0, LOW)))
    return jnp.concatenate(picks, axis=1)


def message_half(b, half, cols, packed, points, tokens, neighbours, scr):
    length, width = points.shape[1:]
    count = neighbours.shape[1]
    part = length // 2
    here = slice(half * part, (half + 1) * part)
    if half == 0:
        scr.source_t[...] = (trans_right(packed[:, cols.source], points[b]) * CUBE).astype(LOW)
    target = (trans_right(packed[:, cols.target], tokens[b, here, :]) * CUBE).astype(LOW)
    target = jnp.concatenate([target, target], axis=1)
    near_t = neighbours[b]
    group = 8
    for at in range(0, count, group):
        value, steep = None, None
        for k in range(at, at + group, 2):
            inside = product(scr.source_t[...], one_hot(near_t, (k, k + 1), here, length)).astype(LOW) + target
            v, t = gelu_cubed(inside)
            scr.slope[b, k, :, here] = t[:, :part]
            scr.slope[b, k + 1, :, here] = t[:, part:]
            v, t = v[:, :part] + v[:, part:], t[:, :part] + t[:, part:]
            value, steep = (v, t) if value is None else (value + v, steep + t)
        if at == 0:
            scr.value_sum[...] = value.astype(WIDE)
            scr.slope_sum[b, :, here] = steep.astype(WIDE)
        else:
            scr.value_sum[...] += value.astype(WIDE)
            scr.slope_sum[b, :, here] += steep.astype(WIDE)
    mixed = (scr.value_sum[...] * (0.5 / (count * CUBE))).astype(LOW)
    scr.mixed_t[b, :, here] = mixed
    scr.node[b, here, :] = tokens[b, here, :].astype(WIDE) + trans_left(mixed, packed[:, cols.msg_out])


def token_back(b, cols, packed, tokens, scr, grads):
    count = scr.slope.shape[1]
    d_out = scr.node[b]
    node_low = d_out.astype(LOW)
    grads[:, cols.msg_out] += product(scr.mixed_t[b], node_low)
    d_mixed = trans_right(packed[:, cols.msg_out], node_low) * (1.5 / count)
    scr.mixed_t[b] = d_mixed.astype(LOW)
    d_target = (d_mixed * scr.slope_sum[b]).astype(LOW)
    grads[:, cols.target] += product(d_target, tokens[b])
    return d_out + trans_left(d_target, packed[:, cols.target])


def source_back(b, cols, packed, points, neighbours, scr, grads):
    length = points.shape[1]
    count = neighbours.shape[1]
    near_t = neighbours[b]
    group = 4
    low = scr.mixed_t[b]
    for at in range(0, count, group):
        edges = range(at, at + group)
        inside = jnp.concatenate([scr.slope[b, k] * low for k in edges], axis=1)
        part = trans_right(inside, one_hot(near_t, edges, slice(0, length), length))
        if at == 0:
            scr.total[...] = part
        else:
            scr.total[...] += part
    d_source = scr.total[...].astype(LOW)
    grads[:, cols.source] += product(d_source, points[b])
    return trans_left(d_source, packed[:, cols.source])


def remote(src, dst, send, recv, to):
    return pltpu.make_async_remote_copy(
        src_ref=src, dst_ref=dst, send_sem=send, recv_sem=recv, device_id=to, device_id_type=pl.DeviceIdType.MESH
    )


class Packed:
    def __init__(self, ref):
        self.ref = ref

    def __getitem__(self, index):
        piece = self.ref[:, :, :, index[1]]
        return piece.reshape(-1, piece.shape[-1])


class Gather:
    def __init__(self, place, ref, groups, sems):
        self.section, self.dp, self.rep, self.chips = place
        self.ref, self.groups = ref, groups
        self.core = lax.rem(self.dp, 2)
        self.chip = self.dp // 2
        self.send, self.recv = sems
        self.line = self.chips == 4

    def half(self, group, which):
        start, stop = self.groups[group]
        size = (stop - start) // 2
        return pl.ds(pl.multiple_of(start + which * size, 128), size)

    def whole(self, group):
        start, stop = self.groups[group]
        return pl.ds(start, stop - start)

    def source(self, k):
        return lax.rem(self.chip - k + self.chips, self.chips)

    def copy(self, spot, send, group, recv, to):
        return remote(spot, spot, self.send.at[send], self.recv.at[group, recv], to)

    def along(self, group, k, chip):
        spot = self.ref.at[chip, self.core, :, self.half(group, self.rep)]
        far = 2 * lax.rem(self.chip + k, self.chips) + self.core
        return self.copy(spot, k - 1, group, k - 1, (self.section, far, self.rep))

    def onward(self, group):
        to, k = 3 * (self.chip - 1), 2 * self.chip - 1
        spot = self.ref.at[self.source(2), self.core, :, self.half(group, self.rep)]
        return self.copy(spot, self.chips - 1, group, k - 1, (self.section, 2 * to + self.core, self.rep))

    def over_rep(self, group, chip):
        spot = self.ref.at[chip, self.core, :, self.half(group, self.rep)]
        return self.copy(spot, self.chips, group, self.chips - 1, (self.section, self.dp, 1 - self.rep))

    def from_rep(self, group):
        spot = self.ref.at[pl.ds(0, self.chips - 1), self.core, :, self.half(group, 1 - self.rep)]
        return self.copy(spot, self.chips, group, self.chips - 1, (self.section, self.dp, 1 - self.rep))

    def over_core(self, group, core):
        spot = self.ref.at[:, core, :, self.whole(group)]
        to = (self.section, 2 * self.chip + 1 - self.core, self.rep)
        return self.copy(spot, self.chips + 1, group, self.chips, to)

    def ends(self, k):
        return jnp.abs(lax.rem(self.chip + k, self.chips) - self.chip) == self.chips - 1

    def inner(self):
        return (self.chip == 1) | (self.chip == 2)

    def direct(self, k, act):
        if self.line:

            @pl.when(jnp.logical_not(self.ends(k)))
            def _():
                act()

        else:
            act()

    def begin(self, group):
        for k in range(1, self.chips):
            self.direct(k, lambda: self.along(group, k, self.chip).start())

    def arrived(self, group, n):
        last = jnp.where(self.chip == 0, 1, 3)
        k = [2, 4 - last, last][n] if self.line else n + 1
        chip = self.source(k)
        self.along(group, k, chip).wait_recv()
        if self.line and n == 0:

            @pl.when(self.inner())
            def _():
                self.onward(group).start()

        self.over_rep(group, chip).start()

    def near(self, group):
        for n in range(self.chips - 2):
            self.arrived(group, n)

    def far(self, group):
        self.arrived(group, self.chips - 2)

    def late(self, group):
        self.from_rep(group).wait_recv()
        self.over_core(group, self.core).start()

    def finish(self, group):
        self.over_core(group, 1 - self.core).wait_recv()

    def drain(self):
        total = self.ref.shape[-1]
        part = pl.ds(0, total // 2)
        home = (self.section, self.dp, 1 - self.rep)
        for k in range(1, self.chips):
            spot = self.ref.at[self.chip, self.core, :, part]
            self.direct(k, lambda: self.copy(spot, k - 1, 0, k - 1, home).wait_send())
        if self.line:

            @pl.when(self.inner())
            def _():
                self.copy(self.ref.at[self.chip, self.core, :, part], self.chips - 1, 0, 0, home).wait_send()

        spot = self.ref.at[pl.ds(0, self.chips - 1), self.core, :, part]
        self.copy(spot, self.chips, 0, 0, home).wait_send()
        self.copy(self.ref.at[:, self.core], self.chips + 1, 0, 0, home).wait_send()


class Scatter:
    def __init__(self, place, grads, share, per, columns, sems, at, bufs):
        self.section, self.dp, self.rep, self.chips = place
        self.grads, self.share, self.per, self.columns = grads, share, per, columns
        self.core = lax.rem(self.dp, 2)
        self.chip = self.dp // 2
        self.sems, self.at = sems, at
        self.core_out, self.core_in, self.rep_in, self.far_in, self.end_out, self.end_in = bufs
        self.size = (columns[1] - columns[0]) // 2
        self.rep_out = self.core_out.at[:, :, : self.size]
        self.far_out = self.core_out.at[:, :, self.size :]

    def rows(self, chip, core):
        return pl.ds(pl.multiple_of((2 * chip + core) * self.per, 16), self.per)

    def half(self, which):
        return pl.ds(pl.multiple_of(self.columns[0] + which * self.size, 128), self.size)

    def local(self, which):
        return pl.ds(pl.multiple_of(which * self.size, 128), self.size)

    def pair(self, kind):
        return self.sems[0].at[self.at, kind], self.sems[1].at[self.at, kind]

    def core_copy(self):
        to = (self.section, 2 * self.chip + 1 - self.core, self.rep)
        return remote(self.core_out, self.core_in, *self.pair(0), to)

    def rep_copy(self):
        return remote(self.rep_out, self.rep_in, *self.pair(1), (self.section, self.dp, 1 - self.rep))

    def far_copy(self, k):
        to = (self.section, 2 * lax.rem(self.chip + k, self.chips) + self.core, self.rep)
        return remote(self.far_out.at[k - 1], self.far_in.at[k - 1], *self.pair(3), to)

    def far_all(self):
        return remote(self.far_out.at[: self.chips - 1], self.far_in, *self.pair(3), (self.section, self.dp, 1 - self.rep))

    def end_copy(self):
        return remote(self.end_out, self.end_in, *self.pair(2), (self.section, self.dp, 1 - self.rep))

    def begin(self):
        start, stop = self.columns
        for chip in range(self.chips):
            self.core_out[chip] = self.grads[self.rows(chip, 1 - self.core), start:stop].astype(LOW)
        self.core_copy().start()

    def middle(self):
        self.core_copy().wait()
        for chip in range(self.chips):
            rows = self.rows(chip, self.core)
            other = self.grads[rows, self.half(1 - self.rep)]
            self.rep_out[chip] = (other + self.core_in[chip, :, self.local(1 - self.rep)].astype(WIDE)).astype(LOW)
        self.rep_copy().start()

    def late(self):
        self.rep_copy().wait_recv()
        for k in range(self.chips):
            chip = lax.rem(self.chip + k, self.chips)
            rows = self.rows(chip, self.core)
            mine = self.grads[rows, self.half(self.rep)]
            mine = mine + self.core_in[chip, :, self.local(self.rep)].astype(WIDE)
            mine = mine + self.rep_in[chip].astype(WIDE)
            if k == 0:
                self.grads[rows, self.half(self.rep)] = mine
            else:
                self.far_out[k - 1] = mine.astype(LOW)
                self.far_copy(k).start()

    def finish(self):
        total = self.grads[self.rows(self.chip, self.core), self.half(self.rep)]
        self.far_all().wait_recv()
        for k in range(1, self.chips):
            total = total + self.far_in[k - 1].astype(WIDE)
        low = total.astype(LOW)
        self.end_out[...] = low
        self.end_copy().start()
        self.share[:, self.half(self.rep)] = low

    def end(self):
        self.end_copy().wait_recv()
        self.share[:, self.half(1 - self.rep)] = self.end_in[...]
        self.rep_copy().wait_send()
        self.end_copy().wait_send()
        self.far_all().wait_send()


class Packets:
    def __init__(self, place, packets, sems, at):
        self.section, self.dp, self.rep, self.chips = place
        self.core, self.chip = lax.rem(self.dp, 2), self.dp // 2
        self.packets, self.sems, self.at = packets, sems, at

    def copy(self, spot, n, to):
        return remote(spot, spot, self.sems.at[0, self.at, n], self.sems.at[1, self.at, n], to)

    def along(self, k, chip):
        spot = self.packets.at[self.core, self.rep, chip]
        far = 2 * lax.rem(self.chip + k, self.chips) + self.core
        return self.copy(spot, k, (self.section, far, self.rep))

    def over_rep(self, rep):
        return self.copy(self.packets.at[self.core, rep], 0, (self.section, self.dp, 1 - self.rep))

    def over_core(self, core):
        to = (self.section, 2 * self.chip + 1 - self.core, self.rep)
        return self.copy(self.packets.at[core], self.chips, to)

    def begin(self, pieces):
        self.packets[self.core, self.rep, self.chip] = jnp.concatenate(pieces, axis=0).astype(LOW)
        for k in range(1, self.chips):
            self.along(k, self.chip).start()

    def middle(self):
        for k in range(1, self.chips):
            self.along(k, lax.rem(self.chip - k + self.chips, self.chips)).wait_recv()
        self.over_rep(self.rep).start()

    def late(self):
        self.over_rep(1 - self.rep).wait_recv()
        self.over_core(self.core).start()

    def finish(self):
        self.over_core(1 - self.core).wait_recv()
        for k in range(1, self.chips):
            self.along(k, self.chip).wait_send()
        self.over_rep(self.rep).wait_send()
        self.over_core(self.core).wait_send()
        width = self.packets.shape[-1]
        result = []
        for at in range(0, self.packets.shape[3], 16):
            part = self.packets[:, :, :, at : at + 16, :].astype(WIDE).reshape(4 * self.chips, 2, 8, width)
            result.append([part[:, m].reshape(32 * self.chips, width).astype(LOW) for m in range(2)])
        return result


def mod_share(scr, late, early, place, out, per):
    width = scr.node.shape[-1]
    second, condition = late.finish()
    (first,) = early.finish()
    scr.turned[...] = condition[0].T
    mine = scr.turned[pl.ds(pl.multiple_of(place[1] * per, 16), per), :]
    for at, part in enumerate(first + second):
        out[:, at * width : (at + 1) * width] = product(mine, part)


def layer_call(cols, linked, sizes, packed_in, raw, points, segments, neighbours, condition, cotangent, per):
    count, length, width = points.shape
    near = neighbours.shape[1]
    per_sim = cols.base.stop - cols.base.start
    chips = sizes[DP] // 2
    part = length // 2
    parts = tuple((cols.up[n].start, cols.down[n].stop) for n in range(CHUNKS))
    groups = (
        (0, cols.msg_out.stop),
        (cols.kv.start, cols.base.stop),
        (cols.mod_one.start, cols.mod_one.stop),
        (cols.up[0].start, cols.mod_two.stop),
    ) + parts[1:]
    summed = (
        (0, cols.gain.stop),
        (cols.target.start, cols.msg_out.stop),
        (cols.kv.start, cols.kv.stop),
        (cols.q.start, cols.base.stop),
    ) + parts
    many = cols.mod_two.start
    rows = 8
    weights_in = list(raw) if linked else [packed_in]
    inputs = weights_in + [points, segments, neighbours, condition, cotangent]
    shape = jax.ShapeDtypeStruct
    outs = [
        shape((count, 2 * per_sim, width), LOW),
        shape((count, length, width), LOW),
        shape((count, length, width), LOW),
    ]
    outs.append(shape((per, many), LOW) if linked else shape((width, many), WIDE))
    outs.append(shape((per if linked else width, 4 * width), WIDE))
    scratch = dict(
        source_t=pltpu.VMEM((width, length), LOW),
        value_sum=pltpu.VMEM((width, part), WIDE),
        tokens=pltpu.VMEM((count, length, width), LOW),
        passed=pltpu.VMEM((count, length, width), LOW),
        mixed_t=pltpu.VMEM((count, width, length), LOW),
        slope=pltpu.VMEM((count, near, width, length), LOW),
        slope_sum=pltpu.VMEM((count, width, length), WIDE),
        node=pltpu.VMEM((count, length, width), WIDE),
        total=pltpu.VMEM((width, length), WIDE),
        point_out=pltpu.VMEM((count, length, width), LOW),
        point_in=pltpu.VMEM((count, length, width), LOW),
        back_in=pltpu.VMEM((count, length, width), LOW),
        modulation=pltpu.VMEM((rows, 4 * width), WIDE),
        condition=pltpu.VMEM((2 * rows, width), WIDE),
        base_unit=pltpu.VMEM((per_sim, width), WIDE),
        base_rows=pltpu.VMEM((per_sim, width), WIDE),
        base_scale=pltpu.VMEM((per_sim, 1), WIDE),
        gain_row=pltpu.VMEM((1, width), WIDE),
        d_gain=pltpu.VMEM((1, width), WIDE),
        d_base_unit=pltpu.VMEM((per_sim, width), WIDE),
        d_base=pltpu.VMEM((per_sim, width), WIDE),
        d_mod=pltpu.VMEM((rows, 4 * width), WIDE),
        lat_sems=pltpu.SemaphoreType.DMA((count,)),
        pass_sems=pltpu.SemaphoreType.DMA((2, 2 * count)),
        back_sems=pltpu.SemaphoreType.DMA((2, count)),
        point_local=pltpu.SemaphoreType.DMA((2,)),
        point_sems=pltpu.SemaphoreType.DMA((2, count)),
    )
    scratch.update(perceiver_scratch(count, length, width, per_sim, cols.chunk))
    bufs = []
    if linked:
        scratch.update(
            packed=pltpu.VMEM((chips, 2, per, cols.total), LOW),
            grads=pltpu.VMEM((width, many), WIDE),
            packets_two=pltpu.VMEM((2, 2, chips, 4 * rows, width), LOW),
            packets_one=pltpu.VMEM((2, 2, chips, 2 * rows, width), LOW),
            turned=pltpu.VMEM((width, 4 * chips * rows), LOW),
            packet_sems=pltpu.SemaphoreType.DMA((2, 2, chips + 1)),
            gather_send=pltpu.SemaphoreType.DMA((chips + 2,)),
            gather_recv=pltpu.SemaphoreType.DMA((len(groups), chips + 1)),
            scatter_send=pltpu.SemaphoreType.DMA((len(summed), 4)),
            scatter_recv=pltpu.SemaphoreType.DMA((len(summed), 4)),
        )
        for start, stop in summed:
            size = stop - start
            bufs += [
                pltpu.VMEM((chips, per, size), LOW),
                pltpu.VMEM((chips, per, size), LOW),
                pltpu.VMEM((chips, per, size // 2), LOW),
                pltpu.VMEM((chips - 1, per, size // 2), LOW),
                pltpu.VMEM((per, size // 2), LOW),
                pltpu.VMEM((per, size // 2), LOW),
            ]
    names = list(scratch)

    def body(*refs):
        ins, refs = refs[: len(inputs)], refs[len(inputs) :]
        results, refs = refs[: len(outs)], refs[len(outs) :]
        scr = types.SimpleNamespace(**dict(zip(names, refs)))
        moved = refs[len(names) :]
        points, segments, neighbours, condition, cotangent = ins[-5:]
        latents, point_mine, point_other = results[:3]
        section, dp, rep = (lax.axis_index(name) for name in (SECTION, DP, REP))
        other = (1 - section, dp, rep)
        if linked:
            packed, grads = Packed(scr.packed), scr.grads
            core, chip = lax.rem(dp, 2), dp // 2
            partners = [other, (section, dp, 1 - rep), (section, 2 * chip + 1 - core, rep)]
            partners += [(section, 2 * lax.rem(chip + k, chips) + core, rep) for k in range(1, chips)]
        else:
            packed, grads = ins[0], results[3]
            partners = [other]
        barrier = pltpu.get_barrier_semaphore()
        for to in partners:
            pl.semaphore_signal(barrier, inc=1, device_id=to, device_id_type=pl.DeviceIdType.MESH)
        if linked:
            place = (section, dp, rep, chips)
            gather = Gather(place, scr.packed, groups, (scr.gather_send, scr.gather_recv))
            msg_in, msg_out, norm_gain, mod_weight, query_base, q_weight, kv_weight, o_weight, up_weight, down_weight = ins[:10]
            mine = scr.packed.at[chip, core]
            mine[:, cols.source] = msg_in[0, :, :width]
            mine[:, cols.target] = msg_in[0, :, width:]
            mine[:, cols.msg_out] = msg_out[0]
            gain = jnp.broadcast_to(norm_gain[...].astype(WIDE), (128, per)).T
            mine[:, cols.gain] = gain.astype(LOW)
            mine[:, cols.kv] = kv_weight[0]
            mine[:, cols.q] = q_weight[0]
            mine[:, cols.o] = o_weight[0]
            mine[:, cols.base] = query_base[0]
            mine[:, cols.mod_one] = mod_weight[0, :, : 2 * width]
            mine[:, cols.mod_two] = mod_weight[0, :, 2 * width :]
            for n in range(CHUNKS):
                piece = slice(n * cols.chunk, (n + 1) * cols.chunk)
                mine[:, cols.up[n]] = up_weight[0, :, piece]
                mine[:, cols.down[n]] = down_weight[0, :, piece]
        pl.semaphore_wait(barrier, len(partners))
        if linked:
            gather.begin(0)
            gather.begin(1)
        first = grads.at[:, : cols.base.stop]
        first[...] = jnp.zeros_like(first)
        for total in (scr.d_gain, scr.d_base_unit, scr.d_base, scr.d_mod, scr.condition):
            total[...] = jnp.zeros_like(total)
        for b in range(count):
            scr.condition[2 * b : 2 * b + 2, :] = condition[b].astype(WIDE)
            scr.cot_t[:, b * 2 * per_sim : (b + 1) * 2 * per_sim] = cotangent[b].T

        tokens = scr.tokens

        @pl.when(section == 0)
        def _():
            tokens[...] = points[...]

        if linked:
            gather.near(0)
            gather.far(0)
            gather.begin(2)
            gather.late(0)
            gather.finish(0)
            gather.near(1)
            gather.begin(3)

        def pass_copy(n):
            b, half = n // 2, lax.rem(n, 2)
            rows = pl.ds(pl.multiple_of(half * part, part), part)
            return remote(
                scr.passed.at[b, rows, :], tokens.at[b, rows, :], scr.pass_sems.at[0, n], scr.pass_sems.at[1, n], other
            )

        def back_copy(b):
            return remote(scr.passed.at[b], scr.back_in.at[b], scr.back_sems.at[0, b], scr.back_sems.at[1, b], other)

        def point_copy(b):
            return remote(scr.point_out.at[b], scr.point_in.at[b], scr.point_sems.at[0, b], scr.point_sems.at[1, b], other)

        def forward(b):
            for half in range(2):
                n = 2 * b + half

                @pl.when(section == 1)
                def _():
                    pass_copy(n).wait_recv()

                message_half(b, half, cols, packed, points, tokens, neighbours, scr)

                @pl.when(section == 0)
                def _():
                    rows = slice(half * part, (half + 1) * part)
                    scr.passed[b, rows, :] = scr.node[b, rows, :].astype(LOW)
                    pass_copy(n).start()

                ahead = jnp.where(b == 2, 8 * half - 1, n + 2)
                gather_at(jnp.where(section == 0, n, ahead), (1, 3, 5, 7) if half else (0, 2, 4))

        def prepare():
            base = packed[:, cols.base].astype(WIDE).T
            scr.base_rows[...] = base
            unit, scale = normalised(base)
            scr.base_unit[...] = unit
            scr.base_scale[...] = scale
            scr.gain_row[...] = packed[:, cols.gain].astype(WIDE).T[:1]
            scr.modulation[:, : 2 * width] = product(scr.condition[...].astype(LOW), packed[:, cols.mod_one])[:rows]

        def gather_step(n):
            if n == 0:
                gather.far(1)
            elif n == 1:
                gather.near(2)
                gather.begin(4)
            elif n == 2:
                gather.far(2)
            elif n == 3:
                gather.late(1)
                gather.near(3)
                gather.begin(5)
            elif n == 4:
                gather.far(3)
            elif n == 5:
                gather.late(2)
                gather.finish(1)
                gather.near(4)
                gather.finish(2)
                prepare()
            elif n == 6:
                gather.far(4)
                gather.late(3)
                gather.near(5)
            else:
                gather.far(5)
                gather.late(4)
                gather.finish(3)

        def gather_at(at, choices):
            if linked:
                for n in choices:

                    @pl.when(at == n)
                    def _():
                        gather_step(n)

        if linked:

            @pl.when(section == 1)
            def _():
                gather_step(0)
                gather_step(1)

        else:
            prepare()

        def early(step, carry):
            late_one = (step == 3) & (section == 1)
            early_one = (step == 2) & (section == 1)
            message = ((step < count) | late_one) & jnp.logical_not(early_one)
            b = jnp.where(message, jnp.minimum(step, count - 1), jnp.where(early_one, 0, step - count))

            @pl.when(message)
            def _():
                forward(b)

            @pl.when(jnp.logical_not(message))
            def _():
                attend(b, cols, packed, segments, scr)
                gather_at(jnp.where(section == 0, 6 + b, 6 + 2 * b), (6, 7))

            return carry

        lax.fori_loop(0, 2 * count, early, 0)
        if linked:
            scatters = [
                Scatter(
                    place, grads, results[3], per, summed[n], (scr.scatter_send, scr.scatter_recv), n,
                    moved[6 * n : 6 * n + 6],
                )
                for n in range(len(summed))
            ]

        scr.modulation[:, 2 * width :] = product(scr.condition[...].astype(LOW), packed[:, cols.mod_two])[:rows]

        def feed_first(b, carry):
            feed_in(b, cols, packed, scr)
            return carry

        lax.fori_loop(0, count, feed_first, 0, unroll=True)
        for at in range(CHUNKS):
            if linked and at > 0:
                gather.finish(3 + at)

            def feed_step(b, carry):
                feed_chunk(b, at, cols, packed, cotangent, scr)
                if linked and at == 0:

                    @pl.when(b == 0)
                    def _():
                        gather.late(5)

                return carry

            lax.fori_loop(0, count, feed_step, 0, unroll=True)
            grads[:, cols.down[at]] = product(scr.cot_t[...], scr.hidden[...])
            grads[:, cols.up[at]] = product(scr.second_t[...], scr.d_up[...])
            if linked:
                scatters[4 + at].begin()
                if at > 0:
                    scatters[3 + at].middle()
                if at > 1:
                    scatters[2 + at].late()

        if linked:
            halves = [slice(width * n, width * (n + 1)) for n in range(4)]
            packet_two = Packets(place, scr.packets_two, scr.packet_sems, 0)
            packet_one = Packets(place, scr.packets_one, scr.packet_sems, 1)

        def token_step(b):
            return token_back(b, cols, packed, tokens, scr, grads)

        def attention_back(b, carry):
            feed_out(b, cols, packed, cotangent, grads, scr)
            if linked:

                @pl.when(b == 0)
                def _():
                    scatters[6].middle()

                @pl.when(b == count - 1)
                def _():
                    packet_two.begin([scr.d_mod[:, halves[2]], scr.d_mod[:, halves[3]], scr.condition[...]])

            attend_back(b, cols, packed, segments, grads, scr)

            @pl.when(section == 1)
            def _():
                scr.passed[b] = token_step(b).astype(LOW)
                back_copy(b).start()

            if linked:

                @pl.when(b == 0)
                def _():
                    scatters[5].late()
                    scatters[4].finish()

                @pl.when(b == 1)
                def _():
                    scatters[6].late()
                    scatters[5].finish()

            return carry

        lax.fori_loop(0, count, attention_back, 0)
        if linked:
            scatters[2].begin()
        d_rows = normalised_back(scr.d_base_unit[...], scr.base_unit[...], scr.base_scale[...])
        grads[:, cols.base] = (d_rows + scr.d_base[...]).T
        grads[:, cols.gain] = jnp.broadcast_to(scr.d_gain[...], (128, width)).T
        if linked:
            scatters[3].begin()
            packet_one.begin([scr.d_mod[:, halves[0]], scr.d_mod[:, halves[1]]])
            packet_two.middle()

            @pl.when(section == 1)
            def _():
                scatters[1].begin()

            scatters[6].finish()
            scatters[2].middle()
        else:
            results[4][...] = trans_left(scr.condition[:rows].astype(LOW), scr.d_mod[...].astype(LOW))

        def backward(b, carry):
            @pl.when(section == 0)
            def _():
                back_copy(b).wait_recv()
                scr.node[b] = scr.node[b] + scr.back_in[b].astype(WIDE)
                scr.node[b] = token_step(b)

            @pl.when(section == 1)
            def _():
                scr.node[b] = jnp.zeros((length, width), WIDE)

            if linked:

                @pl.when((b == count - 1) & (section == 0))
                def _():
                    scatters[1].begin()

            d_points = source_back(b, cols, packed, points, neighbours, scr, grads)
            scr.point_out[b] = (scr.node[b] + d_points).astype(LOW)
            point_copy(b).start()
            if linked:

                @pl.when(b == 0)
                def _():
                    scatters[3].middle()
                    packet_one.middle()
                    packet_two.late()

                    @pl.when(section == 1)
                    def _():
                        scatters[1].middle()

                @pl.when(b == 1)
                def _():
                    packet_one.late()
                    scatters[2].late()

            return carry

        lax.fori_loop(0, count, backward, 0)
        if linked:
            scatters[0].begin()
            scatters[3].late()

            @pl.when(section == 0)
            def _():
                scatters[1].middle()

        feed_latents(0, cols, packed, latents, scr)
        if linked:
            scatters[0].middle()

            @pl.when(section == 1)
            def _():
                scatters[1].late()

        for b in range(1, count):
            feed_latents(b, cols, packed, latents, scr)
        if linked:
            scatters[2].finish()

            @pl.when(section == 0)
            def _():
                scatters[1].late()

            scatters[0].late()
            scatters[3].finish()
            for n in range(4, 4 + CHUNKS):
                scatters[n].end()
            mod_share(scr, packet_two, packet_one, place, results[4], per)
        for b in range(count):
            point_copy(b).wait_recv()
        point_moves = [
            pltpu.make_async_copy(scr.point_out, point_mine, scr.point_local.at[0]),
            pltpu.make_async_copy(scr.point_in, point_other, scr.point_local.at[1]),
        ]
        for move in point_moves:
            move.start()
        if linked:
            scatters[1].finish()
            scatters[0].finish()
            for n in (3, 2, 1, 0):
                scatters[n].end()
            gather.drain()
        for move in point_moves:
            move.wait()

        for b in range(count):
            pltpu.make_async_copy(scr.second.at[b], latents.at[b], scr.lat_sems.at[b]).wait()

        @pl.when(section == 0)
        def _():
            for n in range(2 * count):
                pass_copy(n).wait_send()

        @pl.when(section == 1)
        def _():
            for b in range(count):
                back_copy(b).wait_send()

        for b in range(count):
            point_copy(b).wait_send()

    spec = pl.BlockSpec(memory_space=pltpu.VMEM)
    return pl.pallas_call(
        body,
        out_shape=outs,
        in_specs=[spec] * len(inputs),
        out_specs=[pl.BlockSpec(memory_space=pl.ANY)] * 3 + [spec] * (len(outs) - 3),
        scratch_shapes=list(scratch.values()) + bufs,
        compiler_params=pltpu.CompilerParams(
            vmem_limit_bytes=VMEM_BYTES, collective_id=0, has_side_effects=True
        ),
        cost_estimate=pl.CostEstimate(flops=10**10, bytes_accessed=1 << 24, transcendentals=0),
        name="layers",
    )(*inputs)


def finish_call(cols, latents, point_mine, point_other, share, mod_share):
    per, width = share.shape[0], point_mine.shape[-1]
    pieces = ([cols.msg_out], [cols.gain], [cols.base], [cols.q], [cols.kv], [cols.o], cols.up, cols.down)
    gain_at = 1

    shape = jax.ShapeDtypeStruct
    outs = [shape(latents.shape, LOW), shape(mod_share.shape, WIDE), shape(point_mine.shape, WIDE)]
    outs.append(shape((1, per, 2 * width), WIDE))
    for n, piece in enumerate(pieces):
        outs.append(shape((1, per) if n == gain_at else (1, per, sum(place.stop - place.start for place in piece)), WIDE))
    inputs = (share, point_mine, point_other, latents, mod_share)
    count = len(outs)

    def body(*refs):
        ins, refs = refs[: len(inputs)], refs[len(inputs) :]
        results, refs = refs[:count], refs[count:]
        held, refs = refs[: len(inputs)], refs[len(inputs) :]
        made, sems = refs[:-1], refs[-1]
        arriving = [pltpu.make_async_copy(a, b, sems.at[n]) for n, (a, b) in enumerate(zip(ins, held))]
        for move in arriving:
            move.start()
        share, point_mine, point_other, latents, mod_share = held
        sources = [latents, mod_share, *made]
        leaving = [
            pltpu.make_async_copy(a, b, sems.at[len(inputs) + n]) for n, (a, b) in enumerate(zip(sources, results))
        ]
        arriving[0].wait()
        msg_in, parts = made[1], made[2:]
        msg_in[0, :, :width] = share[:, cols.source].astype(WIDE)
        msg_in[0, :, width:] = share[:, cols.target].astype(WIDE)
        leaving[3].start()
        for n, piece in enumerate(pieces):
            at = 0
            for place in piece:
                value = share[:, place].astype(WIDE)
                size = place.stop - place.start
                if n == gain_at:
                    parts[n][...] = value.T[:1]
                else:
                    parts[n][0, :, at : at + size] = value
                at += size
            leaving[4 + n].start()
        arriving[1].wait()
        arriving[2].wait()
        made[0][...] = point_mine[...].astype(WIDE) + point_other[...].astype(WIDE)
        leaving[2].start()
        for n in (0, 1):
            arriving[3 + n].wait()
            leaving[n].start()
        for move in leaving:
            move.wait()

    whole = pl.BlockSpec(memory_space=pl.ANY)
    results = pl.pallas_call(
        body,
        out_shape=outs,
        in_specs=[whole] * len(inputs),
        out_specs=[whole] * count,
        scratch_shapes=[pltpu.VMEM(a.shape, a.dtype) for a in inputs]
        + [pltpu.VMEM(a.shape, a.dtype) for a in outs[2:]]
        + [pltpu.SemaphoreType.DMA((len(inputs) + count,))],
        compiler_params=pltpu.CompilerParams(vmem_limit_bytes=VMEM_BYTES),
        cost_estimate=pl.CostEstimate(flops=10**6, bytes_accessed=1 << 23, transcendentals=0),
        name="finish",
    )(*inputs)
    latents, mod, point_sum, msg_in, msg_out, gain, base, q, kv, o, up, down = results
    turn = lambda array: jnp.swapaxes(array, 1, 2)
    return (latents[None], point_sum, turn(msg_in), msg_out, gain, mod[None], turn(base), q, kv, o, up, turn(down))


def on_device(
    points,
    segments,
    neighbours,
    condition,
    msg_in,
    msg_out,
    norm_gain,
    mod_weight,
    query_base,
    q_weight,
    kv_weight,
    o_weight,
    up_weight,
    down_weight,
    cotangent,
):
    count, length, width = points.shape
    per = q_weight.shape[1]
    hidden = up_weight.shape[2]
    per_sim = query_base.shape[1]
    cols = Columns(width, hidden, per_sim)
    sizes = {name: lax.axis_size(name) for name in (SECTION, DP, REP)}
    linked = per % 16 == 0 and sizes[DP] % 2 == 0 and sizes[REP] == 2
    raw = (
        jnp.swapaxes(msg_in, 1, 2),
        msg_out,
        norm_gain,
        mod_weight,
        jnp.swapaxes(query_base, 1, 2),
        q_weight,
        kv_weight,
        o_weight,
        up_weight,
        jnp.swapaxes(down_weight, 1, 2),
    )
    near_t = jnp.swapaxes(neighbours, 1, 2)
    if linked:
        outs = layer_call(cols, True, sizes, None, raw, points, segments, near_t, condition, cotangent[0], per)
        return finish_call(cols, *outs)
    turned = msg_in[0].T
    own = jnp.concatenate(
        [
            turned[:, :width],
            jnp.broadcast_to(norm_gain[0][:, None], (per, 128)),
            turned[:, width:],
            msg_out[0],
            kv_weight[0],
            q_weight[0],
            o_weight[0],
            query_base[0].T,
            *sum(
                (
                    [
                        up_weight[0, :, n * cols.chunk : (n + 1) * cols.chunk],
                        down_weight[0, n * cols.chunk : (n + 1) * cols.chunk].T,
                    ]
                    for n in cols.order
                ),
                [],
            ),
            mod_weight[0, :, 2 * width :],
            mod_weight[0, :, : 2 * width],
        ],
        axis=1,
    )
    packed = lax.all_gather(own, DP, axis=0, tiled=True)
    latents, point_mine, point_other, grads, mod_grads = layer_call(
        cols, False, sizes, packed, None, points, segments, near_t, condition, cotangent[0], per
    )
    grads = jnp.concatenate([grads, mod_grads], axis=1)
    share = lax.psum_scatter(grads, DP, scatter_dimension=0, tiled=True)
    share = lax.psum(share.astype(LOW), REP).astype(WIDE)
    return (
        latents[None],
        point_mine.astype(WIDE) + point_other.astype(WIDE),
        jnp.concatenate([share[:, cols.source], share[:, cols.target]], axis=1).T[None],
        share[None, :, cols.msg_out],
        share[None, :, cols.gain.start],
        share[None, :, cols.mod_two.start :],
        share[:, cols.base].T[None],
        share[None, :, cols.q],
        share[None, :, cols.kv],
        share[None, :, cols.o],
        jnp.concatenate([share[None, :, piece] for piece in cols.up], axis=2),
        jnp.concatenate([share[:, piece] for piece in cols.down], axis=1).T[None],
    )


def solution(mesh):
    placed = (
        P((DP, REP), None, None),
        P((DP, REP), None),
        P((DP, REP), None, None),
        P((DP, REP), None, None),
        P(SECTION, None, DP),
        P(SECTION, DP, None),
        P(SECTION, DP),
        P(SECTION, DP, None),
        P(SECTION, None, DP),
        P(SECTION, DP, None),
        P(SECTION, DP, None),
        P(SECTION, DP, None),
        P(SECTION, DP, None),
        P(SECTION, None, DP),
        P(SECTION, (DP, REP), None, None),
    )
    return jax.shard_map(
        on_device,
        mesh=mesh,
        in_specs=placed,
        out_specs=(
            P(SECTION, (DP, REP), None, None),
            P((DP, REP), None, None),
            P(SECTION, None, DP),
            P(SECTION, DP, None),
            P(SECTION, DP),
            P(SECTION, DP, None),
            P(SECTION, None, DP),
            P(SECTION, DP, None),
            P(SECTION, DP, None),
            P(SECTION, DP, None),
            P(SECTION, DP, None),
            P(SECTION, None, DP),
        ),
        check_vma=False,
    )
```
